32 devices in a mesh: pa: 4 (over y, core), pb: 8 (over z, x).
Axes of the slice: x: 2, y: 2, z: 4, core: 2. Of those that a mesh axis runs over, the one named last changes fastest.
Arguments:
- velocity: float32 [3, 2048, 32, 1024], P(None, ('pa', 'pb')), may hold values from -6 to 6
- fluid: float32 [2048, 32, 1024], P(('pa', 'pb')), may hold values from 0.25 to 1
- block_place: int32 [2048], P(('pa', 'pb')), may hold values from 0 to 63, as said below
Outputs:
- velocity_next: float32 [3, 2048, 32, 1024], P(None, ('pa', 'pb'))
- pressure: float32 [2048, 32, 1024], P(('pa', 'pb'))
The draws below stay inside these ranges and needn't reach their ends.
Inputs may be any that keep to these rules, and one draw needn't show every extreme that they name: `block_place`: within each device's 64 consecutive slots every tile position appears exactly once.
All inputs are finite; a program needn't handle non-finite values.
Results may differ from the reference program's by a relative error of at most 0.0015.
Values sent between devices are 32-bit elements; how exact they have to be, the bound alone decides.
No kernel may reach another device: no remote copies, remote signals or barrier semaphores. Data moves between devices by JAX's collectives and lax.ppermute only.
A program may use at most 448 MiB of HBM per device.

```python
import jax
import jax.numpy as jnp
from jax import lax

NX = 2048
NY = 1024
NZ = 32
B = 32
BPD = 64
NBLK = 2048
N_PA = 4
N_PB = 8


def draw_block_place(key, part):
    key = jax.random.fold_in(key, 7)
    device_keys = jax.random.split(key, NBLK // BPD)

    def shuffle_one(device_key):
        return jax.random.permutation(device_key, BPD)
    orders = jax.vmap(shuffle_one)(device_keys)
    return orders.reshape(NBLK).astype(jnp.int32)


def steps_of(rng, dims, cuts, low, high):
    factor_of = 1.0
    for dim, parts in cuts:
        draws = jax.random.uniform(jax.random.fold_in(jax.random.fold_in(rng, 6), dim), (parts,), jnp.float32, low / len(cuts), high / len(cuts))
        factor_of = factor_of * jnp.repeat(jnp.exp(draws), dims[dim] // parts).reshape((-1,) + (1,) * (len(dims) - 1 - dim))
    return factor_of


def normal_values(rng, extent, spread, bound, cuts=(), held_as=jnp.bfloat16):
    drawn = spread * jax.random.normal(rng, extent, jnp.float32)
    if cuts:
        drawn = drawn * steps_of(rng, extent, cuts, -0.22, 0.18)
    return jnp.clip(drawn, -bound, bound).astype(held_as)


def setup_inputs(seed: int = 0) -> dict:
    splits = jax.random.split(jax.random.key(seed), 4)
    return {
        "velocity": normal_values(splits[0], (3, NBLK, B, B * B), 1.0, 6.0, ((1, 32),), jnp.float32),
        "fluid": jnp.clip(0.25 + 0.75 * jax.random.uniform(splits[1], (NBLK, B, B * B), jnp.float32) ** steps_of(splits[1], (NBLK, B, B * B), ((0, 32),), -0.2, 0.2), 0.25, 1.0),
        "block_place": draw_block_place(jax.random.fold_in(splits[3], 71), 0),
    }


step_size = 0.25
viscosity = 0.1


def advance_one(center, flow_center, lower_side, upper_side, fraction):
    diffusion = lower_side[0] + upper_side[0] + lower_side[1] + upper_side[1] + lower_side[2] + upper_side[2] - 6.0 * center
    transport = flow_center[0] * (upper_side[0] - lower_side[0]) + flow_center[1] * (upper_side[1] - lower_side[1]) + flow_center[2] * (upper_side[2] - lower_side[2])
    return fraction * (center + step_size * (viscosity * diffusion - 0.5 * transport))


def wall_mask(layer_count):
    layer_ids = jnp.arange(layer_count)
    open_top = jnp.where(layer_ids < layer_count - 1, 1.0, 0.0).astype(jnp.float32)
    ones_layer = jnp.ones((layer_count,), jnp.float32)
    return jnp.stack([ones_layer, ones_layer, open_top])[:, :, None, None]


def eigen_of(mode_ids, length):
    half_angle = jnp.pi * (mode_ids + 1).astype(jnp.float32) / (2.0 * (length + 1))
    return 4.0 * jnp.sin(half_angle) * jnp.sin(half_angle)


def solve_columns(source, eigen_sum):
    layer_count = source.shape[0]
    first_pivot = eigen_sum + 1.0
    first_ratio = -1.0 / first_pivot
    first_value = source[0] / first_pivot
    top_flags = jnp.arange(1, layer_count) == layer_count - 1

    def eliminate(state_pair, element):
        prior_ratio, prior_value = state_pair
        layer_source, is_top = element
        pivot_value = eigen_sum + jnp.where(is_top, 1.0, 2.0) + prior_ratio
        new_ratio = -1.0 / pivot_value
        new_value = (layer_source + prior_value) / pivot_value
        return (new_ratio, new_value), (new_ratio, new_value)

    unused_state, (ratios, reduced_all) = lax.scan(eliminate, (first_ratio, first_value), (source[1:], top_flags))
    ratios = jnp.concatenate([first_ratio[None], ratios], axis=0)
    reduced_all = jnp.concatenate([first_value[None], reduced_all], axis=0)

    def substitute(following, element):
        layer_ratio, layer_value = element
        solved_layer = layer_value - layer_ratio * following
        return solved_layer, solved_layer

    top_layer = reduced_all[-1]
    unused_last, lower_layers = lax.scan(substitute, top_layer, (ratios[:-1], reduced_all[:-1]), reverse=True)
    return jnp.concatenate([lower_layers, top_layer[None]], axis=0)


def sine_rows(values):
    length = values.shape[-1]
    zero_pad = jnp.zeros(values.shape[:-1] + (1,), values.dtype)
    extended = jnp.concatenate([zero_pad, values, zero_pad, -values[..., ::-1]], axis=-1)
    spectrum = jnp.fft.rfft(extended, axis=-1)
    return (-0.5 * jnp.imag(spectrum[..., 1:length + 1])).astype(values.dtype)


def sine_plane(plane):
    along_x = sine_rows(plane)
    return sine_rows(along_x.T).T


def assemble(blocks, block_place):
    channels = blocks.shape[0]
    tile_y = NY // N_PA
    tile_x = NX // N_PB
    per_device = blocks.reshape(channels, N_PA * N_PB, BPD, B, B * B)
    placing = block_place.reshape(N_PA * N_PB, BPD)
    slot_ids = jnp.arange(BPD, dtype=jnp.int32)
    matches = placing[:, None, :] == slot_ids[None, :, None]
    inverse = jnp.sum(jnp.where(matches, slot_ids[None, None, :], 0), axis=2).astype(jnp.int32)
    ordered = jnp.take_along_axis(per_device, inverse[None, :, :, None, None], axis=2)
    shaped = ordered.reshape(channels, N_PA, N_PB, NZ // B, tile_y // B, tile_x // B, B, B, B)
    return shaped.transpose(0, 3, 6, 1, 4, 7, 2, 5, 8).reshape(channels, NZ, NY, NX)


def disassemble(field, block_place):
    channels = field.shape[0]
    tile_y = NY // N_PA
    tile_x = NX // N_PB
    shaped = field.reshape(channels, NZ // B, B, N_PA, tile_y // B, B, N_PB, tile_x // B, B)
    ordered = shaped.transpose(0, 3, 6, 1, 4, 7, 2, 5, 8).reshape(channels, N_PA * N_PB, BPD, B, B * B)
    placing = block_place.reshape(N_PA * N_PB, BPD)
    picked = jnp.take_along_axis(ordered, placing[None, :, :, None, None], axis=2)
    return picked.reshape(channels, NBLK, B, B * B)


def reference(velocity, fluid, block_place):
    flow = assemble(velocity, block_place)
    fraction = assemble(fluid[None], block_place)[0]
    padded = jnp.pad(flow, ((0, 0), (1, 1), (1, 1), (1, 1)))
    updated = []
    for component in range(3):
        lower_side = (padded[component, 1:-1, 1:-1, :-2], padded[component, 1:-1, :-2, 1:-1], padded[component, :-2, 1:-1, 1:-1])
        upper_side = (padded[component, 1:-1, 1:-1, 2:], padded[component, 1:-1, 2:, 1:-1], padded[component, 2:, 1:-1, 1:-1])
        updated.append(advance_one(flow[component], flow, lower_side, upper_side, fraction))
    provisional = jnp.stack(updated) * wall_mask(NZ)
    padded_star = jnp.pad(provisional, ((0, 0), (1, 0), (1, 0), (1, 0)))
    divergence = (provisional[0] - padded_star[0, 1:, 1:, :-1]) + (provisional[1] - padded_star[1, 1:, :-1, 1:]) + (provisional[2] - padded_star[2, :-1, 1:, 1:])
    scale = 4.0 / ((NX + 1) * (NY + 1))
    modes = lax.map(sine_plane, divergence)
    eigen_sum = eigen_of(jnp.arange(NY), NY)[:, None] + eigen_of(jnp.arange(NX), NX)[None, :]
    solved = solve_columns(-modes * scale, eigen_sum)
    pressure_grid = lax.map(sine_plane, solved)
    padded_p = jnp.pad(pressure_grid, ((0, 1), (0, 1), (0, 1)))
    gradient = jnp.stack([padded_p[:-1, :-1, 1:] - pressure_grid, padded_p[:-1, 1:, :-1] - pressure_grid, padded_p[1:, :-1, :-1] - pressure_grid]) * wall_mask(NZ)
    velocity_grid = provisional - gradient
    return disassemble(velocity_grid, block_place), disassemble(pressure_grid[None], block_place)[0]
```

```python
import functools

import jax
import jax.numpy as jnp
import ml_dtypes
import numpy as np
from jax import lax
from jax.experimental import pallas as pl
from jax.experimental.pallas import tpu as pltpu
from jax.sharding import PartitionSpec as P

NX = 2048
NY = 1024
NZ = 32
B = 32
LANES = 128
highest = lax.Precision.HIGHEST
f32 = jnp.float32
VMEM_LIMIT = 56 * 1024 * 1024


def cosine_basis():
    k = np.arange(NZ)[:, None]
    z = np.arange(NZ)[None, :]
    table = np.cos(np.pi * k * (z + 0.5) / NZ)
    table /= np.sqrt((table**2).sum(axis=1, keepdims=True))
    return table, 2.0 - 2.0 * np.cos(np.pi * np.arange(NZ) / NZ)


def sine_basis(length, lower_gap, upper_gap):
    span = length - 1 + lower_gap + upper_gap
    i = np.arange(length)[:, None]
    k = np.arange(1, length + 1)[None, :]
    table = np.sin(np.pi * k * (i + lower_gap) / span)
    table /= np.sqrt((table**2).sum(axis=0, keepdims=True))
    return table, 4.0 * np.sin(np.pi * np.arange(1, length + 1) / (2 * span)) ** 2


def tile_bases(length):
    return [sine_basis(length, *gaps) for gaps in ((1.0, 0.5), (0.5, 0.5), (0.5, 1.0))]


def split(table):
    table = np.asarray(table, np.float64)
    high = table.astype(np.float32).astype(ml_dtypes.bfloat16)
    low = (table - high.astype(np.float64)).astype(np.float32).astype(ml_dtypes.bfloat16)
    return np.stack([high, low], axis=-3)


def single(table):
    return np.asarray(table, np.float32)


def pieces(values):
    high = values.astype(jnp.bfloat16)
    return high, (values - high.astype(f32)).astype(jnp.bfloat16)


def mm(left, right):
    return jnp.dot(left, right, preferred_element_type=f32)


def table_times(table_ref, values):
    high, low = pieces(values)
    table_high, table_low = table_ref[0], table_ref[1]
    return mm(table_high, high) + (mm(table_high, low) + mm(table_low, high))


def times_table(values, table_ref):
    high, low = pieces(values)
    table_high, table_low = table_ref[0], table_ref[1]
    return mm(high, table_high) + (mm(high, table_low) + mm(low, table_high))


def dot_full(left, right, dims):
    return lax.dot_general(left, right, (dims, ((), ())), precision=highest, preferred_element_type=f32)


def lane_ids(rows=NZ):
    return lax.broadcasted_iota(jnp.int32, (rows, LANES), 1)


def swap_groups(four, lanes):
    low_half = lanes < 64
    even = (lanes & 32) == 0
    first = [
        jnp.where(low_half, four[0], pltpu.roll(four[2], 64, 1)),
        jnp.where(low_half, four[1], pltpu.roll(four[3], 64, 1)),
        jnp.where(low_half, pltpu.roll(four[0], 64, 1), four[2]),
        jnp.where(low_half, pltpu.roll(four[1], 64, 1), four[3]),
    ]
    out = []
    for pair in (0, 2):
        left, right = first[pair], first[pair + 1]
        out.append(jnp.where(even, left, pltpu.roll(right, 32, 1)))
        out.append(jnp.where(even, pltpu.roll(left, 96, 1), right))
    return out


def params():
    return pltpu.CompilerParams(vmem_limit_bytes=VMEM_LIMIT)


def gather_tile(velocity, fluid, inverse, rows_n, cols_n):
    y_span, x_span = rows_n * B, cols_n * B
    quads = cols_n // 4

    def kernel(inverse_ref, *refs):
        flow_refs = refs[:cols_n]
        fraction_refs = refs[cols_n : 2 * cols_n]
        out_ref, low_ref, high_ref = refs[2 * cols_n :]
        step = pl.program_id(0)
        lanes = lane_ids()
        place = step % 4
        chunk = pl.ds(pl.multiple_of(step // 4 * LANES, LANES), LANES)
        mine = (lanes // 32) == place
        for channel in range(4):
            low_edge = jnp.zeros((NZ, LANES), f32)
            high_edge = jnp.zeros((NZ, LANES), f32)
            for jq in range(8):
                for quad in range(quads):
                    four = []
                    for g in range(4):
                        at = quad * 4 + g
                        part = slice(jq * LANES, (jq + 1) * LANES)
                        if channel < 3:
                            four.append(flow_refs[at][channel, 0, :, part])
                        else:
                            four.append(fraction_refs[at][0, :, part])
                    rows = swap_groups(four, lanes)
                    for t in range(4):
                        j = jq * 4 + t
                        out_ref[channel, j, :, quad * LANES : (quad + 1) * LANES] = rows[t]
                        if channel < 3 and quad == 0:
                            low_edge = jnp.where(lanes == j, pltpu.roll(rows[t], j, 1), low_edge)
                        if channel < 3 and quad == quads - 1:
                            high_edge = jnp.where(lanes == j, pltpu.roll(rows[t], j + 1, 1), high_edge)
            if channel < 3:
                shift = place * 32
                low_ref[channel, :, chunk] = jnp.where(mine, pltpu.roll(low_edge, shift, 1), low_ref[channel, :, chunk])
                high_ref[channel, :, chunk] = jnp.where(mine, pltpu.roll(high_edge, shift, 1), high_ref[channel, :, chunk])

    def flow_spec(col):
        return pl.BlockSpec((3, 1, NZ, B * B), lambda s, inv: (0, inv[s * cols_n + col], 0, 0))

    def fraction_spec(col):
        return pl.BlockSpec((1, NZ, B * B), lambda s, inv: (inv[s * cols_n + col], 0, 0))

    edge = pl.BlockSpec((3, NZ, y_span), lambda s, inv: (0, 0, 0))
    return pl.pallas_call(
        kernel,
        grid_spec=pltpu.PrefetchScalarGridSpec(
            num_scalar_prefetch=1,
            grid=(rows_n,),
            in_specs=[flow_spec(c) for c in range(cols_n)] + [fraction_spec(c) for c in range(cols_n)],
            out_specs=[pl.BlockSpec((4, B, NZ, x_span), lambda s, inv: (0, s, 0, 0)), edge, edge],
        ),
        out_shape=[
            jax.ShapeDtypeStruct((4, y_span, NZ, x_span), f32),
            jax.ShapeDtypeStruct((3, NZ, y_span), f32),
            jax.ShapeDtypeStruct((3, NZ, y_span), f32),
        ],
        compiler_params=params(),
    )(inverse, *([velocity] * cols_n), *([fluid] * cols_n))


def advance(tile, x_below, x_above, y_below, y_above, cosine, sine_x, kinds):
    _, y_span, _, x_span = tile.shape
    steps = y_span // B
    chunks = x_span // LANES

    def kernel(kinds_ref, main_ref, prev_ref, next_ref, xb_ref, xa_ref, yb_ref, ya_ref, cosine_ref, sine_ref,
               star_ref, modes_ref, gx_ref, gy_ref, rows_ref, source_ref, carry_ref):
        step = pl.program_id(0)
        lanes = lane_ids()
        layers = lax.broadcasted_iota(jnp.int32, (NZ, LANES), 0)
        first_layer, last_layer = layers == 0, layers == NZ - 1
        first_lane, last_lane = lanes == 0, lanes == LANES - 1

        rows_ref[:, 1 : B + 1] = main_ref[:3]

        @pl.when(step == 0)
        def _():
            rows_ref[:, 0] = yb_ref[...]
            carry_ref[...] = jnp.zeros_like(carry_ref)

        @pl.when(step > 0)
        def _():
            rows_ref[:, 0] = prev_ref[:3, 0]

        @pl.when(step == steps - 1)
        def _():
            rows_ref[:, B + 1] = ya_ref[...]

        @pl.when(step < steps - 1)
        def _():
            rows_ref[:, B + 1] = next_ref[:3, 0]

        def row(j, _):
            y = step * B + j
            at = y % LANES
            y_chunk = pl.ds(pl.multiple_of(y // LANES * LANES, LANES), LANES)
            star = {}
            flow = {}
            for h in range(chunks):
                for c in range(3):
                    flow[c, h] = rows_ref[c, j + 1, :, h * LANES : (h + 1) * LANES]
            for h in range(chunks):
                part = slice(h * LANES, (h + 1) * LANES)
                take_up, take_down = [], []
                for e in range(3):
                    scaled = 0.125 * flow[e, h]
                    take_up.append(0.025 - scaled)
                    take_down.append(0.025 + scaled)
                fraction = main_ref[3, j, :, part]
                for c in range(3):
                    center = flow[c, h]
                    if h == 0:
                        before = pltpu.roll(xb_ref[c, :, y_chunk], (LANES - at) % LANES, 1)
                    else:
                        before = pltpu.roll(flow[c, h - 1], 1, 1)
                    if h == chunks - 1:
                        after = pltpu.roll(xa_ref[c, :, y_chunk], LANES - 1 - at, 1)
                    else:
                        after = pltpu.roll(flow[c, h + 1], LANES - 1, 1)
                    x_low = jnp.where(first_lane, before, pltpu.roll(center, 1, 1))
                    x_up = jnp.where(last_lane, after, pltpu.roll(center, LANES - 1, 1))
                    y_low = rows_ref[c, j, :, part]
                    y_up = rows_ref[c, j + 2, :, part]
                    z_low = jnp.where(first_layer, 0.0, pltpu.roll(center, 1, 0))
                    z_up = jnp.where(last_layer, 0.0, pltpu.roll(center, NZ - 1, 0))
                    total = (
                        0.85 * center
                        + (take_up[0] * x_up + take_down[0] * x_low)
                        + (take_up[1] * y_up + take_down[1] * y_low)
                        + (take_up[2] * z_up + take_down[2] * z_low)
                    )
                    value = fraction * total
                    if c == 2:
                        value = jnp.where(last_layer, 0.0, value)
                    star[c, h] = value
                    star_ref[c, j, :, part] = value
            for h in range(chunks):
                part = slice(h * LANES, (h + 1) * LANES)
                before = 0.0 if h == 0 else pltpu.roll(star[0, h - 1], 1, 1)
                x_low = jnp.where(first_lane, before, pltpu.roll(star[0, h], 1, 1))
                z_low = jnp.where(first_layer, 0.0, pltpu.roll(star[2, h], 1, 0))
                y_low = carry_ref[:, part]
                source_ref[j, :, part] = (x_low - star[0, h]) + (y_low - star[1, h]) + (z_low - star[2, h])
                carry_ref[:, part] = star[1, h]
            edge = pltpu.roll(star[0, chunks - 1], (at + 1) % LANES, 1)
            gx_ref[:, y_chunk] = jnp.where(lanes == at, edge, gx_ref[:, y_chunk])
            return _

        lax.fori_loop(0, B, row, 0)
        gy_ref[...] = carry_ref[...]
        for q in range(B // 8):
            part = source_ref[8 * q : 8 * q + 8].reshape(8 * NZ, x_span)
            layered = table_times(cosine_ref, part)
            modes = times_table(layered, sine_ref)
            modes_ref[:, 8 * q : 8 * q + 8, :] = modes.reshape(NZ, 8, x_span)

    full3 = pl.BlockSpec((3, NZ, y_span), lambda s, kinds: (0, 0, 0))
    return pl.pallas_call(
        kernel,
        grid_spec=pltpu.PrefetchScalarGridSpec(
            num_scalar_prefetch=1,
            grid=(steps,),
            in_specs=[
                pl.BlockSpec((4, B, NZ, x_span), lambda s, kinds: (0, s, 0, 0)),
                pl.BlockSpec((4, 1, NZ, x_span), lambda s, kinds: (0, jnp.maximum(s * B - 1, 0), 0, 0)),
                pl.BlockSpec((4, 1, NZ, x_span), lambda s, kinds: (0, jnp.minimum(s * B + B, y_span - 1), 0, 0)),
                full3,
                full3,
                pl.BlockSpec((3, NZ, x_span), lambda s, kinds: (0, 0, 0)),
                pl.BlockSpec((3, NZ, x_span), lambda s, kinds: (0, 0, 0)),
                pl.BlockSpec((2, 8 * NZ, 8 * NZ), lambda s, kinds: (0, 0, 0)),
                pl.BlockSpec((None, 2, x_span, x_span), lambda s, kinds: (kinds[1], 0, 0, 0)),
            ],
            out_specs=[
                pl.BlockSpec((3, B, NZ, x_span), lambda s, kinds: (0, s, 0, 0)),
                pl.BlockSpec((NZ, B, x_span), lambda s, kinds: (0, s, 0)),
                pl.BlockSpec((NZ, y_span), lambda s, kinds: (0, 0)),
                pl.BlockSpec((NZ, x_span), lambda s, kinds: (0, 0)),
            ],
            scratch_shapes=[
                pltpu.VMEM((3, B + 2, NZ, x_span), f32),
                pltpu.VMEM((B, NZ, x_span), f32),
                pltpu.VMEM((NZ, x_span), f32),
            ],
        ),
        out_shape=[
            jax.ShapeDtypeStruct((3, y_span, NZ, x_span), f32),
            jax.ShapeDtypeStruct((NZ, y_span, x_span), f32),
            jax.ShapeDtypeStruct((NZ, y_span), f32),
            jax.ShapeDtypeStruct((NZ, x_span), f32),
        ],
        compiler_params=params(),
    )(kinds, tile, tile, tile, x_below, x_above, y_below, y_above, cosine, sine_x)


def first_solve(modes, sine_yt, sine_xt, edge_y, edge_x, eigen, levels, kinds):
    layers, y_span, x_span = modes.shape

    def kernel(kinds_ref, modes_ref, yt_ref, xt_ref, edge_y_ref, edge_x_ref, eigen_ref, levels_ref,
               spectrum_ref, along_x_ref, along_y_ref):
        spectrum = table_times(yt_ref, modes_ref[...])
        spectrum_ref[...] = spectrum
        solved = spectrum / (eigen_ref[...] + levels_ref[pl.program_id(0)])
        row_edges = dot_full(edge_y_ref[...], solved, ((1,), (0,)))
        along_x_ref[...] = times_table(row_edges, xt_ref)
        column_edges = dot_full(edge_x_ref[...], solved, ((1,), (1,)))
        along_y_ref[...] = times_table(column_edges, yt_ref)

    return pl.pallas_call(
        kernel,
        grid_spec=pltpu.PrefetchScalarGridSpec(
            num_scalar_prefetch=1,
            grid=(layers,),
            in_specs=[
                pl.BlockSpec((None, y_span, x_span), lambda k, kinds: (k, 0, 0)),
                pl.BlockSpec((None, 2, y_span, y_span), lambda k, kinds: (kinds[0], 0, 0, 0)),
                pl.BlockSpec((None, 2, x_span, x_span), lambda k, kinds: (kinds[1], 0, 0, 0)),
                pl.BlockSpec((None, 8, y_span), lambda k, kinds: (kinds[0], 0, 0)),
                pl.BlockSpec((None, 8, x_span), lambda k, kinds: (kinds[1], 0, 0)),
                pl.BlockSpec((None, y_span, x_span), lambda k, kinds: (kinds[0] * 3 + kinds[1], 0, 0)),
                pl.BlockSpec(memory_space=pltpu.SMEM),
            ],
            out_specs=[
                pl.BlockSpec((None, y_span, x_span), lambda k, kinds: (k, 0, 0)),
                pl.BlockSpec((None, 8, x_span), lambda k, kinds: (k, 0, 0)),
                pl.BlockSpec((None, 8, y_span), lambda k, kinds: (k, 0, 0)),
            ],
        ),
        out_shape=[
            jax.ShapeDtypeStruct((layers, y_span, x_span), f32),
            jax.ShapeDtypeStruct((layers, 8, x_span), f32),
            jax.ShapeDtypeStruct((layers, 8, y_span), f32),
        ],
        compiler_params=params(),
    )(kinds, modes, sine_yt, sine_xt, edge_y, edge_x, eigen, levels)


def second_solve(spectrum, sides_y, sides_x, sine_y, sine_yt, sine_x, sine_xt, edge_y, edge_x, eigen, levels, kinds):
    layers, y_span, x_span = spectrum.shape

    def kernel(kinds_ref, spectrum_ref, sides_y_ref, sides_x_ref, y_ref, x_ref, xt_ref, edge_y_ref, edge_x_ref,
               eigen_ref, levels_ref, out_ref):
        along_x = times_table(sides_y_ref[...], x_ref)
        along_y = times_table(sides_x_ref[...], y_ref)
        left = jnp.concatenate([edge_y_ref[...], along_y], axis=0)
        right = jnp.concatenate([along_x, edge_x_ref[...]], axis=0)
        added = dot_full(left, right, ((0,), (0,)))
        solved = (spectrum_ref[...] + added) / (eigen_ref[...] + levels_ref[pl.program_id(0)])
        out_ref[...] = times_table(table_times(y_ref, solved), xt_ref)

    return pl.pallas_call(
        kernel,
        grid_spec=pltpu.PrefetchScalarGridSpec(
            num_scalar_prefetch=1,
            grid=(layers,),
            in_specs=[
                pl.BlockSpec((None, y_span, x_span), lambda k, kinds: (k, 0, 0)),
                pl.BlockSpec((None, 8, x_span), lambda k, kinds: (k, 0, 0)),
                pl.BlockSpec((None, 8, y_span), lambda k, kinds: (k, 0, 0)),
                pl.BlockSpec((None, 2, y_span, y_span), lambda k, kinds: (kinds[0], 0, 0, 0)),
                pl.BlockSpec((None, 2, x_span, x_span), lambda k, kinds: (kinds[1], 0, 0, 0)),
                pl.BlockSpec((None, 2, x_span, x_span), lambda k, kinds: (kinds[1], 0, 0, 0)),
                pl.BlockSpec((None, 8, y_span), lambda k, kinds: (kinds[0], 0, 0)),
                pl.BlockSpec((None, 8, x_span), lambda k, kinds: (kinds[1], 0, 0)),
                pl.BlockSpec((None, y_span, x_span), lambda k, kinds: (kinds[0] * 3 + kinds[1], 0, 0)),
                pl.BlockSpec(memory_space=pltpu.SMEM),
            ],
            out_specs=pl.BlockSpec((None, y_span, x_span), lambda k, kinds: (k, 0, 0)),
        ),
        out_shape=jax.ShapeDtypeStruct((layers, y_span, x_span), f32),
        compiler_params=params(),
    )(kinds, spectrum, sides_y, sides_x, sine_y, sine_x, sine_xt, edge_y, edge_x, eigen, levels)


def finish(modes, star, sum_x, sum_y, cosine_t, inverse, kinds, slots):
    layers, y_span, x_span = modes.shape
    rows_n, cols_n = y_span // B, x_span // B
    chunks = x_span // LANES

    def kernel(inverse_ref, kinds_ref, modes_ref, after_ref, star_ref, sum_x_ref, sum_y_ref, cosine_ref,
               flow_out, pressure_out, rows_ref, blocks_ref):
        step, col = pl.program_id(0), pl.program_id(1)

        @pl.when(col == 0)
        def _():
            lanes = lane_ids()
            layers_at = lax.broadcasted_iota(jnp.int32, (NZ, LANES), 0)
            last_layer = layers_at == NZ - 1
            last_lane = lanes == LANES - 1
            for q in range(B // 8):
                part = modes_ref[:, 8 * q : 8 * q + 8, :].reshape(8 * NZ, x_span)
                rows_ref[8 * q : 8 * q + 8] = table_times(cosine_ref, part).reshape(8, NZ, x_span)

            @pl.when(step < rows_n - 1)
            def _():
                part = after_ref[...].reshape(8 * NZ, x_span)
                rows_ref[B] = table_times(cosine_ref, part).reshape(8, NZ, x_span)[0]

            @pl.when(step == rows_n - 1)
            def _():
                rows_ref[B] = jnp.where(kinds_ref[0] == 2, 0.0, sum_y_ref[...] - rows_ref[B - 1])

            def four_rows(jq, _):
                y = step * B + jq * 4
                y_chunk = pl.ds(pl.multiple_of(y // LANES * LANES, LANES), LANES)
                block = pl.ds(pl.multiple_of(jq * LANES, LANES), LANES)
                for h in range(chunks):
                    part = slice(h * LANES, (h + 1) * LANES)
                    found = [[], [], [], []]
                    for t in range(4):
                        j = jq * 4 + t
                        here = rows_ref[j, :, part]
                        if h == chunks - 1:
                            after = pltpu.roll(sum_x_ref[:, y_chunk], LANES - 1 - (y + t) % LANES, 1)
                            after = jnp.where(kinds_ref[1] == 2, 0.0, after - here)
                        else:
                            after = pltpu.roll(rows_ref[j, :, (h + 1) * LANES : (h + 2) * LANES], LANES - 1, 1)
                        x_up = jnp.where(last_lane, after, pltpu.roll(here, LANES - 1, 1))
                        y_up = rows_ref[j + 1, :, part]
                        z_up = jnp.where(last_layer, here, pltpu.roll(here, NZ - 1, 0))
                        found[0].append(star_ref[0, j, :, part] - (x_up - here))
                        found[1].append(star_ref[1, j, :, part] - (y_up - here))
                        found[2].append(star_ref[2, j, :, part] - (z_up - here))
                        found[3].append(here)
                    for channel in range(4):
                        swapped = swap_groups(found[channel], lanes)
                        for g in range(4):
                            blocks_ref[4 * h + g, channel, :, block] = swapped[g]
                return _

            lax.fori_loop(0, B // 4, four_rows, 0)

        flow_out[:, 0] = blocks_ref[col, :3]
        pressure_out[0] = blocks_ref[col, 3]

    return pl.pallas_call(
        kernel,
        grid_spec=pltpu.PrefetchScalarGridSpec(
            num_scalar_prefetch=2,
            grid=(rows_n, cols_n),
            in_specs=[
                pl.BlockSpec((layers, B, x_span), lambda s, c, inv, kinds: (0, s, 0)),
                pl.BlockSpec((layers, 8, x_span), lambda s, c, inv, kinds: (0, jnp.minimum((s + 1) * (B // 8), y_span // 8 - 1), 0)),
                pl.BlockSpec((3, B, NZ, x_span), lambda s, c, inv, kinds: (0, s, 0, 0)),
                pl.BlockSpec((NZ, y_span), lambda s, c, inv, kinds: (0, 0)),
                pl.BlockSpec((NZ, x_span), lambda s, c, inv, kinds: (0, 0)),
                pl.BlockSpec((2, 8 * NZ, 8 * NZ), lambda s, c, inv, kinds: (0, 0, 0)),
            ],
            out_specs=[
                pl.BlockSpec((3, 1, NZ, B * B), lambda s, c, inv, kinds: (0, inv[s * cols_n + c], 0, 0)),
                pl.BlockSpec((1, NZ, B * B), lambda s, c, inv, kinds: (inv[s * cols_n + c], 0, 0)),
            ],
            scratch_shapes=[
                pltpu.VMEM((B + 1, NZ, x_span), f32),
                pltpu.VMEM((cols_n, 4, NZ, B * B), f32),
            ],
        ),
        out_shape=[
            jax.ShapeDtypeStruct((3, slots, NZ, B * B), f32),
            jax.ShapeDtypeStruct((slots, NZ, B * B), f32),
        ],
        compiler_params=params(),
    )(inverse, kinds, modes, modes, star, sum_x, sum_y, cosine_t)


def solve_interfaces(lines_x, lines_y, level, global_tables):
    sine_gx, sine_gy, pick_x, pick_y, eig_x, eig_y = global_tables
    count_x, count_y = lines_x.shape[1], lines_y.shape[1]
    hat_x = jnp.dot(lines_x.reshape(2 * count_x, NY), sine_gy, precision=highest)
    hat_y = jnp.dot(lines_y.reshape(2 * count_y, NX), sine_gx, precision=highest)
    left = jnp.concatenate([pick_x, hat_y], axis=0)
    right = jnp.concatenate([hat_x, pick_y], axis=0)
    field = lax.dot_general(left, right, (((0,), (0,)), ((), ())), precision=highest)
    field = field / (eig_x[:, None] + eig_y[None, :] + level)
    sum_x = hat_x[:count_x] + jnp.dot(pick_x[:count_x], field, precision=highest)
    sum_y = hat_y[:count_y] + lax.dot_general(
        pick_y[:count_y], field, (((1,), (1,)), ((), ())), precision=highest
    )
    return jnp.dot(sum_x, sine_gy, precision=highest), jnp.dot(sum_y, sine_gx, precision=highest)


def shards(tables, velocity, fluid, block_place):
    pa_size = lax.axis_size("pa")
    pb_size = lax.axis_size("pb")
    group_count = pa_size * pb_size
    y_span, x_span = NY // pa_size, NX // pb_size
    rows_n, cols_n = y_span // B, x_span // B
    slots = block_place.shape[0]
    pa, pb = lax.axis_index("pa"), lax.axis_index("pb")

    def kind(index, size):
        return jnp.where(index == 0, 0, jnp.where(index == size - 1, 2, 1)).astype(jnp.int32)

    kinds = jnp.stack([kind(pa, pa_size), kind(pb, pb_size)])
    slot_ids = jnp.arange(slots, dtype=jnp.int32)
    matches = block_place[None, :] == slot_ids[:, None]
    inverse = jnp.sum(jnp.where(matches, slot_ids[None, :], 0), axis=1).astype(jnp.int32)

    tile, low_edge, high_edge = gather_tile(velocity, fluid, inverse, rows_n, cols_n)

    def up(values, axis, size):
        return lax.ppermute(values, axis, [(i, i + 1) for i in range(size - 1)])

    def down(values, axis, size):
        return lax.ppermute(values, axis, [(i + 1, i) for i in range(size - 1)])

    x_below, x_above = up(high_edge, "pb", pb_size), down(low_edge, "pb", pb_size)
    y_below, y_above = up(tile[:3, -1], "pa", pa_size), down(tile[:3, 0], "pa", pa_size)

    cosine = jnp.asarray(tables["cosine"])
    local = {name: jnp.asarray(tables[name]) for name in ("y", "yt", "x", "xt", "edge_y", "edge_x", "eigen", "levels")}
    star, modes, flux_x, flux_y = advance(
        tile, x_below, x_above, y_below, y_above, jnp.asarray(tables["cosine8"]), local["x"], kinds
    )
    spectrum, along_x, along_y = first_solve(
        modes, local["yt"], local["xt"], local["edge_y"], local["edge_x"], local["eigen"], local["levels"], kinds
    )
    flux_x = jnp.dot(cosine, flux_x, precision=highest)
    flux_y = jnp.dot(cosine, flux_y, precision=highest)

    repeats = group_count // NZ
    bundle = jnp.concatenate(
        [
            jnp.concatenate([along_x[:, :2], flux_y[:, None]], axis=1),
            jnp.concatenate([along_y[:, :2], flux_x[:, None]], axis=1),
        ],
        axis=2,
    )
    width = x_span + y_span
    bundle = bundle.reshape(NZ, 3 * width // LANES, LANES)
    bundle = jnp.repeat(bundle, repeats, axis=0) if repeats > 1 else bundle
    arrived = lax.all_to_all(bundle, ("pa", "pb"), split_axis=0, concat_axis=0, tiled=True)
    arrived = arrived.reshape(pa_size, pb_size, 3, width)
    on_y, on_x = arrived[..., :x_span], arrived[..., x_span:]
    sums_y = on_y[:-1, :, 1] + on_y[1:, :, 0]
    lines_y = jnp.stack([sums_y, on_y[:-1, :, 2]]).reshape(2, pa_size - 1, NX)
    sums_x = on_x[:, :-1, 1] + on_x[:, 1:, 0]
    lines_x = jnp.stack([sums_x, on_x[:, :-1, 2]]).transpose(0, 2, 1, 3).reshape(2, pb_size - 1, NY)
    level = local["levels"][(pa * pb_size + pb) // repeats]
    global_tables = [jnp.asarray(tables[name]) for name in ("gx", "gy", "pick_x", "pick_y", "eig_x", "eig_y")]
    sum_x, sum_y = solve_interfaces(lines_x, lines_y, level, global_tables)
    none_y, none_x = jnp.zeros((1, NX), f32), jnp.zeros((1, NY), f32)
    high_y = jnp.concatenate([sum_y, none_y]).reshape(pa_size, pb_size, x_span)
    low_y = jnp.concatenate([none_y, sum_y + lines_y[1]]).reshape(pa_size, pb_size, x_span)
    high_x = jnp.concatenate([sum_x, none_x]).reshape(pb_size, pa_size, y_span).transpose(1, 0, 2)
    low_x = jnp.concatenate([none_x, sum_x + lines_x[1]]).reshape(pb_size, pa_size, y_span).transpose(1, 0, 2)
    reply = jnp.stack([jnp.concatenate([low_y, low_x], axis=2), jnp.concatenate([high_y, high_x], axis=2)], axis=2)
    reply = reply.reshape(group_count, 2 * width // LANES, LANES)
    home = lax.all_to_all(reply, ("pa", "pb"), split_axis=0, concat_axis=0, tiled=True)
    home = home[::repeats].reshape(NZ, 2, width)
    blank = ((0, 0), (0, 6), (0, 0))
    sides_y, sides_x = jnp.pad(home[..., :x_span], blank), jnp.pad(home[..., x_span:], blank)
    pressure_modes = second_solve(
        spectrum, sides_y, sides_x, local["y"], local["yt"], local["x"], local["xt"], local["edge_y"],
        local["edge_x"], local["eigen"], local["levels"], kinds
    )
    beyond_y = jnp.dot(cosine.T, home[:, 1, :x_span], precision=highest)
    beyond_x = jnp.dot(cosine.T, home[:, 1, x_span:], precision=highest)
    return tuple(
        finish(pressure_modes, star, beyond_x, beyond_y, jnp.asarray(tables["cosine8t"]), inverse, kinds, slots)
    )


def make_tables(pa_size, pb_size):
    y_span, x_span = NY // pa_size, NX // pb_size
    cosine, levels = cosine_basis()
    cosine8 = np.einsum("kz,ab->kabz", cosine, np.eye(8)).reshape(8 * NZ, 8 * NZ)
    tables = {
        "cosine": single(cosine),
        "levels": single(levels),
        "cosine8": split(cosine8),
        "cosine8t": split(cosine8.T),
    }
    values = {}
    for name, length in (("y", y_span), ("x", x_span)):
        bases = tile_bases(length)
        tables[name] = np.stack([split(b) for b, _ in bases])
        tables[name + "t"] = np.stack([split(b.T) for b, _ in bases])
        edges = np.zeros((3, 8, length))
        for i, (b, _) in enumerate(bases):
            edges[i, 0], edges[i, 1] = b[0], b[-1]
        tables["edge_" + name] = single(edges)
        values[name] = [v for _, v in bases]
    tables["eigen"] = single(
        np.stack([ey[:, None] + ex[None, :] for ey in values["y"] for ex in values["x"]])
    )
    for name, length, tile, size in (("x", NX, x_span, pb_size), ("y", NY, y_span, pa_size)):
        basis, eig = sine_basis(length, 1.0, 1.0)
        above = basis[tile::tile]
        below = basis[tile - 1 : length - 1 : tile]
        tables["g" + name] = single(basis)
        tables["eig_" + name] = single(eig)
        tables["pick_" + name] = single(np.concatenate([above + below, above]))
    return tables


def solution(mesh):
    tables = make_tables(mesh.shape["pa"], mesh.shape["pb"])
    return jax.shard_map(
        functools.partial(shards, tables),
        mesh=mesh,
        in_specs=(P(None, ("pa", "pb"), None, None), P(("pa", "pb"), None, None), P(("pa", "pb"))),
        out_specs=(P(None, ("pa", "pb"), None, None), P(("pa", "pb"), None, None)),
        check_vma=False,
    )
```

```python
import functools

import jax
import jax.numpy as jnp
import ml_dtypes
import numpy as np
from jax import lax
from jax.experimental import pallas as pl
from jax.experimental.pallas import tpu as pltpu
from jax.sharding import PartitionSpec as P

NX = 2048
NY = 1024
NZ = 32
B = 32
LANES = 128
highest = lax.Precision.HIGHEST
f32 = jnp.float32
VMEM_LIMIT = 56 * 1024 * 1024


def cosine_basis():
    k = np.arange(NZ)[:, None]
    z = np.arange(NZ)[None, :]
    table = np.cos(np.pi * k * (z + 0.5) / NZ)
    table /= np.sqrt((table**2).sum(axis=1, keepdims=True))
    return table, 2.0 - 2.0 * np.cos(np.pi * np.arange(NZ) / NZ)


def sine_basis(length, lower_gap, upper_gap):
    span = length - 1 + lower_gap + upper_gap
    i = np.arange(length)[:, None]
    k = np.arange(1, length + 1)[None, :]
    table = np.sin(np.pi * k * (i + lower_gap) / span)
    table /= np.sqrt((table**2).sum(axis=0, keepdims=True))
    return table, 4.0 * np.sin(np.pi * np.arange(1, length + 1) / (2 * span)) ** 2


def tile_bases(length):
    return [sine_basis(length, *gaps) for gaps in ((1.0, 0.5), (0.5, 0.5), (0.5, 1.0))]


def parts_of(table):
    table = np.asarray(table, np.float64)
    high = table.astype(np.float32).astype(ml_dtypes.bfloat16)
    low = (table - high.astype(np.float64)).astype(np.float32).astype(ml_dtypes.bfloat16)
    return high, low


def split(table):
    return np.stack(parts_of(table), axis=-3)


def left_table(table):
    high, low = parts_of(table)
    return np.concatenate([high, high, low], axis=-1)


def right_table(table):
    high, low = parts_of(table)
    return np.concatenate([high, low, high], axis=-2)


def single(table):
    return np.asarray(table, np.float32)


def pieces(values):
    high = values.astype(jnp.bfloat16)
    return high, (values - high.astype(f32)).astype(jnp.bfloat16)


def mm(left, right):
    return jnp.dot(left, right, preferred_element_type=f32)


def table_times(table_ref, values):
    high, low = pieces(values)
    return mm(table_ref[...], jnp.concatenate([high, low, high], axis=0))


def times_table(values, table_ref):
    high, low = pieces(values)
    return mm(jnp.concatenate([high, high, low], axis=1), table_ref[...])


def few_rows_times(values, high, low, product=mm):
    rows = values.shape[0]
    both = jnp.concatenate(pieces(values), axis=0)
    first = product(both, high)
    return first[:rows] + (first[rows:] + product(both[:rows], low))


def dot_full(left, right, dims):
    return lax.dot_general(left, right, (dims, ((), ())), precision=highest, preferred_element_type=f32)


def lane_ids(rows=NZ):
    return lax.broadcasted_iota(jnp.int32, (rows, LANES), 1)


def swap_groups(four, lanes):
    odd = (lanes & 32) != 0
    high = lanes >= 64
    pairs = [jnp.where(odd, four[(d + 1) % 4], four[d]) for d in range(4)]
    picked = [jnp.where(high, pairs[(d + 2) % 4], pairs[d]) for d in range(4)]
    moved = [picked[0]] + [pltpu.roll(picked[d], 32 * d, 1) for d in range(1, 4)]
    pairs = [jnp.where(odd, moved[(1 - t) % 4], moved[-t % 4]) for t in range(4)]
    return [jnp.where(high, pairs[(t - 2) % 4], pairs[t]) for t in range(4)]


def spread(part):
    high, low = pieces(part)
    return jnp.concatenate([high, high, low], axis=0)


def spread_other(part):
    high, low = pieces(part)
    return jnp.concatenate([high, low, high], axis=0)


def params():
    return pltpu.CompilerParams(vmem_limit_bytes=VMEM_LIMIT)


def gather_tile(velocity, fluid, inverse, rows_n, cols_n):
    y_span, x_span = rows_n * B, cols_n * B
    quads = cols_n // 4

    def kernel(inverse_ref, *refs):
        flow_refs = refs[:cols_n]
        fraction_refs = refs[cols_n : 2 * cols_n]
        out_ref, low_ref, high_ref = refs[2 * cols_n :]
        step = pl.program_id(0)
        lanes = lane_ids()
        place = step % 2
        chunk = pl.ds(pl.multiple_of(step // 2 * LANES, LANES), LANES)
        high_mine = ((lanes & 31) // 16) == place
        low_mine = (((lanes + 1) & 31) // 16) == place
        for channel in range(4):
            low_edge = jnp.zeros((NZ, LANES), f32)
            high_edge = jnp.zeros((NZ, LANES), f32)
            for jq in range(8):
                for quad in range(quads):
                    four = []
                    for g in range(4):
                        at = quad * 4 + g
                        part = slice(jq * LANES, (jq + 1) * LANES)
                        if channel < 3:
                            four.append(flow_refs[at][channel, 0, :, part])
                        else:
                            four.append(fraction_refs[at][0, :, part])
                    rows = swap_groups(four, lanes)
                    for t in range(4):
                        out_ref[channel, jq * 4 + t, :, quad * LANES : (quad + 1) * LANES] = rows[t]
                    if channel < 3 and quad == 0:
                        here = ((lanes + 1) & 31) == 2 * jq
                        low_edge = jnp.where(here, pltpu.roll(four[0], (2 * jq + 127) % LANES, 1), low_edge)
                    if channel < 3 and quad == quads - 1:
                        here = (lanes & 31) == 2 * jq
                        high_edge = jnp.where(here, pltpu.roll(four[3], 97 + 2 * jq, 1), high_edge)
            if channel < 3:
                shift = place * 16
                low_ref[channel, :, chunk] = jnp.where(low_mine, pltpu.roll(low_edge, shift, 1), low_ref[channel, :, chunk])
                high_ref[channel, :, chunk] = jnp.where(
                    high_mine, pltpu.roll(high_edge, shift, 1), high_ref[channel, :, chunk])

    def flow_spec(col):
        return pl.BlockSpec((3, 1, NZ, B * B), lambda s, inv: (0, inv[s * cols_n + col], 0, 0))

    def fraction_spec(col):
        return pl.BlockSpec((1, NZ, B * B), lambda s, inv: (inv[s * cols_n + col], 0, 0))

    edge = pl.BlockSpec((3, NZ, 2 * y_span), lambda s, inv: (0, 0, 0))
    return pl.pallas_call(
        kernel,
        grid_spec=pltpu.PrefetchScalarGridSpec(
            num_scalar_prefetch=1,
            grid=(rows_n,),
            in_specs=[flow_spec(c) for c in range(cols_n)] + [fraction_spec(c) for c in range(cols_n)],
            out_specs=[pl.BlockSpec((4, B, NZ, x_span), lambda s, inv: (0, s, 0, 0)), edge, edge],
        ),
        out_shape=[
            jax.ShapeDtypeStruct((4, y_span, NZ, x_span), f32),
            jax.ShapeDtypeStruct((3, NZ, 2 * y_span), f32),
            jax.ShapeDtypeStruct((3, NZ, 2 * y_span), f32),
        ],
        compiler_params=params(),
    )(inverse, *([velocity] * cols_n), *([fluid] * cols_n))


def advance(tile, x_below, x_above, y_below, y_above, cosine, sine_x, kinds):
    _, y_span, _, x_span = tile.shape
    steps = y_span // B
    chunks = x_span // LANES

    def kernel(kinds_ref, main_ref, prev_ref, next_ref, xb_ref, xa_ref, yb_ref, ya_ref, cosine_ref, sine_ref,
               star_ref, modes_ref, gx_ref, gy_ref, rows_ref, source_ref, carry_ref):
        step = pl.program_id(0)
        lanes = lane_ids()
        layers = lax.broadcasted_iota(jnp.int32, (NZ, LANES), 0)
        first_layer, last_layer = layers == 0, layers == NZ - 1
        first_lane, last_lane = lanes == 0, lanes == LANES - 1

        rows_ref[:, 1 : B + 1] = main_ref[:3]

        @pl.when(step == 0)
        def _():
            rows_ref[:, 0] = yb_ref[...]
            carry_ref[...] = jnp.zeros_like(carry_ref)

        @pl.when(step > 0)
        def _():
            rows_ref[:, 0] = prev_ref[:3, 0]

        @pl.when(step == steps - 1)
        def _():
            rows_ref[:, B + 1] = ya_ref[...]

        @pl.when(step < steps - 1)
        def _():
            rows_ref[:, B + 1] = next_ref[:3, 0]

        y_chunk = pl.ds(pl.multiple_of(step // 4 * LANES, LANES), LANES)
        halo_chunk = pl.ds(pl.multiple_of(step // 2 * LANES, LANES), LANES)
        even_lane = (lanes & 1) == 0

        def row(group, r):
            j = group * 8 + r
            held = r % 4 * 32 + (step % 2) * 16 + 2 * (group * 2 + r // 4)
            at = (step % 4) * B + j
            star = {}
            flow = {}
            for h in range(chunks):
                for c in range(3):
                    flow[c, h] = rows_ref[c, j + 1, :, h * LANES : (h + 1) * LANES]
            edge, to_right, to_left = {}, {}, {}
            for c in range(3):
                both = jnp.where(even_lane, xb_ref[c, :, halo_chunk], xa_ref[c, :, halo_chunk])
                edge[c] = pltpu.roll(both, (LANES - held) % LANES, 1)
                for h in range(chunks):
                    to_right[c, h] = pltpu.roll(flow[c, h], 1, 1)
                    to_left[c, h] = pltpu.roll(flow[c, h], LANES - 1, 1)
            for h in range(chunks):
                part = slice(h * LANES, (h + 1) * LANES)
                take_up, take_down = [], []
                for e in range(3):
                    scaled = 0.125 * flow[e, h]
                    take_up.append(0.025 - scaled)
                    take_down.append(0.025 + scaled)
                fraction = main_ref[3, j, :, part]
                for c in range(3):
                    center = flow[c, h]
                    before = edge[c] if h == 0 else to_right[c, h - 1]
                    after = edge[c] if h == chunks - 1 else to_left[c, h + 1]
                    x_low = jnp.where(first_lane, before, to_right[c, h])
                    x_up = jnp.where(last_lane, after, to_left[c, h])
                    y_low = rows_ref[c, j, :, part]
                    y_up = rows_ref[c, j + 2, :, part]
                    z_low = jnp.where(first_layer, 0.0, pltpu.roll(center, 1, 0))
                    z_up = jnp.where(last_layer, 0.0, pltpu.roll(center, NZ - 1, 0))
                    total = (
                        0.85 * center
                        + (take_up[0] * x_up + take_down[0] * x_low)
                        + (take_up[1] * y_up + take_down[1] * y_low)
                        + (take_up[2] * z_up + take_down[2] * z_low)
                    )
                    value = fraction * total
                    if c == 2:
                        value = jnp.where(last_layer, 0.0, value)
                    star[c, h] = value
                    star_ref[c, j, :, part] = value
            before = 0.0
            for h in range(chunks):
                part = slice(h * LANES, (h + 1) * LANES)
                moved = pltpu.roll(star[0, h], 1, 1)
                x_low = jnp.where(first_lane, before, moved)
                before = moved
                z_low = jnp.where(first_layer, 0.0, pltpu.roll(star[2, h], 1, 0))
                y_low = carry_ref[:, part]
                source_ref[j, :, part] = (x_low - star[0, h]) + (y_low - star[1, h]) + (z_low - star[2, h])
                carry_ref[:, part] = star[1, h]
            edge = pltpu.roll(star[0, chunks - 1], (at + 1) % LANES, 1)
            gx_ref[:, y_chunk] = jnp.where(lanes == at, edge, gx_ref[:, y_chunk])

        def transform(group):
            rows = pl.ds(pl.multiple_of(group * 8, 8), 8)
            part = source_ref[rows].reshape(8 * NZ, x_span)
            modes = times_table(table_times(cosine_ref, part), sine_ref)
            modes_ref[:, rows, :] = modes.reshape(NZ, 8, x_span)

        for r in range(8):
            row(0, r)

        def group_of_rows(group, _):
            transform(group - 1)
            for r in range(8):
                row(group, r)
            return _

        lax.fori_loop(1, B // 8, group_of_rows, 0)
        transform(B // 8 - 1)
        gy_ref[...] = carry_ref[...]

    full3 = pl.BlockSpec((3, NZ, 2 * y_span), lambda s, kinds: (0, 0, 0))
    return pl.pallas_call(
        kernel,
        grid_spec=pltpu.PrefetchScalarGridSpec(
            num_scalar_prefetch=1,
            grid=(steps,),
            in_specs=[
                pl.BlockSpec((4, B, NZ, x_span), lambda s, kinds: (0, s, 0, 0)),
                pl.BlockSpec((4, 1, NZ, x_span), lambda s, kinds: (0, jnp.maximum(s * B - 1, 0), 0, 0)),
                pl.BlockSpec((4, 1, NZ, x_span), lambda s, kinds: (0, jnp.minimum(s * B + B, y_span - 1), 0, 0)),
                full3,
                full3,
                pl.BlockSpec((3, NZ, x_span), lambda s, kinds: (0, 0, 0)),
                pl.BlockSpec((3, NZ, x_span), lambda s, kinds: (0, 0, 0)),
                pl.BlockSpec((8 * NZ, 24 * NZ), lambda s, kinds: (0, 0)),
                pl.BlockSpec((None, 3 * x_span, x_span), lambda s, kinds: (kinds[1], 0, 0)),
            ],
            out_specs=[
                pl.BlockSpec((3, B, NZ, x_span), lambda s, kinds: (0, s, 0, 0)),
                pl.BlockSpec((NZ, B, x_span), lambda s, kinds: (0, s, 0)),
                pl.BlockSpec((NZ, y_span), lambda s, kinds: (0, 0)),
                pl.BlockSpec((NZ, x_span), lambda s, kinds: (0, 0)),
            ],
            scratch_shapes=[
                pltpu.VMEM((3, B + 2, NZ, x_span), f32),
                pltpu.VMEM((B, NZ, x_span), f32),
                pltpu.VMEM((NZ, x_span), f32),
            ],
        ),
        out_shape=[
            jax.ShapeDtypeStruct((3, y_span, NZ, x_span), f32),
            jax.ShapeDtypeStruct((NZ, y_span, x_span), f32),
            jax.ShapeDtypeStruct((NZ, y_span), f32),
            jax.ShapeDtypeStruct((NZ, x_span), f32),
        ],
        compiler_params=params(),
    )(kinds, tile, tile, tile, x_below, x_above, y_below, y_above, cosine, sine_x)


def first_solve(modes, sine_y, sine_yt, sine_xt, edge_y, edge_xt, eigen, levels, flux_x, flux_y, cosine, kinds):
    layers, y_span, x_span = modes.shape
    batch = 4
    steps = layers // batch
    sides = 2 * layers

    def kernel(kinds_ref, modes_ref, y_ref, yt_ref, xt_ref, edge_y_ref, edge_xt_ref, eigen_ref, levels_ref,
               flux_x_ref, flux_y_ref, cosine_ref, spectrum_ref, bundle_ref, rows_ref, columns_ref):
        step = pl.program_id(0)
        row_ids = lax.broadcasted_iota(jnp.int32, (sides, y_span), 0)
        column_ids = lax.broadcasted_iota(jnp.int32, (x_span, LANES), 1)

        @pl.when(step == 0)
        def _():
            rows_ref[...] = jnp.zeros_like(rows_ref)
            columns_ref[...] = jnp.zeros_like(columns_ref)

        row_sum, column_sum = [], []
        for i in range(batch):
            k = step * batch + i
            spectrum = table_times(yt_ref, modes_ref[i])
            spectrum_ref[i] = spectrum
            high, low = pieces(spectrum / (eigen_ref[...] + levels_ref[k]))
            edge_high, edge_low = pieces(jnp.where(row_ids % layers == k, edge_y_ref[...], 0.0))
            edges = jnp.concatenate([edge_high, edge_low], axis=0)
            found = mm(edges, high)
            row_sum.append(found[:sides] + (found[sides:] + mm(edge_high, low)))
            edge_high, edge_low = pieces(jnp.where(column_ids % layers == k, edge_xt_ref[...], 0.0))
            column_sum.append(mm(
                jnp.concatenate([high, high, low], axis=1),
                jnp.concatenate([edge_high, edge_low, edge_high], axis=0)))
        rows_ref[...] += (row_sum[0] + row_sum[1]) + (row_sum[2] + row_sum[3])
        columns_ref[...] += (column_sum[0] + column_sum[1]) + (column_sum[2] + column_sum[3])

        @pl.when(step == steps - 1)
        def _():
            along_x = times_table(rows_ref[...], xt_ref)
            along_y = table_times(y_ref, columns_ref[...]).T[:sides]
            cosine_table = cosine_ref[...]
            for line, values, flux_ref in ((0, along_x, flux_y_ref), (x_span, along_y, flux_x_ref)):
                part = slice(line, line + values.shape[1])
                bundle_ref[0, :, part] = values[:layers]
                bundle_ref[1, :, part] = values[layers:]
                bundle_ref[2, :, part] = dot_full(cosine_table, flux_ref[...], ((1,), (0,)))

    return pl.pallas_call(
        kernel,
        grid_spec=pltpu.PrefetchScalarGridSpec(
            num_scalar_prefetch=1,
            grid=(steps,),
            in_specs=[
                pl.BlockSpec((batch, y_span, x_span), lambda k, kinds: (k, 0, 0)),
                pl.BlockSpec((None, y_span, 3 * y_span), lambda k, kinds: (kinds[0], 0, 0)),
                pl.BlockSpec((None, y_span, 3 * y_span), lambda k, kinds: (kinds[0], 0, 0)),
                pl.BlockSpec((None, 3 * x_span, x_span), lambda k, kinds: (kinds[1], 0, 0)),
                pl.BlockSpec((None, sides, y_span), lambda k, kinds: (kinds[0], 0, 0)),
                pl.BlockSpec((None, x_span, LANES), lambda k, kinds: (kinds[1], 0, 0)),
                pl.BlockSpec((None, y_span, x_span), lambda k, kinds: (kinds[0] * 3 + kinds[1], 0, 0)),
                pl.BlockSpec(memory_space=pltpu.SMEM),
                pl.BlockSpec((layers, y_span), lambda k, kinds: (0, 0)),
                pl.BlockSpec((layers, x_span), lambda k, kinds: (0, 0)),
                pl.BlockSpec((layers, layers), lambda k, kinds: (0, 0)),
            ],
            out_specs=[
                pl.BlockSpec((batch, y_span, x_span), lambda k, kinds: (k, 0, 0)),
                pl.BlockSpec((3, layers, x_span + y_span), lambda k, kinds: (0, 0, 0)),
            ],
            scratch_shapes=[pltpu.VMEM((sides, x_span), f32), pltpu.VMEM((y_span, LANES), f32)],
        ),
        out_shape=[
            jax.ShapeDtypeStruct((layers, y_span, x_span), f32),
            jax.ShapeDtypeStruct((3, layers, x_span + y_span), f32),
        ],
        compiler_params=params(),
    )(kinds, modes, sine_y, sine_yt, sine_xt, edge_y, edge_xt, eigen, levels, flux_x, flux_y, cosine)


def second_solve(spectrum, sums, sine_y, sine_yr, sine_x, sine_xt, edge_y, edge_x, eigen, levels, kinds):
    layers, y_span, x_span = spectrum.shape
    batch = 4
    sides = 2 * layers

    def kernel(kinds_ref, spectrum_ref, sums_ref, y_ref, yr_ref, x_ref, xt_ref, edge_y_ref, edge_x_ref,
               eigen_ref, levels_ref, out_ref, left_ref, right_ref):
        step = pl.program_id(0)

        @pl.when(step == 0)
        def _():
            right_ref[:sides] = edge_x_ref[...]
            right_ref[sides:] = times_table(sums_ref[:, :x_span], x_ref)
            left = jnp.concatenate([times_table(sums_ref[:, x_span:], yr_ref), edge_y_ref[...]], axis=0)
            left_high, left_low = pieces(left.T)
            left_ref[...] = jnp.concatenate([left_high, left_high, left_low], axis=1)

        row_ids = lax.broadcasted_iota(jnp.int32, (2 * sides, x_span), 0) % layers
        for i in range(batch):
            k = step * batch + i
            high, low = pieces(jnp.where(row_ids == k, right_ref[...], 0.0))
            added = mm(left_ref[...], jnp.concatenate([high, low, high], axis=0))
            solved = (spectrum_ref[i] + added) / (eigen_ref[...] + levels_ref[k])
            out_ref[i] = times_table(table_times(y_ref, solved), xt_ref)

    return pl.pallas_call(
        kernel,
        grid_spec=pltpu.PrefetchScalarGridSpec(
            num_scalar_prefetch=1,
            grid=(layers // batch,),
            in_specs=[
                pl.BlockSpec((batch, y_span, x_span), lambda k, kinds: (k, 0, 0)),
                pl.BlockSpec((sides, x_span + y_span), lambda k, kinds: (0, 0)),
                pl.BlockSpec((None, y_span, 3 * y_span), lambda k, kinds: (kinds[0], 0, 0)),
                pl.BlockSpec((None, 3 * y_span, y_span), lambda k, kinds: (kinds[0], 0, 0)),
                pl.BlockSpec((None, 3 * x_span, x_span), lambda k, kinds: (kinds[1], 0, 0)),
                pl.BlockSpec((None, 3 * x_span, x_span), lambda k, kinds: (kinds[1], 0, 0)),
                pl.BlockSpec((None, sides, y_span), lambda k, kinds: (kinds[0], 0, 0)),
                pl.BlockSpec((None, sides, x_span), lambda k, kinds: (kinds[1], 0, 0)),
                pl.BlockSpec((None, y_span, x_span), lambda k, kinds: (kinds[0] * 3 + kinds[1], 0, 0)),
                pl.BlockSpec(memory_space=pltpu.SMEM),
            ],
            out_specs=pl.BlockSpec((batch, y_span, x_span), lambda k, kinds: (k, 0, 0)),
            scratch_shapes=[
                pltpu.VMEM((y_span, 6 * sides), jnp.bfloat16),
                pltpu.VMEM((2 * sides, x_span), f32),
            ],
        ),
        out_shape=jax.ShapeDtypeStruct((layers, y_span, x_span), f32),
        compiler_params=params(),
    )(kinds, spectrum, sums, sine_y, sine_yr, sine_x, sine_xt, edge_y, edge_x, eigen, levels)


def finish(modes, star, sums, cosine_inverse, cosine_t, inverse, kinds, slots):
    layers, y_span, x_span = modes.shape
    rows_n, cols_n = y_span // B, x_span // B
    chunks = x_span // LANES

    def kernel(inverse_ref, kinds_ref, modes_ref, after_ref, star_ref, sums_ref, inverse_cosine_ref, cosine_ref,
               flow_out, pressure_out, rows_ref, blocks_ref, beyond_ref, flow_sem, pressure_sem):
        step = pl.program_id(0)
        half = step % 2

        def copies(at_step, at_half):
            found = []
            for col in range(cols_n):
                slot = inverse_ref[at_step * cols_n + col]
                found.append(pltpu.make_async_copy(
                    blocks_ref.at[at_half, col, pl.ds(0, 3)], flow_out.at[:, slot], flow_sem.at[at_half, col]))
                found.append(pltpu.make_async_copy(
                    blocks_ref.at[at_half, col, 3], pressure_out.at[slot], pressure_sem.at[at_half, col]))
            return found

        @pl.when(step >= 2)
        def _():
            for copy in copies(step - 2, half):
                copy.wait()

        @pl.when(step == 0)
        def _():
            beyond_ref[...] = dot_full(inverse_cosine_ref[...], sums_ref[layers:], ((1,), (0,)))

        lanes = lane_ids()
        layers_at = lax.broadcasted_iota(jnp.int32, (NZ, LANES), 0)
        last_layer = layers_at == NZ - 1
        last_lane = lanes == LANES - 1
        for q in range(B // 8):
            part = modes_ref[:, 8 * q : 8 * q + 8, :].reshape(8 * NZ, x_span)
            rows_ref[8 * q : 8 * q + 8] = table_times(cosine_ref, part).reshape(8, NZ, x_span)

        @pl.when(step < rows_n - 1)
        def _():
            part = after_ref[...].reshape(8 * NZ, x_span)
            rows_ref[B] = table_times(cosine_ref, part).reshape(8, NZ, x_span)[0]

        @pl.when(step == rows_n - 1)
        def _():
            rows_ref[B] = jnp.where(kinds_ref[0] == 2, 0.0, beyond_ref[:, :x_span] - rows_ref[B - 1])

        def four_rows(jq, _):
            y = step * B + jq * 4
            y_chunk = pl.ds(pl.multiple_of(x_span + y // LANES * LANES, LANES), LANES)
            block = pl.ds(pl.multiple_of(jq * LANES, LANES), LANES)
            to_left = [
                [pltpu.roll(rows_ref[jq * 4 + t, :, h * LANES : (h + 1) * LANES], LANES - 1, 1) for t in range(4)]
                for h in range(chunks)
            ]
            for h in range(chunks):
                part = slice(h * LANES, (h + 1) * LANES)
                found = [[], [], [], []]
                for t in range(4):
                    j = jq * 4 + t
                    here = rows_ref[j, :, part]
                    if h == chunks - 1:
                        after = pltpu.roll(beyond_ref[:, y_chunk], LANES - 1 - (y + t) % LANES, 1)
                        after = jnp.where(kinds_ref[1] == 2, 0.0, after - here)
                    else:
                        after = to_left[h + 1][t]
                    x_up = jnp.where(last_lane, after, to_left[h][t])
                    y_up = rows_ref[j + 1, :, part]
                    z_up = jnp.where(last_layer, here, pltpu.roll(here, NZ - 1, 0))
                    found[0].append(star_ref[0, j, :, part] - (x_up - here))
                    found[1].append(star_ref[1, j, :, part] - (y_up - here))
                    found[2].append(star_ref[2, j, :, part] - (z_up - here))
                    found[3].append(here)
                for channel in range(4):
                    swapped = swap_groups(found[channel], lanes)
                    for g in range(4):
                        blocks_ref[half, 4 * h + g, channel, :, block] = swapped[g]
            return _

        lax.fori_loop(0, B // 4, four_rows, 0)

        for copy in copies(step, half):
            copy.start()

        @pl.when(step == rows_n - 1)
        def _():
            for copy in copies(step - 1, 1 - half) + copies(step, half):
                copy.wait()

    return pl.pallas_call(
        kernel,
        grid_spec=pltpu.PrefetchScalarGridSpec(
            num_scalar_prefetch=2,
            grid=(rows_n,),
            in_specs=[
                pl.BlockSpec((layers, B, x_span), lambda s, inv, kinds: (0, s, 0)),
                pl.BlockSpec((layers, 8, x_span), lambda s, inv, kinds: (0, jnp.minimum((s + 1) * (B // 8), y_span // 8 - 1), 0)),
                pl.BlockSpec((3, B, NZ, x_span), lambda s, inv, kinds: (0, s, 0, 0)),
                pl.BlockSpec((2 * layers, x_span + y_span), lambda s, inv, kinds: (0, 0)),
                pl.BlockSpec((layers, layers), lambda s, inv, kinds: (0, 0)),
                pl.BlockSpec((8 * NZ, 24 * NZ), lambda s, inv, kinds: (0, 0)),
            ],
            out_specs=[pl.BlockSpec(memory_space=pl.ANY), pl.BlockSpec(memory_space=pl.ANY)],
            scratch_shapes=[
                pltpu.VMEM((B + 1, NZ, x_span), f32),
                pltpu.VMEM((2, cols_n, 4, NZ, B * B), f32),
                pltpu.VMEM((NZ, x_span + y_span), f32),
                pltpu.SemaphoreType.DMA((2, cols_n)),
                pltpu.SemaphoreType.DMA((2, cols_n)),
            ],
        ),
        out_shape=[
            jax.ShapeDtypeStruct((3, slots, NZ, B * B), f32),
            jax.ShapeDtypeStruct((slots, NZ, B * B), f32),
        ],
        compiler_params=params(),
    )(inverse, kinds, modes, modes, star, sums, cosine_inverse, cosine_t)


def solve_interfaces(lines_x, lines_y, picks_x, picks_y, table_x, table_y, eig_x, eig_y, levels, kinds):
    rows_x, rows_y = lines_x.shape[0], lines_y.shape[1]
    half_x = lines_y.shape[2]
    width = min(256, half_x)

    def kernel(kinds_ref, lines_x_ref, lines_y_ref, picks_x_ref, picks_y_ref, table_x_ref, table_y_ref, eig_x_ref,
               eig_y_ref, levels_ref, sum_x_ref, fold_ref, hat_ref, out_hat_ref):
        level = levels_ref[kinds_ref[2]]
        hat_x = few_rows_times(lines_x_ref[...], table_y_ref[0], table_y_ref[1])
        for parity in range(2):
            hat_ref[:, parity * half_x : (parity + 1) * half_x] = few_rows_times(
                lines_y_ref[parity], table_x_ref[parity, 0], table_x_ref[parity, 1])
        right = spread(jnp.concatenate([hat_x, picks_y_ref[0]], axis=0))

        def transposed(a, b):
            return lax.dot_general(a, b, (((1,), (1,)), ((), ())), preferred_element_type=f32)

        along = jnp.zeros((rows_x, NY), f32)
        for start in range(0, 2 * half_x, width):
            part = slice(start, start + width)
            left = spread_other(jnp.concatenate([picks_x_ref[0, :, part], hat_ref[:, part]], axis=0))
            field = lax.dot_general(left, right, (((0,), (0,)), ((), ())), preferred_element_type=f32)
            field = field / (eig_x_ref[part, :1] + eig_y_ref[:1] + level)
            high, low = pieces(field)
            along += few_rows_times(picks_x_ref[1, :, part], high, low)
            out_hat_ref[:, part] = hat_ref[:, part] + few_rows_times(picks_y_ref[1], high, low, transposed)
        sum_x_ref[...] = few_rows_times(hat_x + along, table_y_ref[0], table_y_ref[1])
        for parity in range(2):
            fold_ref[parity] = few_rows_times(
                out_hat_ref[:, parity * half_x : (parity + 1) * half_x],
                table_x_ref[parity, 0], table_x_ref[parity, 1], transposed)

    vmem = pl.BlockSpec(memory_space=pltpu.VMEM)
    return pl.pallas_call(
        kernel,
        grid_spec=pltpu.PrefetchScalarGridSpec(
            num_scalar_prefetch=1,
            grid=(),
            in_specs=[vmem] * 8 + [pl.BlockSpec(memory_space=pltpu.SMEM)],
            out_specs=[vmem, vmem],
            scratch_shapes=[pltpu.VMEM((rows_y, NX), f32), pltpu.VMEM((rows_y, NX), f32)],
        ),
        out_shape=[
            jax.ShapeDtypeStruct((rows_x, NY), f32),
            jax.ShapeDtypeStruct((2, rows_y, half_x), f32),
        ],
        compiler_params=params(),
    )(kinds, lines_x, lines_y, picks_x, picks_y, table_x, table_y, eig_x, eig_y, levels)


def padded_rows(count):
    return -(-2 * count // 16) * 16


def shards(tables, velocity, fluid, block_place):
    pa_size = lax.axis_size("pa")
    pb_size = lax.axis_size("pb")
    group_count = pa_size * pb_size
    y_span, x_span = NY // pa_size, NX // pb_size
    rows_n, cols_n = y_span // B, x_span // B
    slots = block_place.shape[0]
    pa, pb = lax.axis_index("pa"), lax.axis_index("pb")

    def kind(index, size):
        return jnp.where(index == 0, 0, jnp.where(index == size - 1, 2, 1)).astype(jnp.int32)

    repeats = group_count // NZ
    kinds = jnp.stack([kind(pa, pa_size), kind(pb, pb_size), (pa * pb_size + pb) // repeats])
    slot_ids = jnp.arange(slots, dtype=jnp.int32)
    matches = block_place[None, :] == slot_ids[:, None]
    inverse = jnp.sum(jnp.where(matches, slot_ids[None, :], 0), axis=1).astype(jnp.int32)

    tile, low_edge, high_edge = gather_tile(velocity, fluid, inverse, rows_n, cols_n)

    def up(values, axis, size):
        return lax.ppermute(values, axis, [(i, i + 1) for i in range(size - 1)])

    def down(values, axis, size):
        return lax.ppermute(values, axis, [(i + 1, i) for i in range(size - 1)])

    x_below, x_above = up(high_edge, "pb", pb_size), down(low_edge, "pb", pb_size)
    y_below, y_above = up(tile[:3, -1], "pa", pa_size), down(tile[:3, 0], "pa", pa_size)

    cosine = jnp.asarray(tables["cosine"])
    local = {name: jnp.asarray(tables[name]) for name in (
        "y", "yr", "yt", "x", "xt", "edge_y", "edge_x", "edge_xt", "eigen", "levels", "picks_x", "picks_y", "fold_x", "line_y",
        "eig_x", "eig_y")}
    star, modes, flux_x, flux_y = advance(
        tile, x_below, x_above, y_below, y_above, jnp.asarray(tables["cosine8"]), local["x"], kinds
    )
    spectrum, bundle = first_solve(
        modes, local["y"], local["yt"], local["xt"], local["edge_y"], local["edge_xt"], local["eigen"],
        local["levels"], flux_x, flux_y, cosine, kinds
    )
    width = x_span + y_span
    bundle = jnp.repeat(bundle, repeats, axis=1) if repeats > 1 else bundle
    arrived = lax.all_to_all(bundle, ("pa", "pb"), split_axis=1, concat_axis=1, tiled=True)
    arrived = arrived.reshape(3, pa_size, pb_size, width)
    on_y, on_x = arrived[..., :x_span], arrived[..., x_span:]
    count_y, count_x = pa_size - 1, pb_size - 1
    rows_y, rows_x = padded_rows(count_y), padded_rows(count_x)
    sums_y = on_y[1, :-1] + on_y[0, 1:]
    lines_y = jnp.concatenate([sums_y, on_y[2, :-1]]).reshape(2 * count_y, NX)
    lines_y = jnp.pad(lines_y, ((0, rows_y - 2 * count_y), (0, 0)))
    sums_x = on_x[1, :, :-1] + on_x[0, :, 1:]
    lines_x = jnp.stack([sums_x, on_x[2, :, :-1]]).transpose(0, 2, 1, 3).reshape(2 * count_x, NY)
    lines_x = jnp.pad(lines_x, ((0, rows_x - 2 * count_x), (0, 0)))
    lower, upper = lines_y[:, : NX // 2], lines_y[:, NX // 2 :][:, ::-1]
    sum_x, folded = solve_interfaces(
        lines_x, jnp.stack([lower + upper, lower - upper]), local["picks_x"], local["picks_y"], local["fold_x"],
        local["line_y"], local["eig_x"], local["eig_y"], local["levels"], kinds
    )
    sum_x = sum_x[:count_x]
    even, odd = folded[0, :count_y], folded[1, :count_y]
    sum_y = jnp.concatenate([even + odd, (even - odd)[:, ::-1]], axis=1)
    flux_y, flux_x = lines_y[count_y : 2 * count_y], lines_x[count_x : 2 * count_x]
    none_y, none_x = jnp.zeros((1, NX), f32), jnp.zeros((1, NY), f32)
    high_y = jnp.concatenate([sum_y, none_y]).reshape(pa_size, pb_size, x_span)
    low_y = jnp.concatenate([none_y, sum_y + flux_y]).reshape(pa_size, pb_size, x_span)
    high_x = jnp.concatenate([sum_x, none_x]).reshape(pb_size, pa_size, y_span).transpose(1, 0, 2)
    low_x = jnp.concatenate([none_x, sum_x + flux_x]).reshape(pb_size, pa_size, y_span).transpose(1, 0, 2)
    reply = jnp.stack([jnp.concatenate([low_y, low_x], axis=2), jnp.concatenate([high_y, high_x], axis=2)])
    reply = reply.reshape(2, group_count, width)
    home = lax.all_to_all(reply, ("pa", "pb"), split_axis=1, concat_axis=1, tiled=True)
    sums = home[:, ::repeats].reshape(2 * NZ, width)
    pressure_modes = second_solve(
        spectrum, sums, local["y"], local["yr"], local["x"], local["xt"], local["edge_y"], local["edge_x"],
        local["eigen"], local["levels"], kinds
    )
    return tuple(
        finish(pressure_modes, star, sums, jnp.asarray(tables["cosine_t"]), jnp.asarray(tables["cosine8t"]), inverse,
               kinds, slots)
    )


def make_tables(pa_size, pb_size):
    y_span, x_span = NY // pa_size, NX // pb_size
    cosine, levels = cosine_basis()
    cosine8 = np.einsum("kz,ab->kabz", cosine, np.eye(8)).reshape(8 * NZ, 8 * NZ)
    tables = {
        "cosine": single(cosine),
        "levels": single(levels),
        "cosine_t": single(cosine.T),
        "cosine8": left_table(cosine8),
        "cosine8t": left_table(cosine8.T),
    }
    values = {}
    for name, length in (("y", y_span), ("x", x_span)):
        bases = tile_bases(length)
        if name == "x":
            tables["x"] = np.stack([right_table(b) for b, _ in bases])
            tables["xt"] = np.stack([right_table(b.T) for b, _ in bases])
        else:
            tables["y"] = np.stack([left_table(b) for b, _ in bases])
            tables["yr"] = np.stack([right_table(b) for b, _ in bases])
            tables["yt"] = np.stack([left_table(b.T) for b, _ in bases])
        edges = np.stack([np.repeat(b[[0, -1]], NZ, axis=0) for b, _ in bases])
        tables["edge_" + name] = single(edges)
        blank = np.zeros((3, length, LANES - 2 * NZ))
        tables["edge_" + name + "t"] = single(np.concatenate([edges.transpose(0, 2, 1), blank], axis=2))
        values[name] = [v for _, v in bases]
    tables["eigen"] = single(
        np.stack([ey[:, None] + ex[None, :] for ey in values["y"] for ex in values["x"]])
    )
    basis_x, eig_x = sine_basis(NX, 1.0, 1.0)
    basis_y, eig_y = sine_basis(NY, 1.0, 1.0)
    half = NX // 2
    order = np.concatenate([np.arange(0, NX, 2), np.arange(1, NX, 2)])
    tables["fold_x"] = np.stack([split(basis_x[:half, parity::2]) for parity in range(2)])
    tables["line_y"] = split(basis_y)
    tables["eig_x"] = single(np.repeat(eig_x[order][:, None], LANES, axis=1))
    tables["eig_y"] = single(np.repeat(eig_y[None, :], 8, axis=0))
    for name, basis, tile in (("x", basis_x[:, order], x_span), ("y", basis_y, y_span)):
        above, below = basis[tile::tile], basis[tile - 1 : -1 : tile]
        count, length = above.shape
        picks = np.zeros((2, padded_rows(count), length))
        picks[0, : 2 * count] = np.concatenate([above + below, above])
        picks[1, :count] = above + below
        tables["picks_" + name] = single(picks)
    return tables


def solution(mesh):
    tables = make_tables(mesh.shape["pa"], mesh.shape["pb"])
    return jax.shard_map(
        functools.partial(shards, tables),
        mesh=mesh,
        in_specs=(P(None, ("pa", "pb"), None, None), P(("pa", "pb"), None, None), P(("pa", "pb"))),
        out_specs=(P(None, ("pa", "pb"), None, None), P(("pa", "pb"), None, None)),
        check_vma=False,
    )
```

```python
import functools

import jax
import jax.numpy as jnp
import ml_dtypes
import numpy as np
from jax import lax
from jax.experimental import pallas as pl
from jax.experimental.pallas import tpu as pltpu
from jax.sharding import PartitionSpec as P

NX = 2048
NY = 1024
NZ = 32
B = 32
LANES = 128
highest = lax.Precision.HIGHEST
f32 = jnp.float32
VMEM_LIMIT = 56 * 1024 * 1024


def cosine_basis():
    k = np.arange(NZ)[:, None]
    z = np.arange(NZ)[None, :]
    table = np.cos(np.pi * k * (z + 0.5) / NZ)
    table /= np.sqrt((table**2).sum(axis=1, keepdims=True))
    return table, 2.0 - 2.0 * np.cos(np.pi * np.arange(NZ) / NZ)


def sine_basis(length, lower_gap, upper_gap):
    span = length - 1 + lower_gap + upper_gap
    i = np.arange(length)[:, None]
    k = np.arange(1, length + 1)[None, :]
    table = np.sin(np.pi * k * (i + lower_gap) / span)
    table /= np.sqrt((table**2).sum(axis=0, keepdims=True))
    return table, 4.0 * np.sin(np.pi * np.arange(1, length + 1) / (2 * span)) ** 2


def tile_bases(length):
    return [sine_basis(length, *gaps) for gaps in ((1.0, 0.5), (0.5, 0.5), (0.5, 1.0))]


def parts_of(table):
    table = np.asarray(table, np.float64)
    high = table.astype(np.float32).astype(ml_dtypes.bfloat16)
    low = (table - high.astype(np.float64)).astype(np.float32).astype(ml_dtypes.bfloat16)
    return high, low


def split(table):
    return np.stack(parts_of(table), axis=-3)


def left_table(table):
    high, low = parts_of(table)
    return np.concatenate([high, high, low], axis=-1)


def right_table(table):
    high, low = parts_of(table)
    return np.concatenate([high, low, high], axis=-2)


def single(table):
    return np.asarray(table, np.float32)


def pieces(values):
    high = values.astype(jnp.bfloat16)
    return high, (values - high.astype(f32)).astype(jnp.bfloat16)


def mm(left, right):
    return jnp.dot(left, right, preferred_element_type=f32)


def table_times(table_ref, values):
    high, low = pieces(values)
    return mm(table_ref[...], jnp.concatenate([high, low, high], axis=0))


def times_table(values, table_ref):
    high, low = pieces(values)
    return mm(jnp.concatenate([high, high, low], axis=1), table_ref[...])


def mm_transposed(left, right):
    return lax.dot_general(left, right, (((1,), (1,)), ((), ())), preferred_element_type=f32)


def few_rows_times(values, high, low, product=mm):
    rows = values.shape[0]
    both = jnp.concatenate(pieces(values), axis=0)
    first = product(both, high)
    return first[:rows] + (first[rows:] + product(both[:rows], low))


def inverse_of(values):
    found = pl.reciprocal(values, approx=True)
    found = found * (2.0 - values * found)
    return found * (2.0 - values * found)


def dot_full(left, right, dims):
    return lax.dot_general(left, right, (dims, ((), ())), precision=highest, preferred_element_type=f32)


def lane_ids(rows=NZ):
    return lax.broadcasted_iota(jnp.int32, (rows, LANES), 1)


def swap_groups(four, lanes):
    odd = (lanes & 32) != 0
    high = lanes >= 64
    pairs = [jnp.where(odd, four[(d + 1) % 4], four[d]) for d in range(4)]
    picked = [jnp.where(high, pairs[(d + 2) % 4], pairs[d]) for d in range(4)]
    moved = [picked[0]] + [pltpu.roll(picked[d], 32 * d, 1) for d in range(1, 4)]
    pairs = [jnp.where(odd, moved[(1 - t) % 4], moved[-t % 4]) for t in range(4)]
    return [jnp.where(high, pairs[(t - 2) % 4], pairs[t]) for t in range(4)]


def spread(part):
    high, low = pieces(part)
    return jnp.concatenate([high, high, low], axis=0)


def spread_other(part):
    high, low = pieces(part)
    return jnp.concatenate([high, low, high], axis=0)


def params():
    return pltpu.CompilerParams(vmem_limit_bytes=VMEM_LIMIT)


def gather_tile(velocity, fluid, inverse, rows_n, cols_n):
    y_span, x_span = rows_n * B, cols_n * B
    quads = cols_n // 4

    def kernel(inverse_ref, *refs):
        flow_refs = refs[:cols_n]
        fraction_refs = refs[cols_n : 2 * cols_n]
        out_ref, low_ref, high_ref = refs[2 * cols_n :]
        step = pl.program_id(0)
        lanes = lane_ids()
        place = step % 2
        chunk = pl.ds(pl.multiple_of(step // 2 * LANES, LANES), LANES)
        high_mine = ((lanes & 31) // 16) == place
        low_mine = (((lanes + 1) & 31) // 16) == place
        for channel in range(4):
            low_edge = jnp.zeros((NZ, LANES), f32)
            high_edge = jnp.zeros((NZ, LANES), f32)
            for jq in range(8):
                for quad in range(quads):
                    four = []
                    for g in range(4):
                        at = quad * 4 + g
                        part = slice(jq * LANES, (jq + 1) * LANES)
                        if channel < 3:
                            four.append(flow_refs[at][channel, 0, :, part])
                        else:
                            four.append(fraction_refs[at][0, :, part])
                    rows = swap_groups(four, lanes)
                    for t in range(4):
                        out_ref[channel, jq * 4 + t, :, quad * LANES : (quad + 1) * LANES] = rows[t]
                    if channel < 3 and quad == 0:
                        here = ((lanes + 1) & 31) == 2 * jq
                        low_edge = jnp.where(here, pltpu.roll(four[0], (2 * jq + 127) % LANES, 1), low_edge)
                    if channel < 3 and quad == quads - 1:
                        here = (lanes & 31) == 2 * jq
                        high_edge = jnp.where(here, pltpu.roll(four[3], 97 + 2 * jq, 1), high_edge)
            if channel < 3:
                shift = place * 16
                low_ref[channel, :, chunk] = jnp.where(low_mine, pltpu.roll(low_edge, shift, 1), low_ref[channel, :, chunk])
                high_ref[channel, :, chunk] = jnp.where(
                    high_mine, pltpu.roll(high_edge, shift, 1), high_ref[channel, :, chunk])

    def flow_spec(col):
        return pl.BlockSpec((3, 1, NZ, B * B), lambda s, inv: (0, inv[s * cols_n + col], 0, 0))

    def fraction_spec(col):
        return pl.BlockSpec((1, NZ, B * B), lambda s, inv: (inv[s * cols_n + col], 0, 0))

    edge = pl.BlockSpec((3, NZ, 2 * y_span), lambda s, inv: (0, 0, 0))
    return pl.pallas_call(
        kernel,
        grid_spec=pltpu.PrefetchScalarGridSpec(
            num_scalar_prefetch=1,
            grid=(rows_n,),
            in_specs=[flow_spec(c) for c in range(cols_n)] + [fraction_spec(c) for c in range(cols_n)],
            out_specs=[pl.BlockSpec((4, B, NZ, x_span), lambda s, inv: (0, s, 0, 0)), edge, edge],
        ),
        out_shape=[
            jax.ShapeDtypeStruct((4, y_span, NZ, x_span), f32),
            jax.ShapeDtypeStruct((3, NZ, 2 * y_span), f32),
            jax.ShapeDtypeStruct((3, NZ, 2 * y_span), f32),
        ],
        compiler_params=params(),
    )(inverse, *([velocity] * cols_n), *([fluid] * cols_n))


def advance(tile, x_below, x_above, y_below, y_above, cosine, sine_x, shift, kinds):
    _, y_span, _, x_span = tile.shape
    steps = y_span // B
    chunks = x_span // LANES

    def kernel(kinds_ref, main_ref, prev_ref, next_ref, xb_ref, xa_ref, yb_ref, ya_ref, cosine_ref, sine_ref, shift_ref,
               star_ref, modes_ref, gx_ref, gy_ref, rows_ref, source_ref, carry_ref, even_ref, odd_ref):
        step = pl.program_id(0)
        lanes = lane_ids()
        layers = lax.broadcasted_iota(jnp.int32, (NZ, LANES), 0)
        first_layer, last_layer = layers == 0, layers == NZ - 1
        first_lane, last_lane = lanes == 0, lanes == LANES - 1

        rows_ref[:, 1 : B + 1] = main_ref[:3]

        @pl.when(step == 0)
        def _():
            rows_ref[:, 0] = yb_ref[...]
            carry_ref[...] = jnp.zeros_like(carry_ref)

        @pl.when(step > 0)
        def _():
            rows_ref[:, 0] = prev_ref[:3, 0]

        @pl.when(step == steps - 1)
        def _():
            rows_ref[:, B + 1] = ya_ref[...]

        @pl.when(step < steps - 1)
        def _():
            rows_ref[:, B + 1] = next_ref[:3, 0]

        y_chunk = pl.ds(pl.multiple_of(step // 4 * LANES, LANES), LANES)
        halo_chunk = pl.ds(pl.multiple_of(step // 2 * LANES, LANES), LANES)
        even_lane = (lanes & 1) == 0

        def row(group, r, moved_ref):
            j = group * 8 + r
            held = r % 4 * 32 + (step % 2) * 16 + 2 * (group * 2 + r // 4)
            at = (step % 4) * B + j
            star = {}
            flow = {}
            for h in range(chunks):
                for c in range(3):
                    flow[c, h] = rows_ref[c, j + 1, :, h * LANES : (h + 1) * LANES]
            edge = {}
            for c in range(3):
                both = jnp.where(even_lane, xb_ref[c, :, halo_chunk], xa_ref[c, :, halo_chunk])
                edge[c] = pltpu.roll(both, (LANES - held) % LANES, 1)
            for h in range(chunks):
                part = slice(h * LANES, (h + 1) * LANES)
                take_up, take_down = [], []
                for e in range(3):
                    scaled = 0.125 * flow[e, h]
                    take_up.append(0.025 - scaled)
                    take_down.append(0.025 + scaled)
                fraction = main_ref[3, j, :, part]
                for c in range(3):
                    center = flow[c, h]
                    x_low = moved_ref[c, r, :, part]
                    x_up = moved_ref[c, r, :, x_span + h * LANES : x_span + (h + 1) * LANES]
                    if h == 0:
                        x_low = jnp.where(first_lane, edge[c], x_low)
                    if h == chunks - 1:
                        x_up = jnp.where(last_lane, edge[c], x_up)
                    y_low = rows_ref[c, j, :, part]
                    y_up = rows_ref[c, j + 2, :, part]
                    z_low = jnp.where(first_layer, 0.0, pltpu.roll(center, 1, 0))
                    z_up = jnp.where(last_layer, 0.0, pltpu.roll(center, NZ - 1, 0))
                    total = (
                        0.85 * center
                        + (take_up[0] * x_up + take_down[0] * x_low)
                        + (take_up[1] * y_up + take_down[1] * y_low)
                        + (take_up[2] * z_up + take_down[2] * z_low)
                    )
                    value = fraction * total
                    if c == 2:
                        value = jnp.where(last_layer, 0.0, value)
                    star[c, h] = value
                    star_ref[c, j, :, part] = value
            before = 0.0
            for h in range(chunks):
                part = slice(h * LANES, (h + 1) * LANES)
                moved = pltpu.roll(star[0, h], 1, 1)
                x_low = jnp.where(first_lane, before, moved)
                before = moved
                z_low = jnp.where(first_layer, 0.0, pltpu.roll(star[2, h], 1, 0))
                y_low = carry_ref[:, part]
                source_ref[j, :, part] = (x_low - star[0, h]) + (y_low - star[1, h]) + (z_low - star[2, h])
                carry_ref[:, part] = star[1, h]
            edge = pltpu.roll(star[0, chunks - 1], (at + 1) % LANES, 1)
            gx_ref[:, y_chunk] = jnp.where(lanes == at, edge, gx_ref[:, y_chunk])

        def transform(group):
            rows = pl.ds(pl.multiple_of(group * 8, 8), 8)
            part = source_ref[rows].reshape(8 * NZ, x_span)
            modes = times_table(table_times(cosine_ref, part), sine_ref)
            modes_ref[:, rows, :] = modes.reshape(NZ, 8, x_span)

        def shift(group, moved_ref):
            for c in range(3):
                center = rows_ref[c, pl.ds(group * 8 + 1, 8)].reshape(8 * NZ, x_span)
                moved = mm(jnp.concatenate(pieces(center), axis=1), shift_ref[...])
                moved_ref[c] = moved.reshape(8, NZ, 2 * x_span)

        shift(0, even_ref)

        def two_groups(pair, _):
            group = 2 * pair
            transform(jnp.maximum(group - 1, 0))
            shift(group + 1, odd_ref)
            for r in range(8):
                row(group, r, even_ref)
            transform(group)
            shift(jnp.minimum(group + 2, B // 8 - 1), even_ref)
            for r in range(8):
                row(group + 1, r, odd_ref)
            return _

        lax.fori_loop(0, B // 16, two_groups, 0)
        transform(B // 8 - 1)
        gy_ref[...] = carry_ref[...]

    full3 = pl.BlockSpec((3, NZ, 2 * y_span), lambda s, kinds: (0, 0, 0))
    return pl.pallas_call(
        kernel,
        grid_spec=pltpu.PrefetchScalarGridSpec(
            num_scalar_prefetch=1,
            grid=(steps,),
            in_specs=[
                pl.BlockSpec((4, B, NZ, x_span), lambda s, kinds: (0, s, 0, 0)),
                pl.BlockSpec((4, 1, NZ, x_span), lambda s, kinds: (0, jnp.maximum(s * B - 1, 0), 0, 0)),
                pl.BlockSpec((4, 1, NZ, x_span), lambda s, kinds: (0, jnp.minimum(s * B + B, y_span - 1), 0, 0)),
                full3,
                full3,
                pl.BlockSpec((3, NZ, x_span), lambda s, kinds: (0, 0, 0)),
                pl.BlockSpec((3, NZ, x_span), lambda s, kinds: (0, 0, 0)),
                pl.BlockSpec((8 * NZ, 24 * NZ), lambda s, kinds: (0, 0)),
                pl.BlockSpec((None, 3 * x_span, x_span), lambda s, kinds: (kinds[1], 0, 0)),
                pl.BlockSpec((2 * x_span, 2 * x_span), lambda s, kinds: (0, 0)),
            ],
            out_specs=[
                pl.BlockSpec((3, B, NZ, x_span), lambda s, kinds: (0, s, 0, 0)),
                pl.BlockSpec((NZ, B, x_span), lambda s, kinds: (0, s, 0)),
                pl.BlockSpec((NZ, y_span), lambda s, kinds: (0, 0)),
                pl.BlockSpec((NZ, x_span), lambda s, kinds: (0, 0)),
            ],
            scratch_shapes=[
                pltpu.VMEM((3, B + 2, NZ, x_span), f32),
                pltpu.VMEM((B, NZ, x_span), f32),
                pltpu.VMEM((NZ, x_span), f32),
                pltpu.VMEM((3, 8, NZ, 2 * x_span), f32),
                pltpu.VMEM((3, 8, NZ, 2 * x_span), f32),
            ],
        ),
        out_shape=[
            jax.ShapeDtypeStruct((3, y_span, NZ, x_span), f32),
            jax.ShapeDtypeStruct((NZ, y_span, x_span), f32),
            jax.ShapeDtypeStruct((NZ, y_span), f32),
            jax.ShapeDtypeStruct((NZ, x_span), f32),
        ],
        compiler_params=params(),
    )(kinds, tile, tile, tile, x_below, x_above, y_below, y_above, cosine, sine_x, shift)


def first_solve(modes, sine_yt, sine_ytr, sine_xt, edge_y, edge_x, eigen, levels, flux_x, flux_y, cosine, kinds):
    layers, y_span, x_span = modes.shape
    batch = 4
    steps = layers // batch
    sides = 2 * layers

    def kernel(kinds_ref, modes_ref, yt_ref, ytr_ref, xt_ref, edge_y_ref, edge_x_ref, eigen_ref, levels_ref,
               flux_x_ref, flux_y_ref, cosine_ref, spectrum_ref, bundle_ref, rows_ref, columns_ref):
        step = pl.program_id(0)
        for i in range(batch):
            k = step * batch + i
            spectrum = table_times(yt_ref, modes_ref[i])
            spectrum_ref[i] = spectrum
            high, low = pieces(spectrum * inverse_of(eigen_ref[...] + levels_ref[k]))
            found = mm(edge_y_ref[...], high) + mm(edge_y_ref[...], low)
            found = found[:8] + found[8:]
            rows_ref[pl.ds(k, 1)] = found[0:1]
            rows_ref[pl.ds(layers + k, 1)] = found[1:2]
            found = mm_transposed(edge_x_ref[...], high) + mm_transposed(edge_x_ref[...], low)
            found = found[:8] + found[8:]
            columns_ref[pl.ds(k, 1)] = found[0:1]
            columns_ref[pl.ds(layers + k, 1)] = found[1:2]

        @pl.when(step == steps - 1)
        def _():
            along_x = times_table(rows_ref[...], xt_ref)
            along_y = times_table(columns_ref[...], ytr_ref)
            cosine_table = cosine_ref[...]
            for line, values, flux_ref in ((0, along_x, flux_y_ref), (x_span, along_y, flux_x_ref)):
                part = slice(line, line + values.shape[1])
                bundle_ref[0, :, part] = values[:layers]
                bundle_ref[1, :, part] = values[layers:]
                bundle_ref[2, :, part] = dot_full(cosine_table, flux_ref[...], ((1,), (0,)))

    return pl.pallas_call(
        kernel,
        grid_spec=pltpu.PrefetchScalarGridSpec(
            num_scalar_prefetch=1,
            grid=(steps,),
            in_specs=[
                pl.BlockSpec((batch, y_span, x_span), lambda k, kinds: (k, 0, 0)),
                pl.BlockSpec((None, y_span, 3 * y_span), lambda k, kinds: (kinds[0], 0, 0)),
                pl.BlockSpec((None, 3 * y_span, y_span), lambda k, kinds: (kinds[0], 0, 0)),
                pl.BlockSpec((None, 3 * x_span, x_span), lambda k, kinds: (kinds[1], 0, 0)),
                pl.BlockSpec((None, 16, y_span), lambda k, kinds: (kinds[0], 0, 0)),
                pl.BlockSpec((None, 16, x_span), lambda k, kinds: (kinds[1], 0, 0)),
                pl.BlockSpec((None, y_span, x_span), lambda k, kinds: (kinds[0] * 3 + kinds[1], 0, 0)),
                pl.BlockSpec(memory_space=pltpu.SMEM),
                pl.BlockSpec((layers, y_span), lambda k, kinds: (0, 0)),
                pl.BlockSpec((layers, x_span), lambda k, kinds: (0, 0)),
                pl.BlockSpec((layers, layers), lambda k, kinds: (0, 0)),
            ],
            out_specs=[
                pl.BlockSpec((batch, y_span, x_span), lambda k, kinds: (k, 0, 0)),
                pl.BlockSpec((3, layers, x_span + y_span), lambda k, kinds: (0, 0, 0)),
            ],
            scratch_shapes=[pltpu.VMEM((sides, x_span), f32), pltpu.VMEM((sides, y_span), f32)],
        ),
        out_shape=[
            jax.ShapeDtypeStruct((layers, y_span, x_span), f32),
            jax.ShapeDtypeStruct((3, layers, x_span + y_span), f32),
        ],
        compiler_params=params(),
    )(kinds, modes, sine_yt, sine_ytr, sine_xt, edge_y, edge_x, eigen, levels, flux_x, flux_y, cosine)


def second_solve(spectrum, sums, sine_y, sine_yr, sine_x, sine_xt, edge_y, edge_x, eigen, levels, kinds):
    layers, y_span, x_span = spectrum.shape
    batch = 4
    sides = 2 * layers

    def kernel(kinds_ref, spectrum_ref, sums_ref, y_ref, yr_ref, x_ref, xt_ref, edge_y_ref, edge_x_ref,
               eigen_ref, levels_ref, out_ref, left_ref, right_ref):
        step = pl.program_id(0)

        @pl.when(step == 0)
        def _():
            right_ref[:sides] = edge_x_ref[...]
            right_ref[sides:] = times_table(sums_ref[:, :x_span], x_ref)
            left = jnp.concatenate([times_table(sums_ref[:, x_span:], yr_ref), edge_y_ref[...]], axis=0)
            left_high, left_low = pieces(left.T)
            left_ref[...] = jnp.concatenate([left_high, left_high, left_low], axis=1)

        row_ids = lax.broadcasted_iota(jnp.int32, (2 * sides, x_span), 0) & (layers - 1)
        for i in range(batch):
            k = step * batch + i
            high, low = pieces(jnp.where(row_ids == k, right_ref[...], 0.0))
            added = mm(left_ref[...], jnp.concatenate([high, low, high], axis=0))
            solved = (spectrum_ref[i] + added) * inverse_of(eigen_ref[...] + levels_ref[k])
            out_ref[i] = times_table(table_times(y_ref, solved), xt_ref)

    return pl.pallas_call(
        kernel,
        grid_spec=pltpu.PrefetchScalarGridSpec(
            num_scalar_prefetch=1,
            grid=(layers // batch,),
            in_specs=[
                pl.BlockSpec((batch, y_span, x_span), lambda k, kinds: (k, 0, 0)),
                pl.BlockSpec((sides, x_span + y_span), lambda k, kinds: (0, 0)),
                pl.BlockSpec((None, y_span, 3 * y_span), lambda k, kinds: (kinds[0], 0, 0)),
                pl.BlockSpec((None, 3 * y_span, y_span), lambda k, kinds: (kinds[0], 0, 0)),
                pl.BlockSpec((None, 3 * x_span, x_span), lambda k, kinds: (kinds[1], 0, 0)),
                pl.BlockSpec((None, 3 * x_span, x_span), lambda k, kinds: (kinds[1], 0, 0)),
                pl.BlockSpec((None, sides, y_span), lambda k, kinds: (kinds[0], 0, 0)),
                pl.BlockSpec((None, sides, x_span), lambda k, kinds: (kinds[1], 0, 0)),
                pl.BlockSpec((None, y_span, x_span), lambda k, kinds: (kinds[0] * 3 + kinds[1], 0, 0)),
                pl.BlockSpec(memory_space=pltpu.SMEM),
            ],
            out_specs=pl.BlockSpec((batch, y_span, x_span), lambda k, kinds: (k, 0, 0)),
            scratch_shapes=[
                pltpu.VMEM((y_span, 6 * sides), jnp.bfloat16),
                pltpu.VMEM((2 * sides, x_span), f32),
            ],
        ),
        out_shape=jax.ShapeDtypeStruct((layers, y_span, x_span), f32),
        compiler_params=params(),
    )(kinds, spectrum, sums, sine_y, sine_yr, sine_x, sine_xt, edge_y, edge_x, eigen, levels)


def finish(modes, star, sums, cosine_inverse, cosine_t, inverse, kinds, slots):
    layers, y_span, x_span = modes.shape
    rows_n, cols_n = y_span // B, x_span // B
    chunks = x_span // LANES

    def kernel(inverse_ref, kinds_ref, modes_ref, after_ref, star_ref, sums_ref, inverse_cosine_ref, cosine_ref,
               flow_out, pressure_out, rows_ref, blocks_ref, beyond_ref, flow_sem, pressure_sem):
        step = pl.program_id(0)
        half = step % 2

        def copies(at_step, at_half):
            found = []
            for col in range(cols_n):
                slot = inverse_ref[at_step * cols_n + col]
                found.append(pltpu.make_async_copy(
                    blocks_ref.at[at_half, col, pl.ds(0, 3)], flow_out.at[:, slot], flow_sem.at[at_half, col]))
                found.append(pltpu.make_async_copy(
                    blocks_ref.at[at_half, col, 3], pressure_out.at[slot], pressure_sem.at[at_half, col]))
            return found

        @pl.when(step >= 2)
        def _():
            for copy in copies(step - 2, half):
                copy.wait()

        @pl.when(step == 0)
        def _():
            beyond_ref[...] = dot_full(inverse_cosine_ref[...], sums_ref[layers:], ((1,), (0,)))

        lanes = lane_ids()
        layers_at = lax.broadcasted_iota(jnp.int32, (NZ, LANES), 0)
        last_layer = layers_at == NZ - 1
        last_lane = lanes == LANES - 1
        for q in range(B // 8):
            part = modes_ref[:, 8 * q : 8 * q + 8, :].reshape(8 * NZ, x_span)
            rows_ref[8 * q : 8 * q + 8] = table_times(cosine_ref, part).reshape(8, NZ, x_span)

        @pl.when(step < rows_n - 1)
        def _():
            part = after_ref[...].reshape(8 * NZ, x_span)
            rows_ref[B] = table_times(cosine_ref, part).reshape(8, NZ, x_span)[0]

        @pl.when(step == rows_n - 1)
        def _():
            rows_ref[B] = jnp.where(kinds_ref[0] == 2, 0.0, beyond_ref[:, :x_span] - rows_ref[B - 1])

        def four_rows(jq, _):
            y = step * B + jq * 4
            y_chunk = pl.ds(pl.multiple_of(x_span + y // LANES * LANES, LANES), LANES)
            block = pl.ds(pl.multiple_of(jq * LANES, LANES), LANES)
            to_left = [
                [pltpu.roll(rows_ref[jq * 4 + t, :, h * LANES : (h + 1) * LANES], LANES - 1, 1) for t in range(4)]
                for h in range(chunks)
            ]
            for h in range(chunks):
                part = slice(h * LANES, (h + 1) * LANES)
                found = [[], [], [], []]
                for t in range(4):
                    j = jq * 4 + t
                    here = rows_ref[j, :, part]
                    if h == chunks - 1:
                        after = pltpu.roll(beyond_ref[:, y_chunk], LANES - 1 - (y + t) % LANES, 1)
                        after = jnp.where(kinds_ref[1] == 2, 0.0, after - here)
                    else:
                        after = to_left[h + 1][t]
                    x_up = jnp.where(last_lane, after, to_left[h][t])
                    y_up = rows_ref[j + 1, :, part]
                    z_up = jnp.where(last_layer, here, pltpu.roll(here, NZ - 1, 0))
                    found[0].append(star_ref[0, j, :, part] - (x_up - here))
                    found[1].append(star_ref[1, j, :, part] - (y_up - here))
                    found[2].append(star_ref[2, j, :, part] - (z_up - here))
                    found[3].append(here)
                for channel in range(4):
                    swapped = swap_groups(found[channel], lanes)
                    for g in range(4):
                        blocks_ref[half, 4 * h + g, channel, :, block] = swapped[g]
            return _

        lax.fori_loop(0, B // 4, four_rows, 0)

        for copy in copies(step, half):
            copy.start()

        @pl.when(step == rows_n - 1)
        def _():
            for copy in copies(step - 1, 1 - half) + copies(step, half):
                copy.wait()

    return pl.pallas_call(
        kernel,
        grid_spec=pltpu.PrefetchScalarGridSpec(
            num_scalar_prefetch=2,
            grid=(rows_n,),
            in_specs=[
                pl.BlockSpec((layers, B, x_span), lambda s, inv, kinds: (0, s, 0)),
                pl.BlockSpec((layers, 8, x_span), lambda s, inv, kinds: (0, jnp.minimum((s + 1) * (B // 8), y_span // 8 - 1), 0)),
                pl.BlockSpec((3, B, NZ, x_span), lambda s, inv, kinds: (0, s, 0, 0)),
                pl.BlockSpec((2 * layers, x_span + y_span), lambda s, inv, kinds: (0, 0)),
                pl.BlockSpec((layers, layers), lambda s, inv, kinds: (0, 0)),
                pl.BlockSpec((8 * NZ, 24 * NZ), lambda s, inv, kinds: (0, 0)),
            ],
            out_specs=[pl.BlockSpec(memory_space=pl.ANY), pl.BlockSpec(memory_space=pl.ANY)],
            scratch_shapes=[
                pltpu.VMEM((B + 1, NZ, x_span), f32),
                pltpu.VMEM((2, cols_n, 4, NZ, B * B), f32),
                pltpu.VMEM((NZ, x_span + y_span), f32),
                pltpu.SemaphoreType.DMA((2, cols_n)),
                pltpu.SemaphoreType.DMA((2, cols_n)),
            ],
        ),
        out_shape=[
            jax.ShapeDtypeStruct((3, slots, NZ, B * B), f32),
            jax.ShapeDtypeStruct((slots, NZ, B * B), f32),
        ],
        compiler_params=params(),
    )(inverse, kinds, modes, modes, star, sums, cosine_inverse, cosine_t)


def solve_interfaces(lines_x, lines_y, picks_x, picks_y, table_x, table_y, eig_x, eig_y, levels, kinds):
    rows_x, rows_y = lines_x.shape[0], lines_y.shape[1]
    half_x = lines_y.shape[2]
    width = min(256, half_x)

    def kernel(kinds_ref, lines_x_ref, lines_y_ref, picks_x_ref, picks_y_ref, table_x_ref, table_y_ref, eig_x_ref,
               eig_y_ref, levels_ref, sum_x_ref, fold_ref, hat_ref, out_hat_ref):
        level = levels_ref[kinds_ref[2]]
        hat_x = few_rows_times(lines_x_ref[...], table_y_ref[0], table_y_ref[1])
        for parity in range(2):
            hat_ref[:, parity * half_x : (parity + 1) * half_x] = few_rows_times(
                lines_y_ref[parity], table_x_ref[parity, 0], table_x_ref[parity, 1])
        right = spread(jnp.concatenate([hat_x, picks_y_ref[0]], axis=0))
        along = jnp.zeros((rows_x, NY), f32)
        for start in range(0, 2 * half_x, width):
            part = slice(start, start + width)
            left = spread_other(jnp.concatenate([picks_x_ref[0, :, part], hat_ref[:, part]], axis=0))
            field = lax.dot_general(left, right, (((0,), (0,)), ((), ())), preferred_element_type=f32)
            field = field * inverse_of(eig_x_ref[part, :1] + eig_y_ref[:1] + level)
            high, low = pieces(field)
            along += few_rows_times(picks_x_ref[1, :, part], high, low)
            out_hat_ref[:, part] = hat_ref[:, part] + few_rows_times(picks_y_ref[1], high, low, mm_transposed)
        sum_x_ref[...] = few_rows_times(hat_x + along, table_y_ref[0], table_y_ref[1])
        for parity in range(2):
            fold_ref[parity] = few_rows_times(
                out_hat_ref[:, parity * half_x : (parity + 1) * half_x],
                table_x_ref[parity, 0], table_x_ref[parity, 1], mm_transposed)

    vmem = pl.BlockSpec(memory_space=pltpu.VMEM)
    return pl.pallas_call(
        kernel,
        grid_spec=pltpu.PrefetchScalarGridSpec(
            num_scalar_prefetch=1,
            grid=(),
            in_specs=[vmem] * 8 + [pl.BlockSpec(memory_space=pltpu.SMEM)],
            out_specs=[vmem, vmem],
            scratch_shapes=[pltpu.VMEM((rows_y, NX), f32), pltpu.VMEM((rows_y, NX), f32)],
        ),
        out_shape=[
            jax.ShapeDtypeStruct((rows_x, NY), f32),
            jax.ShapeDtypeStruct((2, rows_y, half_x), f32),
        ],
        compiler_params=params(),
    )(kinds, lines_x, lines_y, picks_x, picks_y, table_x, table_y, eig_x, eig_y, levels)


def padded_rows(count):
    return -(-2 * count // 16) * 16


def shards(tables, velocity, fluid, block_place):
    pa_size = lax.axis_size("pa")
    pb_size = lax.axis_size("pb")
    group_count = pa_size * pb_size
    y_span, x_span = NY // pa_size, NX // pb_size
    rows_n, cols_n = y_span // B, x_span // B
    slots = block_place.shape[0]
    pa, pb = lax.axis_index("pa"), lax.axis_index("pb")

    def kind(index, size):
        return jnp.where(index == 0, 0, jnp.where(index == size - 1, 2, 1)).astype(jnp.int32)

    repeats = group_count // NZ
    kinds = jnp.stack([kind(pa, pa_size), kind(pb, pb_size), (pa * pb_size + pb) // repeats])
    slot_ids = jnp.arange(slots, dtype=jnp.int32)
    matches = block_place[None, :] == slot_ids[:, None]
    inverse = jnp.sum(jnp.where(matches, slot_ids[None, :], 0), axis=1).astype(jnp.int32)

    tile, low_edge, high_edge = gather_tile(velocity, fluid, inverse, rows_n, cols_n)

    def up(values, axis, size):
        return lax.ppermute(values, axis, [(i, i + 1) for i in range(size - 1)])

    def down(values, axis, size):
        return lax.ppermute(values, axis, [(i + 1, i) for i in range(size - 1)])

    x_below, x_above = up(high_edge, "pb", pb_size), down(low_edge, "pb", pb_size)
    y_below, y_above = up(tile[:3, -1], "pa", pa_size), down(tile[:3, 0], "pa", pa_size)

    cosine = jnp.asarray(tables["cosine"])
    local = {name: jnp.asarray(tables[name]) for name in (
        "y", "yr", "yt", "ytr", "x", "xt", "edge_y", "edge_x", "few_y", "few_x", "eigen", "levels", "picks_x", "picks_y", "fold_x", "line_y",
        "eig_x", "eig_y")}
    star, modes, flux_x, flux_y = advance(
        tile, x_below, x_above, y_below, y_above, jnp.asarray(tables["cosine8"]), local["x"],
        jnp.asarray(tables["shift"]), kinds
    )
    spectrum, bundle = first_solve(
        modes, local["yt"], local["ytr"], local["xt"], local["few_y"], local["few_x"], local["eigen"],
        local["levels"], flux_x, flux_y, cosine, kinds
    )
    width = x_span + y_span
    bundle = jnp.repeat(bundle, repeats, axis=1) if repeats > 1 else bundle
    arrived = lax.all_to_all(bundle, ("pa", "pb"), split_axis=1, concat_axis=1, tiled=True)
    arrived = arrived.reshape(3, pa_size, pb_size, width)
    on_y, on_x = arrived[..., :x_span], arrived[..., x_span:]
    count_y, count_x = pa_size - 1, pb_size - 1
    rows_y, rows_x = padded_rows(count_y), padded_rows(count_x)
    sums_y = on_y[1, :-1] + on_y[0, 1:]
    lines_y = jnp.concatenate([sums_y, on_y[2, :-1]]).reshape(2 * count_y, NX)
    lines_y = jnp.pad(lines_y, ((0, rows_y - 2 * count_y), (0, 0)))
    sums_x = on_x[1, :, :-1] + on_x[0, :, 1:]
    lines_x = jnp.stack([sums_x, on_x[2, :, :-1]]).transpose(0, 2, 1, 3).reshape(2 * count_x, NY)
    lines_x = jnp.pad(lines_x, ((0, rows_x - 2 * count_x), (0, 0)))
    lower, upper = lines_y[:, : NX // 2], lines_y[:, NX // 2 :][:, ::-1]
    sum_x, folded = solve_interfaces(
        lines_x, jnp.stack([lower + upper, lower - upper]), local["picks_x"], local["picks_y"], local["fold_x"],
        local["line_y"], local["eig_x"], local["eig_y"], local["levels"], kinds
    )
    sum_x = sum_x[:count_x]
    even, odd = folded[0, :count_y], folded[1, :count_y]
    sum_y = jnp.concatenate([even + odd, (even - odd)[:, ::-1]], axis=1)
    flux_y, flux_x = lines_y[count_y : 2 * count_y], lines_x[count_x : 2 * count_x]
    none_y, none_x = jnp.zeros((1, NX), f32), jnp.zeros((1, NY), f32)
    high_y = jnp.concatenate([sum_y, none_y]).reshape(pa_size, pb_size, x_span)
    low_y = jnp.concatenate([none_y, sum_y + flux_y]).reshape(pa_size, pb_size, x_span)
    high_x = jnp.concatenate([sum_x, none_x]).reshape(pb_size, pa_size, y_span).transpose(1, 0, 2)
    low_x = jnp.concatenate([none_x, sum_x + flux_x]).reshape(pb_size, pa_size, y_span).transpose(1, 0, 2)
    reply = jnp.stack([jnp.concatenate([low_y, low_x], axis=2), jnp.concatenate([high_y, high_x], axis=2)])
    reply = reply.reshape(2, group_count, width)
    home = lax.all_to_all(reply, ("pa", "pb"), split_axis=1, concat_axis=1, tiled=True)
    sums = home[:, ::repeats].reshape(2 * NZ, width)
    pressure_modes = second_solve(
        spectrum, sums, local["y"], local["yr"], local["x"], local["xt"], local["edge_y"], local["edge_x"],
        local["eigen"], local["levels"], kinds
    )
    return tuple(
        finish(pressure_modes, star, sums, jnp.asarray(tables["cosine_t"]), jnp.asarray(tables["cosine8t"]), inverse,
               kinds, slots)
    )


def make_tables(pa_size, pb_size):
    y_span, x_span = NY // pa_size, NX // pb_size
    cosine, levels = cosine_basis()
    cosine8 = np.einsum("kz,ab->kabz", cosine, np.eye(8)).reshape(8 * NZ, 8 * NZ)
    tables = {
        "cosine": single(cosine),
        "levels": single(levels),
        "cosine_t": single(cosine.T),
        "cosine8": left_table(cosine8),
        "cosine8t": left_table(cosine8.T),
    }
    below = np.eye(x_span, k=1)
    shift = np.concatenate([below, below.T], axis=1)
    tables["shift"] = np.concatenate([shift, shift], axis=0).astype(ml_dtypes.bfloat16)
    values = {}
    for name, length in (("y", y_span), ("x", x_span)):
        bases = tile_bases(length)
        if name == "x":
            tables["x"] = np.stack([right_table(b) for b, _ in bases])
            tables["xt"] = np.stack([right_table(b.T) for b, _ in bases])
        else:
            tables["y"] = np.stack([left_table(b) for b, _ in bases])
            tables["yr"] = np.stack([right_table(b) for b, _ in bases])
            tables["yt"] = np.stack([left_table(b.T) for b, _ in bases])
            tables["ytr"] = np.stack([right_table(b.T) for b, _ in bases])
        edges = np.stack([np.repeat(b[[0, -1]], NZ, axis=0) for b, _ in bases])
        tables["edge_" + name] = single(edges)
        few = np.zeros((3, 16, length), ml_dtypes.bfloat16)
        for i, (b, _) in enumerate(bases):
            few[i, 0:2], few[i, 8:10] = parts_of(b[[0, -1]])
        tables["few_" + name] = few
        values[name] = [v for _, v in bases]
    tables["eigen"] = single(
        np.stack([ey[:, None] + ex[None, :] for ey in values["y"] for ex in values["x"]])
    )
    basis_x, eig_x = sine_basis(NX, 1.0, 1.0)
    basis_y, eig_y = sine_basis(NY, 1.0, 1.0)
    half = NX // 2
    order = np.concatenate([np.arange(0, NX, 2), np.arange(1, NX, 2)])
    tables["fold_x"] = np.stack([split(basis_x[:half, parity::2]) for parity in range(2)])
    tables["line_y"] = split(basis_y)
    tables["eig_x"] = single(np.repeat(eig_x[order][:, None], LANES, axis=1))
    tables["eig_y"] = single(np.repeat(eig_y[None, :], 8, axis=0))
    for name, basis, tile in (("x", basis_x[:, order], x_span), ("y", basis_y, y_span)):
        above, below = basis[tile::tile], basis[tile - 1 : -1 : tile]
        count, length = above.shape
        picks = np.zeros((2, padded_rows(count), length))
        picks[0, : 2 * count] = np.concatenate([above + below, above])
        picks[1, :count] = above + below
        tables["picks_" + name] = single(picks)
    return tables


def solution(mesh):
    tables = make_tables(mesh.shape["pa"], mesh.shape["pb"])
    return jax.shard_map(
        functools.partial(shards, tables),
        mesh=mesh,
        in_specs=(P(None, ("pa", "pb"), None, None), P(("pa", "pb"), None, None), P(("pa", "pb"))),
        out_specs=(P(None, ("pa", "pb"), None, None), P(("pa", "pb"), None, None)),
        check_vma=False,
    )
```

```python
import functools

import jax
import jax.numpy as jnp
import ml_dtypes
import numpy as np
from jax import lax
from jax.experimental import pallas as pl
from jax.experimental.pallas import tpu as pltpu
from jax.sharding import PartitionSpec as P

NX = 2048
NY = 1024
NZ = 32
B = 32
LANES = 128
highest = lax.Precision.HIGHEST
f32 = jnp.float32
VMEM_LIMIT = 56 * 1024 * 1024


def cosine_basis():
    k = np.arange(NZ)[:, None]
    z = np.arange(NZ)[None, :]
    table = np.cos(np.pi * k * (z + 0.5) / NZ)
    table /= np.sqrt((table**2).sum(axis=1, keepdims=True))
    return table, 2.0 - 2.0 * np.cos(np.pi * np.arange(NZ) / NZ)


def sine_basis(length, lower_gap, upper_gap):
    span = length - 1 + lower_gap + upper_gap
    i = np.arange(length)[:, None]
    k = np.arange(1, length + 1)[None, :]
    table = np.sin(np.pi * k * (i + lower_gap) / span)
    table /= np.sqrt((table**2).sum(axis=0, keepdims=True))
    return table, 4.0 * np.sin(np.pi * np.arange(1, length + 1) / (2 * span)) ** 2


def tile_bases(length):
    return [sine_basis(length, *gaps) for gaps in ((1.0, 0.5), (0.5, 0.5), (0.5, 1.0))]


def parts_of(table):
    table = np.asarray(table, np.float64)
    high = table.astype(np.float32).astype(ml_dtypes.bfloat16)
    low = (table - high.astype(np.float64)).astype(np.float32).astype(ml_dtypes.bfloat16)
    return high, low


def split(table):
    return np.stack(parts_of(table), axis=-3)


def left_table(table):
    return np.concatenate(parts_of(table), axis=-2)


def right_table(table):
    high, low = parts_of(table)
    return np.concatenate([high, low, high], axis=-2)


def single(table):
    return np.asarray(table, np.float32)


def pieces(values):
    high = values.astype(jnp.bfloat16)
    return high, (values - high.astype(f32)).astype(jnp.bfloat16)


def mm(left, right):
    return jnp.dot(left, right, preferred_element_type=f32)


def table_times(table_ref, values):
    high, low = pieces(values)
    rows = table_ref.shape[0] // 2
    found = mm(table_ref[...], high)
    return found[:rows] + (found[rows:] + mm(table_ref[:rows], low))


def times_table(values, table_ref):
    high, low = pieces(values)
    return mm(jnp.concatenate([high, high, low], axis=1), table_ref[...])


def mm_transposed(left, right):
    return lax.dot_general(left, right, (((1,), (1,)), ((), ())), preferred_element_type=f32)


def few_rows_times(values, high, low, product=mm):
    rows = values.shape[0]
    both = jnp.concatenate(pieces(values), axis=0)
    first = product(both, high)
    return first[:rows] + (first[rows:] + product(both[:rows], low))


def inverse_of(values):
    found = pl.reciprocal(values, approx=True)
    found = found * (2.0 - values * found)
    return found * (2.0 - values * found)


def dot_full(left, right, dims):
    return lax.dot_general(left, right, (dims, ((), ())), precision=highest, preferred_element_type=f32)


def lane_ids(rows=NZ):
    return lax.broadcasted_iota(jnp.int32, (rows, LANES), 1)


def swap_groups(four, lanes):
    odd = (lanes & 32) != 0
    high = lanes >= 64
    pairs = [jnp.where(odd, four[(d + 1) % 4], four[d]) for d in range(4)]
    picked = [jnp.where(high, pairs[(d + 2) % 4], pairs[d]) for d in range(4)]
    moved = [picked[0]] + [pltpu.roll(picked[d], 32 * d, 1) for d in range(1, 4)]
    pairs = [jnp.where(odd, moved[(1 - t) % 4], moved[-t % 4]) for t in range(4)]
    return [jnp.where(high, pairs[(t - 2) % 4], pairs[t]) for t in range(4)]


def spread(part):
    high, low = pieces(part)
    return jnp.concatenate([high, high, low], axis=0)


def spread_other(part):
    high, low = pieces(part)
    return jnp.concatenate([high, low, high], axis=0)


def params():
    return pltpu.CompilerParams(vmem_limit_bytes=VMEM_LIMIT)


def gather_tile(velocity, fluid, inverse, rows_n, cols_n):
    y_span, x_span = rows_n * B, cols_n * B
    quads = cols_n // 4

    def kernel(inverse_ref, *refs):
        flow_refs = refs[:cols_n]
        fraction_refs = refs[cols_n : 2 * cols_n]
        out_ref, low_ref, high_ref = refs[2 * cols_n :]
        step = pl.program_id(0)
        lanes = lane_ids()
        place = step % 2
        chunk = pl.ds(pl.multiple_of(step // 2 * LANES, LANES), LANES)
        high_mine = ((lanes & 31) // 16) == place
        low_mine = (((lanes + 1) & 31) // 16) == place
        for channel in range(4):
            low_edge = jnp.zeros((NZ, LANES), f32)
            high_edge = jnp.zeros((NZ, LANES), f32)
            for jq in range(8):
                for quad in range(quads):
                    four = []
                    for g in range(4):
                        at = quad * 4 + g
                        part = slice(jq * LANES, (jq + 1) * LANES)
                        if channel < 3:
                            four.append(flow_refs[at][channel, 0, :, part])
                        else:
                            four.append(fraction_refs[at][0, :, part])
                    rows = swap_groups(four, lanes)
                    for t in range(4):
                        out_ref[channel, jq * 4 + t, :, quad * LANES : (quad + 1) * LANES] = rows[t]
                    if channel < 3 and quad == 0:
                        here = ((lanes + 1) & 31) == 2 * jq
                        low_edge = jnp.where(here, pltpu.roll(four[0], (2 * jq + 127) % LANES, 1), low_edge)
                    if channel < 3 and quad == quads - 1:
                        here = (lanes & 31) == 2 * jq
                        high_edge = jnp.where(here, pltpu.roll(four[3], 97 + 2 * jq, 1), high_edge)
            if channel < 3:
                shift = place * 16
                low_ref[channel, :, chunk] = jnp.where(low_mine, pltpu.roll(low_edge, shift, 1), low_ref[channel, :, chunk])
                high_ref[channel, :, chunk] = jnp.where(
                    high_mine, pltpu.roll(high_edge, shift, 1), high_ref[channel, :, chunk])

    def flow_spec(col):
        return pl.BlockSpec((3, 1, NZ, B * B), lambda s, inv: (0, inv[s * cols_n + col], 0, 0))

    def fraction_spec(col):
        return pl.BlockSpec((1, NZ, B * B), lambda s, inv: (inv[s * cols_n + col], 0, 0))

    edge = pl.BlockSpec((3, NZ, 2 * y_span), lambda s, inv: (0, 0, 0))
    return pl.pallas_call(
        kernel,
        grid_spec=pltpu.PrefetchScalarGridSpec(
            num_scalar_prefetch=1,
            grid=(rows_n,),
            in_specs=[flow_spec(c) for c in range(cols_n)] + [fraction_spec(c) for c in range(cols_n)],
            out_specs=[pl.BlockSpec((4, B, NZ, x_span), lambda s, inv: (0, s, 0, 0)), edge, edge],
        ),
        out_shape=[
            jax.ShapeDtypeStruct((4, y_span, NZ, x_span), f32),
            jax.ShapeDtypeStruct((3, NZ, 2 * y_span), f32),
            jax.ShapeDtypeStruct((3, NZ, 2 * y_span), f32),
        ],
        compiler_params=params(),
    )(inverse, *([velocity] * cols_n), *([fluid] * cols_n))


def advance(tile, x_below, x_above, y_below, y_above, cosine, sine_x, kinds):
    _, y_span, _, x_span = tile.shape
    steps = y_span // B
    chunks = x_span // LANES

    def kernel(kinds_ref, main_ref, prev_ref, next_ref, xb_ref, xa_ref, yb_ref, ya_ref, cosine_ref, sine_ref,
               star_ref, modes_ref, gx_ref, gy_ref, rows_ref, source_ref, carry_ref):
        step = pl.program_id(0)
        lanes = lane_ids()
        layers = lax.broadcasted_iota(jnp.int32, (NZ, LANES), 0)
        first_layer, last_layer = layers == 0, layers == NZ - 1
        first_lane, last_lane = lanes == 0, lanes == LANES - 1

        @pl.when(step == 0)
        def _():
            rows_ref[:, 0] = yb_ref[...]
            carry_ref[...] = jnp.zeros_like(carry_ref)

        @pl.when(step > 0)
        def _():
            rows_ref[:, 0] = prev_ref[:3, 0]

        @pl.when(step == steps - 1)
        def _():
            rows_ref[:, 1] = ya_ref[...]

        @pl.when(step < steps - 1)
        def _():
            rows_ref[:, 1] = next_ref[:3, 0]

        y_chunk = pl.ds(pl.multiple_of(step // 4 * LANES, LANES), LANES)
        halo_chunk = pl.ds(pl.multiple_of(step // 2 * LANES, LANES), LANES)
        even_lane = (lanes & 1) == 0

        def neighbour_row(group, r, c, part):
            if 0 <= r < 8:
                return main_ref[c, group * 8 + r, :, part]
            if r < 0:
                inside = main_ref[c, jnp.maximum(group * 8 - 1, 0), :, part]
                return jnp.where(group == 0, rows_ref[c, 0, :, part], inside)
            inside = main_ref[c, jnp.minimum(group * 8 + 8, B - 1), :, part]
            return jnp.where(group == B // 8 - 1, rows_ref[c, 1, :, part], inside)

        lane_parts = [slice(h * LANES, (h + 1) * LANES) for h in range(chunks)]

        def rows(group):
            carried = [carry_ref[:, part] for part in lane_parts]
            gathered = gx_ref[:, y_chunk]
            for r in range(8):
                j = group * 8 + r
                held = r % 4 * 32 + (step % 2) * 16 + 2 * (group * 2 + r // 4)
                at = (step % 4) * B + j
                speed = [[0.125 * main_ref[e, j, :, part] for part in lane_parts] for e in range(3)]
                source = []
                for c in range(3):
                    both = jnp.where(even_lane, xb_ref[c, :, halo_chunk], xa_ref[c, :, halo_chunk])
                    edge = pltpu.roll(both, (LANES - held) % LANES, 1)
                    centers = [main_ref[c, j, :, part] for part in lane_parts]
                    to_right = [pltpu.roll(center, 1, 1) for center in centers]
                    to_left = [pltpu.roll(center, LANES - 1, 1) for center in centers]
                    star = []
                    for h, part in enumerate(lane_parts):
                        center = centers[h]
                        before = edge if h == 0 else to_right[h - 1]
                        after = edge if h == chunks - 1 else to_left[h + 1]
                        x_low = jnp.where(first_lane, before, to_right[h])
                        x_up = jnp.where(last_lane, after, to_left[h])
                        total = x_up + x_low
                        moved = speed[0][h] * (x_up - x_low)
                        y_low = neighbour_row(group, r - 1, c, part)
                        y_up = neighbour_row(group, r + 1, c, part)
                        total = total + (y_up + y_low)
                        moved = moved + speed[1][h] * (y_up - y_low)
                        z_low = jnp.where(first_layer, 0.0, pltpu.roll(center, 1, 0))
                        z_up = jnp.where(last_layer, 0.0, pltpu.roll(center, NZ - 1, 0))
                        total = total + (z_up + z_low)
                        moved = moved + speed[2][h] * (z_up - z_low)
                        value = main_ref[3, j, :, part] * ((0.85 * center + 0.025 * total) - moved)
                        if c == 2:
                            value = jnp.where(last_layer, 0.0, value)
                        star_ref[c, j, :, part] = value
                        star.append(value)
                    if c == 0:
                        moved = [pltpu.roll(value, 1, 1) for value in star]
                        for h in range(chunks):
                            before = 0.0 if h == 0 else moved[h - 1]
                            source.append(jnp.where(first_lane, before, moved[h]) - star[h])
                        edge = pltpu.roll(star[-1], (at + 1) % LANES, 1)
                        gathered = jnp.where(lanes == at, edge, gathered)
                    elif c == 1:
                        source = [source[h] + (carried[h] - star[h]) for h in range(chunks)]
                        carried = star
                    else:
                        for h, part in enumerate(lane_parts):
                            z_low = jnp.where(first_layer, 0.0, pltpu.roll(star[h], 1, 0))
                            source_ref[j, :, part] = source[h] + (z_low - star[h])
            for h, part in enumerate(lane_parts):
                carry_ref[:, part] = carried[h]
            gx_ref[:, y_chunk] = gathered

        def transform(group):
            rows_at = pl.ds(pl.multiple_of(group * 8, 8), 8)
            part = source_ref[rows_at].reshape(8 * NZ, x_span)
            modes = times_table(table_times(cosine_ref, part), sine_ref)
            modes_ref[:, rows_at, :] = modes.reshape(NZ, 8, x_span)

        rows(0)

        def group_of_rows(group, _):
            transform(group - 1)
            rows(group)
            return _

        lax.fori_loop(1, B // 8, group_of_rows, 0)
        transform(B // 8 - 1)
        gy_ref[...] = carry_ref[...]

    full3 = pl.BlockSpec((3, NZ, 2 * y_span), lambda s, kinds: (0, 0, 0))
    return pl.pallas_call(
        kernel,
        grid_spec=pltpu.PrefetchScalarGridSpec(
            num_scalar_prefetch=1,
            grid=(steps,),
            in_specs=[
                pl.BlockSpec((4, B, NZ, x_span), lambda s, kinds: (0, s, 0, 0)),
                pl.BlockSpec((4, 1, NZ, x_span), lambda s, kinds: (0, jnp.maximum(s * B - 1, 0), 0, 0)),
                pl.BlockSpec((4, 1, NZ, x_span), lambda s, kinds: (0, jnp.minimum(s * B + B, y_span - 1), 0, 0)),
                full3,
                full3,
                pl.BlockSpec((3, NZ, x_span), lambda s, kinds: (0, 0, 0)),
                pl.BlockSpec((3, NZ, x_span), lambda s, kinds: (0, 0, 0)),
                pl.BlockSpec((16 * NZ, 8 * NZ), lambda s, kinds: (0, 0)),
                pl.BlockSpec((None, 3 * x_span, x_span), lambda s, kinds: (kinds[1], 0, 0)),
            ],
            out_specs=[
                pl.BlockSpec((3, B, NZ, x_span), lambda s, kinds: (0, s, 0, 0)),
                pl.BlockSpec((NZ, B, x_span), lambda s, kinds: (0, s, 0)),
                pl.BlockSpec((NZ, y_span), lambda s, kinds: (0, 0)),
                pl.BlockSpec((NZ, x_span), lambda s, kinds: (0, 0)),
            ],
            scratch_shapes=[
                pltpu.VMEM((3, 2, NZ, x_span), f32),
                pltpu.VMEM((B, NZ, x_span), f32),
                pltpu.VMEM((NZ, x_span), f32),
            ],
        ),
        out_shape=[
            jax.ShapeDtypeStruct((3, y_span, NZ, x_span), f32),
            jax.ShapeDtypeStruct((NZ, y_span, x_span), f32),
            jax.ShapeDtypeStruct((NZ, y_span), f32),
            jax.ShapeDtypeStruct((NZ, x_span), f32),
        ],
        compiler_params=params(),
    )(kinds, tile, tile, tile, x_below, x_above, y_below, y_above, cosine, sine_x)


def first_solve(modes, sine_yt, sine_ytr, sine_xt, edge_y, edge_x, eigen, levels, flux_x, flux_y, cosine, kinds):
    layers, y_span, x_span = modes.shape
    batch = 4
    steps = layers // batch
    sides = 2 * layers

    def kernel(kinds_ref, modes_ref, yt_ref, ytr_ref, xt_ref, edge_y_ref, edge_x_ref, eigen_ref, levels_ref,
               flux_x_ref, flux_y_ref, cosine_ref, spectrum_ref, bundle_ref, rows_ref, columns_ref):
        step = pl.program_id(0)
        for i in range(batch):
            k = step * batch + i
            spectrum = table_times(yt_ref, modes_ref[i])
            spectrum_ref[i] = spectrum
            solved = spectrum * inverse_of(eigen_ref[...] + levels_ref[k])
            high, low = pieces(solved)
            for side in range(2):
                found = [
                    jnp.sum(solved[:, start : start + LANES] * edge_y_ref[side], axis=0, keepdims=True)
                    for start in range(0, x_span, LANES)
                ]
                rows_ref[pl.ds(side * layers + k, 1)] = jnp.concatenate(found, axis=1)
            found = mm_transposed(edge_x_ref[...], high) + mm_transposed(edge_x_ref[...], low)
            found = found[:8] + found[8:]
            columns_ref[pl.ds(k, 1)] = found[0:1]
            columns_ref[pl.ds(layers + k, 1)] = found[1:2]

        @pl.when(step == steps - 1)
        def _():
            along_x = times_table(rows_ref[...], xt_ref)
            along_y = times_table(columns_ref[...], ytr_ref)
            cosine_table = cosine_ref[...]
            for line, values, flux_ref in ((0, along_x, flux_y_ref), (x_span, along_y, flux_x_ref)):
                part = slice(line, line + values.shape[1])
                bundle_ref[0, :, part] = values[:layers]
                bundle_ref[1, :, part] = values[layers:]
                bundle_ref[2, :, part] = dot_full(cosine_table, flux_ref[...], ((1,), (0,)))

    return pl.pallas_call(
        kernel,
        grid_spec=pltpu.PrefetchScalarGridSpec(
            num_scalar_prefetch=1,
            grid=(steps,),
            in_specs=[
                pl.BlockSpec((batch, y_span, x_span), lambda k, kinds: (k, 0, 0)),
                pl.BlockSpec((None, 2 * y_span, y_span), lambda k, kinds: (kinds[0], 0, 0)),
                pl.BlockSpec((None, 3 * y_span, y_span), lambda k, kinds: (kinds[0], 0, 0)),
                pl.BlockSpec((None, 3 * x_span, x_span), lambda k, kinds: (kinds[1], 0, 0)),
                pl.BlockSpec((None, 2, y_span, LANES), lambda k, kinds: (kinds[0], 0, 0, 0)),
                pl.BlockSpec((None, 16, x_span), lambda k, kinds: (kinds[1], 0, 0)),
                pl.BlockSpec((None, y_span, x_span), lambda k, kinds: (kinds[0] * 3 + kinds[1], 0, 0)),
                pl.BlockSpec(memory_space=pltpu.SMEM),
                pl.BlockSpec((layers, y_span), lambda k, kinds: (0, 0)),
                pl.BlockSpec((layers, x_span), lambda k, kinds: (0, 0)),
                pl.BlockSpec((layers, layers), lambda k, kinds: (0, 0)),
            ],
            out_specs=[
                pl.BlockSpec((batch, y_span, x_span), lambda k, kinds: (k, 0, 0)),
                pl.BlockSpec((3, layers, x_span + y_span), lambda k, kinds: (0, 0, 0)),
            ],
            scratch_shapes=[pltpu.VMEM((sides, x_span), f32), pltpu.VMEM((sides, y_span), f32)],
        ),
        out_shape=[
            jax.ShapeDtypeStruct((layers, y_span, x_span), f32),
            jax.ShapeDtypeStruct((3, layers, x_span + y_span), f32),
        ],
        compiler_params=params(),
    )(kinds, modes, sine_yt, sine_ytr, sine_xt, edge_y, edge_x, eigen, levels, flux_x, flux_y, cosine)


def second_solve(spectrum, sums, sine_y, sine_yr, sine_x, sine_xt, edge_y, edge_x, eigen, levels, kinds):
    layers, y_span, x_span = spectrum.shape
    batch = 8
    sides = 2 * layers

    def kernel(kinds_ref, spectrum_ref, sums_ref, y_ref, yr_ref, x_ref, xt_ref, edge_y_ref, edge_x_ref,
               eigen_ref, levels_ref, out_ref, along_x_ref, along_y_ref):
        step = pl.program_id(0)

        @pl.when(step == 0)
        def _():
            along_x_ref[...] = times_table(sums_ref[:, :x_span], x_ref)
            along_y_ref[...] = times_table(sums_ref[:, x_span:], yr_ref)

        low_side = pl.ds(pl.multiple_of(step * batch, batch), batch)
        high_side = pl.ds(pl.multiple_of(layers + step * batch, batch), batch)
        left = jnp.concatenate([along_y_ref[low_side], along_y_ref[high_side], edge_y_ref[...]], axis=0)
        right = jnp.concatenate([edge_x_ref[...], along_x_ref[low_side], along_x_ref[high_side]], axis=0)
        left_high = left.astype(jnp.bfloat16).astype(f32)
        blank = jnp.zeros((LANES - 12 * batch, y_span), f32)
        left = jnp.concatenate([left_high, left_high, left - left_high, blank], axis=0).T.astype(jnp.bfloat16)
        blank = jnp.zeros((LANES - 12 * batch, x_span), jnp.bfloat16)
        row_ids = lax.broadcasted_iota(jnp.int32, (4 * batch, x_span), 0) & (batch - 1)
        for start in range(0, batch, 4):
            along_y = []
            for i in range(start, start + 4):
                high, low = pieces(jnp.where(row_ids == i, right, 0.0))
                added = mm(left, jnp.concatenate([high, low, high, blank], axis=0))
                solved = (spectrum_ref[i] + added) * inverse_of(eigen_ref[...] + levels_ref[step * batch + i])
                along_y.append(table_times(y_ref, solved))
            found = times_table(jnp.concatenate(along_y, axis=0), xt_ref)
            out_ref[start : start + 4] = found.reshape(4, y_span, x_span)

    return pl.pallas_call(
        kernel,
        grid_spec=pltpu.PrefetchScalarGridSpec(
            num_scalar_prefetch=1,
            grid=(layers // batch,),
            in_specs=[
                pl.BlockSpec((batch, y_span, x_span), lambda k, kinds: (k, 0, 0)),
                pl.BlockSpec((sides, x_span + y_span), lambda k, kinds: (0, 0)),
                pl.BlockSpec((None, 2 * y_span, y_span), lambda k, kinds: (kinds[0], 0, 0)),
                pl.BlockSpec((None, 3 * y_span, y_span), lambda k, kinds: (kinds[0], 0, 0)),
                pl.BlockSpec((None, 3 * x_span, x_span), lambda k, kinds: (kinds[1], 0, 0)),
                pl.BlockSpec((None, 3 * x_span, x_span), lambda k, kinds: (kinds[1], 0, 0)),
                pl.BlockSpec((None, 2 * batch, y_span), lambda k, kinds: (kinds[0], 0, 0)),
                pl.BlockSpec((None, 2 * batch, x_span), lambda k, kinds: (kinds[1], 0, 0)),
                pl.BlockSpec((None, y_span, x_span), lambda k, kinds: (kinds[0] * 3 + kinds[1], 0, 0)),
                pl.BlockSpec(memory_space=pltpu.SMEM),
            ],
            out_specs=pl.BlockSpec((batch, y_span, x_span), lambda k, kinds: (k, 0, 0)),
            scratch_shapes=[
                pltpu.VMEM((sides, x_span), f32),
                pltpu.VMEM((sides, y_span), f32),
            ],
        ),
        out_shape=jax.ShapeDtypeStruct((layers, y_span, x_span), f32),
        compiler_params=params(),
    )(kinds, spectrum, sums, sine_y, sine_yr, sine_x, sine_xt, edge_y, edge_x, eigen, levels)


def finish(modes, star, sums, cosine_inverse, cosine_t, inverse, kinds, slots):
    layers, y_span, x_span = modes.shape
    rows_n, cols_n = y_span // B, x_span // B
    chunks = x_span // LANES

    def kernel(inverse_ref, kinds_ref, modes_ref, after_ref, star_ref, sums_ref, inverse_cosine_ref, cosine_ref,
               flow_out, pressure_out, rows_ref, blocks_ref, beyond_ref, flow_sem, pressure_sem):
        step = pl.program_id(0)
        half = step % 2

        def copies(at_step, at_half):
            found = []
            for col in range(cols_n):
                slot = inverse_ref[at_step * cols_n + col]
                found.append(pltpu.make_async_copy(
                    blocks_ref.at[at_half, col, pl.ds(0, 3)], flow_out.at[:, slot], flow_sem.at[at_half, col]))
                found.append(pltpu.make_async_copy(
                    blocks_ref.at[at_half, col, 3], pressure_out.at[slot], pressure_sem.at[at_half, col]))
            return found

        @pl.when(step >= 2)
        def _():
            for copy in copies(step - 2, half):
                copy.wait()

        @pl.when(step == 0)
        def _():
            beyond_ref[...] = dot_full(inverse_cosine_ref[...], sums_ref[layers:], ((1,), (0,)))

        lanes = lane_ids()
        layers_at = lax.broadcasted_iota(jnp.int32, (NZ, LANES), 0)
        last_layer = layers_at == NZ - 1
        last_lane = lanes == LANES - 1
        def layers_of(part):
            return table_times(cosine_ref, part.reshape(8 * NZ, x_span)).reshape(8, NZ, x_span)

        @pl.when(step == 0)
        def _():
            rows_ref[:8] = layers_of(modes_ref[:, :8, :])

        @pl.when(step > 0)
        def _():
            rows_ref[:8] = rows_ref[B:]

        def four_rows(jq):
            y = step * B + jq * 4
            y_chunk = pl.ds(pl.multiple_of(x_span + step * B // LANES * LANES, LANES), LANES)
            block = slice(jq * LANES, (jq + 1) * LANES)
            to_left = [
                [pltpu.roll(rows_ref[jq * 4 + t, :, h * LANES : (h + 1) * LANES], LANES - 1, 1) for t in range(4)]
                for h in range(chunks)
            ]
            for h in range(chunks):
                part = slice(h * LANES, (h + 1) * LANES)
                found = [[], [], [], []]
                for t in range(4):
                    j = jq * 4 + t
                    here = rows_ref[j, :, part]
                    if h == chunks - 1:
                        after = pltpu.roll(beyond_ref[:, y_chunk], LANES - 1 - (y + t) % LANES, 1)
                        after = jnp.where(kinds_ref[1] == 2, 0.0, after - here)
                    else:
                        after = to_left[h + 1][t]
                    x_up = jnp.where(last_lane, after, to_left[h][t])
                    y_up = rows_ref[j + 1, :, part]
                    z_up = jnp.where(last_layer, here, pltpu.roll(here, NZ - 1, 0))
                    found[0].append(star_ref[0, j, :, part] - (x_up - here))
                    found[1].append(star_ref[1, j, :, part] - (y_up - here))
                    found[2].append(star_ref[2, j, :, part] - (z_up - here))
                    found[3].append(here)
                for channel in range(4):
                    swapped = swap_groups(found[channel], lanes)
                    for g in range(4):
                        blocks_ref[half, 4 * h + g, channel, :, block] = swapped[g]

        groups = B // 8
        rows_ref[8:16] = layers_of(modes_ref[:, 8:16, :])
        for group in range(groups):
            ahead = group + 2
            if ahead < groups:
                rows_ref[8 * ahead : 8 * ahead + 8] = layers_of(modes_ref[:, 8 * ahead : 8 * ahead + 8, :])
            elif ahead == groups:
                beyond = jnp.where(kinds_ref[0] == 2, 0.0, beyond_ref[:, :x_span] - rows_ref[B - 1])
                found = layers_of(after_ref[...])
                rows_ref[B] = jnp.where(step == rows_n - 1, beyond, found[0])
                rows_ref[B + 1 :] = found[1:]
            four_rows(2 * group)
            four_rows(2 * group + 1)

        for copy in copies(step, half):
            copy.start()

        @pl.when(step == rows_n - 1)
        def _():
            for copy in copies(step - 1, 1 - half) + copies(step, half):
                copy.wait()

    return pl.pallas_call(
        kernel,
        grid_spec=pltpu.PrefetchScalarGridSpec(
            num_scalar_prefetch=2,
            grid=(rows_n,),
            in_specs=[
                pl.BlockSpec((layers, B, x_span), lambda s, inv, kinds: (0, s, 0)),
                pl.BlockSpec((layers, 8, x_span), lambda s, inv, kinds: (0, jnp.minimum((s + 1) * (B // 8), y_span // 8 - 1), 0)),
                pl.BlockSpec((3, B, NZ, x_span), lambda s, inv, kinds: (0, s, 0, 0)),
                pl.BlockSpec((2 * layers, x_span + y_span), lambda s, inv, kinds: (0, 0)),
                pl.BlockSpec((layers, layers), lambda s, inv, kinds: (0, 0)),
                pl.BlockSpec((16 * NZ, 8 * NZ), lambda s, inv, kinds: (0, 0)),
            ],
            out_specs=[pl.BlockSpec(memory_space=pl.ANY), pl.BlockSpec(memory_space=pl.ANY)],
            scratch_shapes=[
                pltpu.VMEM((B + 8, NZ, x_span), f32),
                pltpu.VMEM((2, cols_n, 4, NZ, B * B), f32),
                pltpu.VMEM((NZ, x_span + y_span), f32),
                pltpu.SemaphoreType.DMA((2, cols_n)),
                pltpu.SemaphoreType.DMA((2, cols_n)),
            ],
        ),
        out_shape=[
            jax.ShapeDtypeStruct((3, slots, NZ, B * B), f32),
            jax.ShapeDtypeStruct((slots, NZ, B * B), f32),
        ],
        compiler_params=params(),
    )(inverse, kinds, modes, modes, star, sums, cosine_inverse, cosine_t)


def solve_interfaces(lines_x, lines_y, picks_x, picks_y, table_x, table_y, eig_x, eig_y, levels, kinds):
    rows_x, rows_y = lines_x.shape[0], lines_y.shape[1]
    half_x = lines_y.shape[2]
    width = min(256, half_x)

    def kernel(kinds_ref, lines_x_ref, lines_y_ref, picks_x_ref, picks_y_ref, table_x_ref, table_y_ref, eig_x_ref,
               eig_y_ref, levels_ref, sum_x_ref, fold_ref, hat_ref, out_hat_ref):
        level = levels_ref[kinds_ref[2]]
        hat_x = few_rows_times(lines_x_ref[...], table_y_ref[0], table_y_ref[1])
        for parity in range(2):
            hat_ref[:, parity * half_x : (parity + 1) * half_x] = few_rows_times(
                lines_y_ref[parity], table_x_ref[parity, 0], table_x_ref[parity, 1])
        right = spread(jnp.concatenate([hat_x, picks_y_ref[0]], axis=0))
        along = jnp.zeros((rows_x, NY), f32)
        for start in range(0, 2 * half_x, width):
            part = slice(start, start + width)
            left = spread_other(jnp.concatenate([picks_x_ref[0, :, part], hat_ref[:, part]], axis=0))
            field = lax.dot_general(left, right, (((0,), (0,)), ((), ())), preferred_element_type=f32)
            field = field * inverse_of(eig_x_ref[part, :1] + eig_y_ref[:1] + level)
            high, low = pieces(field)
            along += few_rows_times(picks_x_ref[1, :, part], high, low)
            out_hat_ref[:, part] = hat_ref[:, part] + few_rows_times(picks_y_ref[1], high, low, mm_transposed)
        sum_x_ref[...] = few_rows_times(hat_x + along, table_y_ref[0], table_y_ref[1])
        for parity in range(2):
            fold_ref[parity] = few_rows_times(
                out_hat_ref[:, parity * half_x : (parity + 1) * half_x],
                table_x_ref[parity, 0], table_x_ref[parity, 1], mm_transposed)

    vmem = pl.BlockSpec(memory_space=pltpu.VMEM)
    return pl.pallas_call(
        kernel,
        grid_spec=pltpu.PrefetchScalarGridSpec(
            num_scalar_prefetch=1,
            grid=(),
            in_specs=[vmem] * 8 + [pl.BlockSpec(memory_space=pltpu.SMEM)],
            out_specs=[vmem, vmem],
            scratch_shapes=[pltpu.VMEM((rows_y, NX), f32), pltpu.VMEM((rows_y, NX), f32)],
        ),
        out_shape=[
            jax.ShapeDtypeStruct((rows_x, NY), f32),
            jax.ShapeDtypeStruct((2, rows_y, half_x), f32),
        ],
        compiler_params=params(),
    )(kinds, lines_x, lines_y, picks_x, picks_y, table_x, table_y, eig_x, eig_y, levels)


def padded_rows(count):
    return -(-2 * count // 16) * 16


def shards(tables, velocity, fluid, block_place):
    pa_size = lax.axis_size("pa")
    pb_size = lax.axis_size("pb")
    group_count = pa_size * pb_size
    y_span, x_span = NY // pa_size, NX // pb_size
    rows_n, cols_n = y_span // B, x_span // B
    slots = block_place.shape[0]
    pa, pb = lax.axis_index("pa"), lax.axis_index("pb")

    def kind(index, size):
        return jnp.where(index == 0, 0, jnp.where(index == size - 1, 2, 1)).astype(jnp.int32)

    repeats = group_count // NZ
    kinds = jnp.stack([kind(pa, pa_size), kind(pb, pb_size), (pa * pb_size + pb) // repeats])
    slot_ids = jnp.arange(slots, dtype=jnp.int32)
    matches = block_place[None, :] == slot_ids[:, None]
    inverse = jnp.sum(jnp.where(matches, slot_ids[None, :], 0), axis=1).astype(jnp.int32)

    tile, low_edge, high_edge = gather_tile(velocity, fluid, inverse, rows_n, cols_n)

    def up(values, axis, size):
        return lax.ppermute(values, axis, [(i, i + 1) for i in range(size - 1)])

    def down(values, axis, size):
        return lax.ppermute(values, axis, [(i + 1, i) for i in range(size - 1)])

    x_below, x_above = up(high_edge, "pb", pb_size), down(low_edge, "pb", pb_size)
    y_below, y_above = up(tile[:3, -1], "pa", pa_size), down(tile[:3, 0], "pa", pa_size)

    cosine = jnp.asarray(tables["cosine"])
    local = {name: jnp.asarray(tables[name]) for name in (
        "y", "yr", "yt", "ytr", "x", "xt", "edge_y", "edge_x", "wide_y", "few_x", "eigen", "levels", "picks_x", "picks_y", "fold_x", "line_y",
        "eig_x", "eig_y")}
    star, modes, flux_x, flux_y = advance(
        tile, x_below, x_above, y_below, y_above, jnp.asarray(tables["cosine8"]), local["x"], kinds
    )
    spectrum, bundle = first_solve(
        modes, local["yt"], local["ytr"], local["xt"], local["wide_y"], local["few_x"], local["eigen"],
        local["levels"], flux_x, flux_y, cosine, kinds
    )
    width = x_span + y_span
    bundle = jnp.repeat(bundle, repeats, axis=1) if repeats > 1 else bundle
    arrived = lax.all_to_all(bundle, ("pa", "pb"), split_axis=1, concat_axis=1, tiled=True)
    arrived = arrived.reshape(3, pa_size, pb_size, width)
    on_y, on_x = arrived[..., :x_span], arrived[..., x_span:]
    count_y, count_x = pa_size - 1, pb_size - 1
    rows_y, rows_x = padded_rows(count_y), padded_rows(count_x)
    sums_y = on_y[1, :-1] + on_y[0, 1:]
    lines_y = jnp.concatenate([sums_y, on_y[2, :-1]]).reshape(2 * count_y, NX)
    lines_y = jnp.pad(lines_y, ((0, rows_y - 2 * count_y), (0, 0)))
    sums_x = on_x[1, :, :-1] + on_x[0, :, 1:]
    lines_x = jnp.stack([sums_x, on_x[2, :, :-1]]).transpose(0, 2, 1, 3).reshape(2 * count_x, NY)
    lines_x = jnp.pad(lines_x, ((0, rows_x - 2 * count_x), (0, 0)))
    lower, upper = lines_y[:, : NX // 2], lines_y[:, NX // 2 :][:, ::-1]
    sum_x, folded = solve_interfaces(
        lines_x, jnp.stack([lower + upper, lower - upper]), local["picks_x"], local["picks_y"], local["fold_x"],
        local["line_y"], local["eig_x"], local["eig_y"], local["levels"], kinds
    )
    sum_x = sum_x[:count_x]
    even, odd = folded[0, :count_y], folded[1, :count_y]
    sum_y = jnp.concatenate([even + odd, (even - odd)[:, ::-1]], axis=1)
    flux_y, flux_x = lines_y[count_y : 2 * count_y], lines_x[count_x : 2 * count_x]
    none_y, none_x = jnp.zeros((1, NX), f32), jnp.zeros((1, NY), f32)
    high_y = jnp.concatenate([sum_y, none_y]).reshape(pa_size, pb_size, x_span)
    low_y = jnp.concatenate([none_y, sum_y + flux_y]).reshape(pa_size, pb_size, x_span)
    high_x = jnp.concatenate([sum_x, none_x]).reshape(pb_size, pa_size, y_span).transpose(1, 0, 2)
    low_x = jnp.concatenate([none_x, sum_x + flux_x]).reshape(pb_size, pa_size, y_span).transpose(1, 0, 2)
    reply = jnp.stack([jnp.concatenate([low_y, low_x], axis=2), jnp.concatenate([high_y, high_x], axis=2)])
    reply = reply.reshape(2, group_count, width)
    home = lax.all_to_all(reply, ("pa", "pb"), split_axis=1, concat_axis=1, tiled=True)
    sums = home[:, ::repeats].reshape(2 * NZ, width)
    pressure_modes = second_solve(
        spectrum, sums, local["y"], local["yr"], local["x"], local["xt"], local["edge_y"], local["edge_x"],
        local["eigen"], local["levels"], kinds
    )
    return tuple(
        finish(pressure_modes, star, sums, jnp.asarray(tables["cosine_t"]), jnp.asarray(tables["cosine8t"]), inverse,
               kinds, slots)
    )


def make_tables(pa_size, pb_size):
    y_span, x_span = NY // pa_size, NX // pb_size
    cosine, levels = cosine_basis()
    cosine8 = np.einsum("kz,ab->kabz", cosine, np.eye(8)).reshape(8 * NZ, 8 * NZ)
    tables = {
        "cosine": single(cosine),
        "levels": single(levels),
        "cosine_t": single(cosine.T),
        "cosine8": left_table(cosine8),
        "cosine8t": left_table(cosine8.T),
    }
    values = {}
    for name, length in (("y", y_span), ("x", x_span)):
        bases = tile_bases(length)
        if name == "x":
            tables["x"] = np.stack([right_table(b) for b, _ in bases])
            tables["xt"] = np.stack([right_table(b.T) for b, _ in bases])
        else:
            tables["y"] = np.stack([left_table(b) for b, _ in bases])
            tables["yr"] = np.stack([right_table(b) for b, _ in bases])
            tables["yt"] = np.stack([left_table(b.T) for b, _ in bases])
            tables["ytr"] = np.stack([right_table(b.T) for b, _ in bases])
        edges = np.stack([np.repeat(b[[0, -1]], 8, axis=0) for b, _ in bases])
        tables["edge_" + name] = single(edges)
        few = np.zeros((3, 16, length), ml_dtypes.bfloat16)
        for i, (b, _) in enumerate(bases):
            few[i, 0:2], few[i, 8:10] = parts_of(b[[0, -1]])
        tables["few_" + name] = few
        tables["wide_" + name] = single(np.stack([
            np.repeat(b[[0, -1]][:, :, None], LANES, axis=2) for b, _ in bases]))
        values[name] = [v for _, v in bases]
    tables["eigen"] = single(
        np.stack([ey[:, None] + ex[None, :] for ey in values["y"] for ex in values["x"]])
    )
    basis_x, eig_x = sine_basis(NX, 1.0, 1.0)
    basis_y, eig_y = sine_basis(NY, 1.0, 1.0)
    half = NX // 2
    order = np.concatenate([np.arange(0, NX, 2), np.arange(1, NX, 2)])
    tables["fold_x"] = np.stack([split(basis_x[:half, parity::2]) for parity in range(2)])
    tables["line_y"] = split(basis_y)
    tables["eig_x"] = single(np.repeat(eig_x[order][:, None], LANES, axis=1))
    tables["eig_y"] = single(np.repeat(eig_y[None, :], 8, axis=0))
    for name, basis, tile in (("x", basis_x[:, order], x_span), ("y", basis_y, y_span)):
        above, below = basis[tile::tile], basis[tile - 1 : -1 : tile]
        count, length = above.shape
        picks = np.zeros((2, padded_rows(count), length))
        picks[0, : 2 * count] = np.concatenate([above + below, above])
        picks[1, :count] = above + below
        tables["picks_" + name] = single(picks)
    return tables


def solution(mesh):
    tables = make_tables(mesh.shape["pa"], mesh.shape["pb"])
    return jax.shard_map(
        functools.partial(shards, tables),
        mesh=mesh,
        in_specs=(P(None, ("pa", "pb"), None, None), P(("pa", "pb"), None, None), P(("pa", "pb"))),
        out_specs=(P(None, ("pa", "pb"), None, None), P(("pa", "pb"), None, None)),
        check_vma=False,
    )
```

```python
import functools

import jax
import jax.numpy as jnp
import ml_dtypes
import numpy as np
from jax import lax
from jax.experimental import pallas as pl
from jax.experimental.pallas import tpu as pltpu
from jax.sharding import PartitionSpec as P

NX = 2048
NY = 1024
NZ = 32
B = 32
LANES = 128
highest = lax.Precision.HIGHEST
f32 = jnp.float32
VMEM_LIMIT = 56 * 1024 * 1024


def cosine_basis():
    k = np.arange(NZ)[:, None]
    z = np.arange(NZ)[None, :]
    table = np.cos(np.pi * k * (z + 0.5) / NZ)
    table /= np.sqrt((table**2).sum(axis=1, keepdims=True))
    return table, 2.0 - 2.0 * np.cos(np.pi * np.arange(NZ) / NZ)


def sine_basis(length, lower_gap, upper_gap):
    span = length - 1 + lower_gap + upper_gap
    i = np.arange(length)[:, None]
    k = np.arange(1, length + 1)[None, :]
    table = np.sin(np.pi * k * (i + lower_gap) / span)
    table /= np.sqrt((table**2).sum(axis=0, keepdims=True))
    return table, 4.0 * np.sin(np.pi * np.arange(1, length + 1) / (2 * span)) ** 2


def tile_bases(length):
    return [sine_basis(length, *gaps) for gaps in ((1.0, 0.5), (0.5, 0.5), (0.5, 1.0))]


def parts_of(table):
    table = np.asarray(table, np.float64)
    high = table.astype(np.float32).astype(ml_dtypes.bfloat16)
    low = (table - high.astype(np.float64)).astype(np.float32).astype(ml_dtypes.bfloat16)
    return high, low


def split(table):
    return np.stack(parts_of(table), axis=-3)


def left_table(table):
    high, low = parts_of(table)
    return np.concatenate([high, high, low], axis=-1)


def right_table(table):
    high, low = parts_of(table)
    return np.concatenate([high, low, high], axis=-2)


def single(table):
    return np.asarray(table, np.float32)


def pieces(values):
    high = values.astype(jnp.bfloat16)
    return high, (values - high.astype(f32)).astype(jnp.bfloat16)


def mm(left, right):
    return jnp.dot(left, right, preferred_element_type=f32)


def table_times(table_ref, values):
    high, low = pieces(values)
    return mm(table_ref[...], jnp.concatenate([high, low, high], axis=0))


def times_table(values, table_ref):
    high, low = pieces(values)
    return mm(jnp.concatenate([high, high, low], axis=1), table_ref[...])


def mm_transposed(left, right):
    return lax.dot_general(left, right, (((1,), (1,)), ((), ())), preferred_element_type=f32)


def few_rows_times(values, high, low, product=mm):
    rows = values.shape[0]
    both = jnp.concatenate(pieces(values), axis=0)
    first = product(both, high)
    return first[:rows] + (first[rows:] + product(both[:rows], low))


def inverse_of(values):
    found = pl.reciprocal(values, approx=True)
    found = found * (2.0 - values * found)
    return found * (2.0 - values * found)


def dot_full(left, right, dims):
    return lax.dot_general(left, right, (dims, ((), ())), precision=highest, preferred_element_type=f32)


def lane_ids(rows=NZ):
    return lax.broadcasted_iota(jnp.int32, (rows, LANES), 1)


def swap_groups(four, lanes):
    odd = (lanes & 32) != 0
    high = lanes >= 64
    pairs = [jnp.where(odd, four[(d + 1) % 4], four[d]) for d in range(4)]
    picked = [jnp.where(high, pairs[(d + 2) % 4], pairs[d]) for d in range(4)]
    moved = [picked[0]] + [pltpu.roll(picked[d], 32 * d, 1) for d in range(1, 4)]
    pairs = [jnp.where(odd, moved[(1 - t) % 4], moved[-t % 4]) for t in range(4)]
    return [jnp.where(high, pairs[(t - 2) % 4], pairs[t]) for t in range(4)]


def spread(part):
    high, low = pieces(part)
    return jnp.concatenate([high, high, low], axis=0)


def spread_other(part):
    high, low = pieces(part)
    return jnp.concatenate([high, low, high], axis=0)


def params():
    return pltpu.CompilerParams(vmem_limit_bytes=VMEM_LIMIT)


def gather_tile(velocity, fluid, inverse, rows_n, cols_n):
    y_span, x_span = rows_n * B, cols_n * B
    quads = cols_n // 4

    def kernel(inverse_ref, *refs):
        flow_refs = refs[:cols_n]
        fraction_refs = refs[cols_n : 2 * cols_n]
        out_ref, low_ref, high_ref = refs[2 * cols_n :]
        step = pl.program_id(0)
        lanes = lane_ids()
        place = step % 2
        chunk = pl.ds(pl.multiple_of(step // 2 * LANES, LANES), LANES)
        high_mine = ((lanes & 31) // 16) == place
        low_mine = (((lanes + 1) & 31) // 16) == place
        for channel in range(4):
            low_edge = jnp.zeros((NZ, LANES), f32)
            high_edge = jnp.zeros((NZ, LANES), f32)
            for jq in range(8):
                for quad in range(quads):
                    four = []
                    for g in range(4):
                        at = quad * 4 + g
                        part = slice(jq * LANES, (jq + 1) * LANES)
                        if channel < 3:
                            four.append(flow_refs[at][channel, 0, :, part])
                        else:
                            four.append(fraction_refs[at][0, :, part])
                    rows = swap_groups(four, lanes)
                    for t in range(4):
                        out_ref[channel, jq * 4 + t, :, quad * LANES : (quad + 1) * LANES] = rows[t]
                    if channel < 3 and quad == 0:
                        here = ((lanes + 1) & 31) == 2 * jq
                        low_edge = jnp.where(here, pltpu.roll(four[0], (2 * jq + 127) % LANES, 1), low_edge)
                    if channel < 3 and quad == quads - 1:
                        here = (lanes & 31) == 2 * jq
                        high_edge = jnp.where(here, pltpu.roll(four[3], 97 + 2 * jq, 1), high_edge)
            if channel < 3:
                shift = place * 16
                low_ref[channel, :, chunk] = jnp.where(low_mine, pltpu.roll(low_edge, shift, 1), low_ref[channel, :, chunk])
                high_ref[channel, :, chunk] = jnp.where(
                    high_mine, pltpu.roll(high_edge, shift, 1), high_ref[channel, :, chunk])

    def flow_spec(col):
        return pl.BlockSpec((3, 1, NZ, B * B), lambda s, inv: (0, inv[s * cols_n + col], 0, 0))

    def fraction_spec(col):
        return pl.BlockSpec((1, NZ, B * B), lambda s, inv: (inv[s * cols_n + col], 0, 0))

    edge = pl.BlockSpec((3, NZ, 2 * y_span), lambda s, inv: (0, 0, 0))
    return pl.pallas_call(
        kernel,
        grid_spec=pltpu.PrefetchScalarGridSpec(
            num_scalar_prefetch=1,
            grid=(rows_n,),
            in_specs=[flow_spec(c) for c in range(cols_n)] + [fraction_spec(c) for c in range(cols_n)],
            out_specs=[pl.BlockSpec((4, B, NZ, x_span), lambda s, inv: (0, s, 0, 0)), edge, edge],
        ),
        out_shape=[
            jax.ShapeDtypeStruct((4, y_span, NZ, x_span), f32),
            jax.ShapeDtypeStruct((3, NZ, 2 * y_span), f32),
            jax.ShapeDtypeStruct((3, NZ, 2 * y_span), f32),
        ],
        compiler_params=params(),
    )(inverse, *([velocity] * cols_n), *([fluid] * cols_n))


def advance(tile, x_below, x_above, y_below, y_above, cosine, sine_x, kinds):
    _, y_span, _, x_span = tile.shape
    steps = y_span // B
    chunks = x_span // LANES

    def kernel(kinds_ref, main_ref, prev_ref, next_ref, xb_ref, xa_ref, yb_ref, ya_ref, cosine_ref, sine_ref,
               star_ref, modes_ref, gx_ref, gy_ref, mean_ref, rows_ref, source_ref, carry_ref):
        step = pl.program_id(0)
        lanes = lane_ids()
        layers = lax.broadcasted_iota(jnp.int32, (NZ, LANES), 0)
        first_layer, last_layer = layers == 0, layers == NZ - 1
        first_lane, last_lane = lanes == 0, lanes == LANES - 1

        rows_ref[:, 1 : B + 1] = main_ref[:3]

        @pl.when(step == 0)
        def _():
            rows_ref[:, 0] = yb_ref[...]
            carry_ref[...] = jnp.zeros_like(carry_ref)

        @pl.when(step > 0)
        def _():
            rows_ref[:, 0] = prev_ref[:3, 0]

        @pl.when(step == steps - 1)
        def _():
            rows_ref[:, B + 1] = ya_ref[...]

        @pl.when(step < steps - 1)
        def _():
            rows_ref[:, B + 1] = next_ref[:3, 0]

        y_chunk = pl.ds(pl.multiple_of(step // 4 * LANES, LANES), LANES)
        halo_chunk = pl.ds(pl.multiple_of(step // 2 * LANES, LANES), LANES)
        even_lane = (lanes & 1) == 0

        def row(group, r):
            j = group * 8 + r
            held = r % 4 * 32 + (step % 2) * 16 + 2 * (group * 2 + r // 4)
            at = (step % 4) * B + j
            star = {}
            flow = {}
            for h in range(chunks):
                for c in range(3):
                    flow[c, h] = rows_ref[c, j + 1, :, h * LANES : (h + 1) * LANES]
            edge, to_right, to_left = {}, {}, {}
            for c in range(3):
                both = jnp.where(even_lane, xb_ref[c, :, halo_chunk], xa_ref[c, :, halo_chunk])
                edge[c] = pltpu.roll(both, (LANES - held) % LANES, 1)
                for h in range(chunks):
                    to_right[c, h] = pltpu.roll(flow[c, h], 1, 1)
                    to_left[c, h] = pltpu.roll(flow[c, h], LANES - 1, 1)
            for h in range(chunks):
                part = slice(h * LANES, (h + 1) * LANES)
                take_up, take_down = [], []
                for e in range(3):
                    scaled = 0.125 * flow[e, h]
                    take_up.append(0.025 - scaled)
                    take_down.append(0.025 + scaled)
                fraction = main_ref[3, j, :, part]
                for c in range(3):
                    center = flow[c, h]
                    before = edge[c] if h == 0 else to_right[c, h - 1]
                    after = edge[c] if h == chunks - 1 else to_left[c, h + 1]
                    x_low = jnp.where(first_lane, before, to_right[c, h])
                    x_up = jnp.where(last_lane, after, to_left[c, h])
                    y_low = rows_ref[c, j, :, part]
                    y_up = rows_ref[c, j + 2, :, part]
                    z_low = jnp.where(first_layer, 0.0, pltpu.roll(center, 1, 0))
                    z_up = jnp.where(last_layer, 0.0, pltpu.roll(center, NZ - 1, 0))
                    total = (
                        0.85 * center
                        + (take_up[0] * x_up + take_down[0] * x_low)
                        + (take_up[1] * y_up + take_down[1] * y_low)
                        + (take_up[2] * z_up + take_down[2] * z_low)
                    )
                    value = fraction * total
                    if c == 2:
                        value = jnp.where(last_layer, 0.0, value)
                    star[c, h] = value
                    star_ref[c, j, :, part] = value
            before = 0.0
            for h in range(chunks):
                part = slice(h * LANES, (h + 1) * LANES)
                moved = pltpu.roll(star[0, h], 1, 1)
                x_low = jnp.where(first_lane, before, moved)
                before = moved
                z_low = jnp.where(first_layer, 0.0, pltpu.roll(star[2, h], 1, 0))
                y_low = carry_ref[:, part]
                source_ref[j, :, part] = (x_low - star[0, h]) + (y_low - star[1, h]) + (z_low - star[2, h])
                carry_ref[:, part] = star[1, h]
            edge = pltpu.roll(star[0, chunks - 1], (at + 1) % LANES, 1)
            gx_ref[:, y_chunk] = jnp.where(lanes == at, edge, gx_ref[:, y_chunk])

        def transform(group):
            rows = pl.ds(pl.multiple_of(group * 8, 8), 8)
            part = source_ref[rows]
            mean_ref[rows, :] = jnp.sum(part, axis=1) * NZ**-0.5
            part = part.reshape(8 * NZ, x_span)
            modes = times_table(table_times(cosine_ref, part), sine_ref)
            modes_ref[:, rows, :] = modes.reshape(NZ, 8, x_span)

        for r in range(8):
            row(0, r)

        def group_of_rows(group, _):
            transform(group - 1)
            for r in range(8):
                row(group, r)
            return _

        lax.fori_loop(1, B // 8, group_of_rows, 0)
        transform(B // 8 - 1)
        gy_ref[...] = carry_ref[...]

    full3 = pl.BlockSpec((3, NZ, 2 * y_span), lambda s, kinds: (0, 0, 0))
    return pl.pallas_call(
        kernel,
        grid_spec=pltpu.PrefetchScalarGridSpec(
            num_scalar_prefetch=1,
            grid=(steps,),
            in_specs=[
                pl.BlockSpec((4, B, NZ, x_span), lambda s, kinds: (0, s, 0, 0)),
                pl.BlockSpec((4, 1, NZ, x_span), lambda s, kinds: (0, jnp.maximum(s * B - 1, 0), 0, 0)),
                pl.BlockSpec((4, 1, NZ, x_span), lambda s, kinds: (0, jnp.minimum(s * B + B, y_span - 1), 0, 0)),
                full3,
                full3,
                pl.BlockSpec((3, NZ, x_span), lambda s, kinds: (0, 0, 0)),
                pl.BlockSpec((3, NZ, x_span), lambda s, kinds: (0, 0, 0)),
                pl.BlockSpec((8 * NZ, 24 * NZ), lambda s, kinds: (0, 0)),
                pl.BlockSpec((None, 3 * x_span, x_span), lambda s, kinds: (kinds[1], 0, 0)),
            ],
            out_specs=[
                pl.BlockSpec((3, B, NZ, x_span), lambda s, kinds: (0, s, 0, 0)),
                pl.BlockSpec((NZ, B, x_span), lambda s, kinds: (0, s, 0)),
                pl.BlockSpec((NZ, y_span), lambda s, kinds: (0, 0)),
                pl.BlockSpec((NZ, x_span), lambda s, kinds: (0, 0)),
                pl.BlockSpec((B, x_span), lambda s, kinds: (s, 0)),
            ],
            scratch_shapes=[
                pltpu.VMEM((3, B + 2, NZ, x_span), f32),
                pltpu.VMEM((B, NZ, x_span), f32),
                pltpu.VMEM((NZ, x_span), f32),
            ],
        ),
        out_shape=[
            jax.ShapeDtypeStruct((3, y_span, NZ, x_span), f32),
            jax.ShapeDtypeStruct((NZ, y_span, x_span), f32),
            jax.ShapeDtypeStruct((NZ, y_span), f32),
            jax.ShapeDtypeStruct((NZ, x_span), f32),
            jax.ShapeDtypeStruct((y_span, x_span), f32),
        ],
        compiler_params=params(),
    )(kinds, tile, tile, tile, x_below, x_above, y_below, y_above, cosine, sine_x)


def first_solve(modes, sine_yt, sine_ytr, sine_xt, edge_y, edge_x, eigen, levels, flux_x, flux_y, cosine, mean, exact_yt, exact_x, kinds):
    layers, y_span, x_span = modes.shape
    batch = 4
    steps = layers // batch
    sides = 2 * layers

    def kernel(kinds_ref, modes_ref, yt_ref, ytr_ref, xt_ref, edge_y_ref, edge_x_ref, eigen_ref, levels_ref,
               flux_x_ref, flux_y_ref, cosine_ref, mean_ref, exact_yt_ref, exact_x_ref, spectrum_ref, bundle_ref, rows_ref, columns_ref, exact_ref):
        step = pl.program_id(0)
        @pl.when(step == 0)
        def _():
            along_x = dot_full(mean_ref[...], exact_x_ref[...], ((1,), (0,)))
            exact_ref[...] = dot_full(exact_yt_ref[...], along_x, ((1,), (0,)))

        for i in range(batch):
            k = step * batch + i
            spectrum = table_times(yt_ref, modes_ref[i])
            if i == 0:
                spectrum = jnp.where(step == 0, exact_ref[...], spectrum)
            spectrum_ref[i] = spectrum
            high, low = pieces(spectrum * inverse_of(eigen_ref[...] + levels_ref[k]))
            found = mm(edge_y_ref[...], high) + mm(edge_y_ref[...], low)
            found = found[:8] + found[8:]
            rows_ref[pl.ds(k, 1)] = found[0:1]
            rows_ref[pl.ds(layers + k, 1)] = found[1:2]
            found = mm_transposed(edge_x_ref[...], high) + mm_transposed(edge_x_ref[...], low)
            found = found[:8] + found[8:]
            columns_ref[pl.ds(k, 1)] = found[0:1]
            columns_ref[pl.ds(layers + k, 1)] = found[1:2]

        @pl.when(step == steps - 1)
        def _():
            along_x = times_table(rows_ref[...], xt_ref)
            along_y = times_table(columns_ref[...], ytr_ref)
            cosine_table = cosine_ref[...]
            for line, values, flux_ref in ((0, along_x, flux_y_ref), (x_span, along_y, flux_x_ref)):
                part = slice(line, line + values.shape[1])
                bundle_ref[0, :, part] = values[:layers]
                bundle_ref[1, :, part] = values[layers:]
                bundle_ref[2, :, part] = dot_full(cosine_table, flux_ref[...], ((1,), (0,)))

    return pl.pallas_call(
        kernel,
        grid_spec=pltpu.PrefetchScalarGridSpec(
            num_scalar_prefetch=1,
            grid=(steps,),
            in_specs=[
                pl.BlockSpec((batch, y_span, x_span), lambda k, kinds: (k, 0, 0)),
                pl.BlockSpec((None, y_span, 3 * y_span), lambda k, kinds: (kinds[0], 0, 0)),
                pl.BlockSpec((None, 3 * y_span, y_span), lambda k, kinds: (kinds[0], 0, 0)),
                pl.BlockSpec((None, 3 * x_span, x_span), lambda k, kinds: (kinds[1], 0, 0)),
                pl.BlockSpec((None, 16, y_span), lambda k, kinds: (kinds[0], 0, 0)),
                pl.BlockSpec((None, 16, x_span), lambda k, kinds: (kinds[1], 0, 0)),
                pl.BlockSpec((None, y_span, x_span), lambda k, kinds: (kinds[0] * 3 + kinds[1], 0, 0)),
                pl.BlockSpec(memory_space=pltpu.SMEM),
                pl.BlockSpec((layers, y_span), lambda k, kinds: (0, 0)),
                pl.BlockSpec((layers, x_span), lambda k, kinds: (0, 0)),
                pl.BlockSpec((layers, layers), lambda k, kinds: (0, 0)),
                pl.BlockSpec((y_span, x_span), lambda k, kinds: (0, 0)),
                pl.BlockSpec((None, y_span, y_span), lambda k, kinds: (kinds[0], 0, 0)),
                pl.BlockSpec((None, x_span, x_span), lambda k, kinds: (kinds[1], 0, 0)),
            ],
            out_specs=[
                pl.BlockSpec((batch, y_span, x_span), lambda k, kinds: (k, 0, 0)),
                pl.BlockSpec((3, layers, x_span + y_span), lambda k, kinds: (0, 0, 0)),
            ],
            scratch_shapes=[pltpu.VMEM((sides, x_span), f32), pltpu.VMEM((sides, y_span), f32), pltpu.VMEM((y_span, x_span), f32)],
        ),
        out_shape=[
            jax.ShapeDtypeStruct((layers, y_span, x_span), f32),
            jax.ShapeDtypeStruct((3, layers, x_span + y_span), f32),
        ],
        compiler_params=params(),
    )(kinds, modes, sine_yt, sine_ytr, sine_xt, edge_y, edge_x, eigen, levels, flux_x, flux_y, cosine, mean, exact_yt, exact_x)


def second_solve(spectrum, sums, sine_y, sine_yr, sine_x, sine_xt, edge_y, edge_x, eigen, levels, kinds):
    layers, y_span, x_span = spectrum.shape
    batch = 8
    sides = 2 * layers

    def kernel(kinds_ref, spectrum_ref, sums_ref, y_ref, yr_ref, x_ref, xt_ref, edge_y_ref, edge_x_ref,
               eigen_ref, levels_ref, out_ref, along_x_ref, along_y_ref):
        step = pl.program_id(0)

        @pl.when(step == 0)
        def _():
            along_x_ref[...] = times_table(sums_ref[:, :x_span], x_ref)
            along_y_ref[...] = times_table(sums_ref[:, x_span:], yr_ref)

        low_side = pl.ds(pl.multiple_of(step * batch, batch), batch)
        high_side = pl.ds(pl.multiple_of(layers + step * batch, batch), batch)
        left = jnp.concatenate([along_y_ref[low_side], along_y_ref[high_side], edge_y_ref[...]], axis=0)
        right = jnp.concatenate([edge_x_ref[...], along_x_ref[low_side], along_x_ref[high_side]], axis=0)
        left_high = left.astype(jnp.bfloat16).astype(f32)
        blank = jnp.zeros((LANES - 12 * batch, y_span), f32)
        left = jnp.concatenate([left_high, left_high, left - left_high, blank], axis=0).T.astype(jnp.bfloat16)
        blank = jnp.zeros((LANES - 12 * batch, x_span), jnp.bfloat16)
        row_ids = lax.broadcasted_iota(jnp.int32, (4 * batch, x_span), 0) & (batch - 1)
        for start in range(0, batch, 4):
            along_y = []
            for i in range(start, start + 4):
                high, low = pieces(jnp.where(row_ids == i, right, 0.0))
                added = mm(left, jnp.concatenate([high, low, high, blank], axis=0))
                solved = (spectrum_ref[i] + added) * inverse_of(eigen_ref[...] + levels_ref[step * batch + i])
                along_y.append(table_times(y_ref, solved))
            found = times_table(jnp.concatenate(along_y, axis=0), xt_ref)
            out_ref[start : start + 4] = found.reshape(4, y_span, x_span)

    return pl.pallas_call(
        kernel,
        grid_spec=pltpu.PrefetchScalarGridSpec(
            num_scalar_prefetch=1,
            grid=(layers // batch,),
            in_specs=[
                pl.BlockSpec((batch, y_span, x_span), lambda k, kinds: (k, 0, 0)),
                pl.BlockSpec((sides, x_span + y_span), lambda k, kinds: (0, 0)),
                pl.BlockSpec((None, y_span, 3 * y_span), lambda k, kinds: (kinds[0], 0, 0)),
                pl.BlockSpec((None, 3 * y_span, y_span), lambda k, kinds: (kinds[0], 0, 0)),
                pl.BlockSpec((None, 3 * x_span, x_span), lambda k, kinds: (kinds[1], 0, 0)),
                pl.BlockSpec((None, 3 * x_span, x_span), lambda k, kinds: (kinds[1], 0, 0)),
                pl.BlockSpec((None, 2 * batch, y_span), lambda k, kinds: (kinds[0], 0, 0)),
                pl.BlockSpec((None, 2 * batch, x_span), lambda k, kinds: (kinds[1], 0, 0)),
                pl.BlockSpec((None, y_span, x_span), lambda k, kinds: (kinds[0] * 3 + kinds[1], 0, 0)),
                pl.BlockSpec(memory_space=pltpu.SMEM),
            ],
            out_specs=pl.BlockSpec((batch, y_span, x_span), lambda k, kinds: (k, 0, 0)),
            scratch_shapes=[
                pltpu.VMEM((sides, x_span), f32),
                pltpu.VMEM((sides, y_span), f32),
            ],
        ),
        out_shape=jax.ShapeDtypeStruct((layers, y_span, x_span), f32),
        compiler_params=params(),
    )(kinds, spectrum, sums, sine_y, sine_yr, sine_x, sine_xt, edge_y, edge_x, eigen, levels)


def finish(modes, star, sums, cosine_inverse, cosine_t, inverse, kinds, slots):
    layers, y_span, x_span = modes.shape
    rows_n, cols_n = y_span // B, x_span // B
    chunks = x_span // LANES

    def kernel(inverse_ref, kinds_ref, modes_ref, after_ref, star_ref, sums_ref, inverse_cosine_ref, cosine_ref,
               flow_out, pressure_out, rows_ref, blocks_ref, beyond_ref, flow_sem, pressure_sem):
        step = pl.program_id(0)
        half = step % 2

        def copies(at_step, at_half):
            found = []
            for col in range(cols_n):
                slot = inverse_ref[at_step * cols_n + col]
                found.append(pltpu.make_async_copy(
                    blocks_ref.at[at_half, col, pl.ds(0, 3)], flow_out.at[:, slot], flow_sem.at[at_half, col]))
                found.append(pltpu.make_async_copy(
                    blocks_ref.at[at_half, col, 3], pressure_out.at[slot], pressure_sem.at[at_half, col]))
            return found

        @pl.when(step >= 2)
        def _():
            for copy in copies(step - 2, half):
                copy.wait()

        @pl.when(step == 0)
        def _():
            beyond_ref[...] = dot_full(inverse_cosine_ref[...], sums_ref[layers:], ((1,), (0,)))

        lanes = lane_ids()
        layers_at = lax.broadcasted_iota(jnp.int32, (NZ, LANES), 0)
        last_layer = layers_at == NZ - 1
        last_lane = lanes == LANES - 1
        def layers_of(part):
            return table_times(cosine_ref, part.reshape(8 * NZ, x_span)).reshape(8, NZ, x_span)

        @pl.when(step == 0)
        def _():
            rows_ref[:8] = layers_of(modes_ref[:, :8, :])

        @pl.when(step > 0)
        def _():
            rows_ref[:8] = rows_ref[B:]

        def four_rows(jq):
            y = step * B + jq * 4
            y_chunk = pl.ds(pl.multiple_of(x_span + step * B // LANES * LANES, LANES), LANES)
            block = slice(jq * LANES, (jq + 1) * LANES)
            to_left = [
                [pltpu.roll(rows_ref[jq * 4 + t, :, h * LANES : (h + 1) * LANES], LANES - 1, 1) for t in range(4)]
                for h in range(chunks)
            ]
            for h in range(chunks):
                part = slice(h * LANES, (h + 1) * LANES)
                found = [[], [], [], []]
                for t in range(4):
                    j = jq * 4 + t
                    here = rows_ref[j, :, part]
                    if h == chunks - 1:
                        after = pltpu.roll(beyond_ref[:, y_chunk], LANES - 1 - (y + t) % LANES, 1)
                        after = jnp.where(kinds_ref[1] == 2, 0.0, after - here)
                    else:
                        after = to_left[h + 1][t]
                    x_up = jnp.where(last_lane, after, to_left[h][t])
                    y_up = rows_ref[j + 1, :, part]
                    z_up = jnp.where(last_layer, here, pltpu.roll(here, NZ - 1, 0))
                    found[0].append(star_ref[0, j, :, part] - (x_up - here))
                    found[1].append(star_ref[1, j, :, part] - (y_up - here))
                    found[2].append(star_ref[2, j, :, part] - (z_up - here))
                    found[3].append(here)
                for channel in range(4):
                    swapped = swap_groups(found[channel], lanes)
                    for g in range(4):
                        blocks_ref[half, 4 * h + g, channel, :, block] = swapped[g]

        groups = B // 8
        rows_ref[8:16] = layers_of(modes_ref[:, 8:16, :])
        for group in range(groups):
            ahead = group + 2
            if ahead < groups:
                rows_ref[8 * ahead : 8 * ahead + 8] = layers_of(modes_ref[:, 8 * ahead : 8 * ahead + 8, :])
            elif ahead == groups:
                beyond = jnp.where(kinds_ref[0] == 2, 0.0, beyond_ref[:, :x_span] - rows_ref[B - 1])
                found = layers_of(after_ref[...])
                rows_ref[B] = jnp.where(step == rows_n - 1, beyond, found[0])
                rows_ref[B + 1 :] = found[1:]
            four_rows(2 * group)
            four_rows(2 * group + 1)

        for copy in copies(step, half):
            copy.start()

        @pl.when(step == rows_n - 1)
        def _():
            for copy in copies(step - 1, 1 - half) + copies(step, half):
                copy.wait()

    return pl.pallas_call(
        kernel,
        grid_spec=pltpu.PrefetchScalarGridSpec(
            num_scalar_prefetch=2,
            grid=(rows_n,),
            in_specs=[
                pl.BlockSpec((layers, B, x_span), lambda s, inv, kinds: (0, s, 0)),
                pl.BlockSpec((layers, 8, x_span), lambda s, inv, kinds: (0, jnp.minimum((s + 1) * (B // 8), y_span // 8 - 1), 0)),
                pl.BlockSpec((3, B, NZ, x_span), lambda s, inv, kinds: (0, s, 0, 0)),
                pl.BlockSpec((2 * layers, x_span + y_span), lambda s, inv, kinds: (0, 0)),
                pl.BlockSpec((layers, layers), lambda s, inv, kinds: (0, 0)),
                pl.BlockSpec((8 * NZ, 24 * NZ), lambda s, inv, kinds: (0, 0)),
            ],
            out_specs=[pl.BlockSpec(memory_space=pl.ANY), pl.BlockSpec(memory_space=pl.ANY)],
            scratch_shapes=[
                pltpu.VMEM((B + 8, NZ, x_span), f32),
                pltpu.VMEM((2, cols_n, 4, NZ, B * B), f32),
                pltpu.VMEM((NZ, x_span + y_span), f32),
                pltpu.SemaphoreType.DMA((2, cols_n)),
                pltpu.SemaphoreType.DMA((2, cols_n)),
            ],
        ),
        out_shape=[
            jax.ShapeDtypeStruct((3, slots, NZ, B * B), f32),
            jax.ShapeDtypeStruct((slots, NZ, B * B), f32),
        ],
        compiler_params=params(),
    )(inverse, kinds, modes, modes, star, sums, cosine_inverse, cosine_t)


def solve_interfaces(lines_x, lines_y, picks_x, picks_y, table_x, table_y, eig_x, eig_y, levels, kinds):
    rows_x, rows_y = lines_x.shape[0], lines_y.shape[1]
    half_x = lines_y.shape[2]
    width = min(256, half_x)

    def kernel(kinds_ref, lines_x_ref, lines_y_ref, picks_x_ref, picks_y_ref, table_x_ref, table_y_ref, eig_x_ref,
               eig_y_ref, levels_ref, sum_x_ref, fold_ref, hat_ref, out_hat_ref):
        level = levels_ref[kinds_ref[2]]
        hat_x = few_rows_times(lines_x_ref[...], table_y_ref[0], table_y_ref[1])
        for parity in range(2):
            hat_ref[:, parity * half_x : (parity + 1) * half_x] = few_rows_times(
                lines_y_ref[parity], table_x_ref[parity, 0], table_x_ref[parity, 1])
        right = spread(jnp.concatenate([hat_x, picks_y_ref[0]], axis=0))
        along = jnp.zeros((rows_x, NY), f32)
        for start in range(0, 2 * half_x, width):
            part = slice(start, start + width)
            left = spread_other(jnp.concatenate([picks_x_ref[0, :, part], hat_ref[:, part]], axis=0))
            field = lax.dot_general(left, right, (((0,), (0,)), ((), ())), preferred_element_type=f32)
            field = field * inverse_of(eig_x_ref[part, :1] + eig_y_ref[:1] + level)
            high, low = pieces(field)
            along += few_rows_times(picks_x_ref[1, :, part], high, low)
            out_hat_ref[:, part] = hat_ref[:, part] + few_rows_times(picks_y_ref[1], high, low, mm_transposed)
        sum_x_ref[...] = few_rows_times(hat_x + along, table_y_ref[0], table_y_ref[1])
        for parity in range(2):
            fold_ref[parity] = few_rows_times(
                out_hat_ref[:, parity * half_x : (parity + 1) * half_x],
                table_x_ref[parity, 0], table_x_ref[parity, 1], mm_transposed)

    vmem = pl.BlockSpec(memory_space=pltpu.VMEM)
    return pl.pallas_call(
        kernel,
        grid_spec=pltpu.PrefetchScalarGridSpec(
            num_scalar_prefetch=1,
            grid=(),
            in_specs=[vmem] * 8 + [pl.BlockSpec(memory_space=pltpu.SMEM)],
            out_specs=[vmem, vmem],
            scratch_shapes=[pltpu.VMEM((rows_y, NX), f32), pltpu.VMEM((rows_y, NX), f32)],
        ),
        out_shape=[
            jax.ShapeDtypeStruct((rows_x, NY), f32),
            jax.ShapeDtypeStruct((2, rows_y, half_x), f32),
        ],
        compiler_params=params(),
    )(kinds, lines_x, lines_y, picks_x, picks_y, table_x, table_y, eig_x, eig_y, levels)


def padded_rows(count):
    return -(-2 * count // 16) * 16


def shards(tables, velocity, fluid, block_place):
    pa_size = lax.axis_size("pa")
    pb_size = lax.axis_size("pb")
    group_count = pa_size * pb_size
    y_span, x_span = NY // pa_size, NX // pb_size
    rows_n, cols_n = y_span // B, x_span // B
    slots = block_place.shape[0]
    pa, pb = lax.axis_index("pa"), lax.axis_index("pb")

    def kind(index, size):
        return jnp.where(index == 0, 0, jnp.where(index == size - 1, 2, 1)).astype(jnp.int32)

    repeats = group_count // NZ
    kinds = jnp.stack([kind(pa, pa_size), kind(pb, pb_size), (pa * pb_size + pb) // repeats])
    slot_ids = jnp.arange(slots, dtype=jnp.int32)
    matches = block_place[None, :] == slot_ids[:, None]
    inverse = jnp.sum(jnp.where(matches, slot_ids[None, :], 0), axis=1).astype(jnp.int32)

    tile, low_edge, high_edge = gather_tile(velocity, fluid, inverse, rows_n, cols_n)

    def up(values, axis, size):
        return lax.ppermute(values, axis, [(i, i + 1) for i in range(size - 1)])

    def down(values, axis, size):
        return lax.ppermute(values, axis, [(i + 1, i) for i in range(size - 1)])

    x_below, x_above = up(high_edge, "pb", pb_size), down(low_edge, "pb", pb_size)
    y_below, y_above = up(tile[:3, -1], "pa", pa_size), down(tile[:3, 0], "pa", pa_size)

    cosine = jnp.asarray(tables["cosine"])
    local = {name: jnp.asarray(tables[name]) for name in (
        "y", "yr", "yt", "ytr", "x", "xt", "edge_y", "edge_x", "few_y", "few_x", "exact_yt", "exact_x", "eigen", "levels", "picks_x", "picks_y", "fold_x", "line_y",
        "eig_x", "eig_y")}
    star, modes, flux_x, flux_y, mean = advance(
        tile, x_below, x_above, y_below, y_above, jnp.asarray(tables["cosine8"]), local["x"], kinds
    )
    spectrum, bundle = first_solve(
        modes, local["yt"], local["ytr"], local["xt"], local["few_y"], local["few_x"], local["eigen"],
        local["levels"], flux_x, flux_y, cosine, mean, local["exact_yt"], local["exact_x"], kinds
    )
    width = x_span + y_span
    bundle = jnp.repeat(bundle, repeats, axis=1) if repeats > 1 else bundle
    arrived = lax.all_to_all(bundle, ("pa", "pb"), split_axis=1, concat_axis=1, tiled=True)
    arrived = arrived.reshape(3, pa_size, pb_size, width)
    on_y, on_x = arrived[..., :x_span], arrived[..., x_span:]
    count_y, count_x = pa_size - 1, pb_size - 1
    rows_y, rows_x = padded_rows(count_y), padded_rows(count_x)
    sums_y = on_y[1, :-1] + on_y[0, 1:]
    lines_y = jnp.concatenate([sums_y, on_y[2, :-1]]).reshape(2 * count_y, NX)
    lines_y = jnp.pad(lines_y, ((0, rows_y - 2 * count_y), (0, 0)))
    sums_x = on_x[1, :, :-1] + on_x[0, :, 1:]
    lines_x = jnp.stack([sums_x, on_x[2, :, :-1]]).transpose(0, 2, 1, 3).reshape(2 * count_x, NY)
    lines_x = jnp.pad(lines_x, ((0, rows_x - 2 * count_x), (0, 0)))
    lower, upper = lines_y[:, : NX // 2], lines_y[:, NX // 2 :][:, ::-1]
    sum_x, folded = solve_interfaces(
        lines_x, jnp.stack([lower + upper, lower - upper]), local["picks_x"], local["picks_y"], local["fold_x"],
        local["line_y"], local["eig_x"], local["eig_y"], local["levels"], kinds
    )
    sum_x = sum_x[:count_x]
    even, odd = folded[0, :count_y], folded[1, :count_y]
    sum_y = jnp.concatenate([even + odd, (even - odd)[:, ::-1]], axis=1)
    flux_y, flux_x = lines_y[count_y : 2 * count_y], lines_x[count_x : 2 * count_x]
    none_y, none_x = jnp.zeros((1, NX), f32), jnp.zeros((1, NY), f32)
    high_y = jnp.concatenate([sum_y, none_y]).reshape(pa_size, pb_size, x_span)
    low_y = jnp.concatenate([none_y, sum_y + flux_y]).reshape(pa_size, pb_size, x_span)
    high_x = jnp.concatenate([sum_x, none_x]).reshape(pb_size, pa_size, y_span).transpose(1, 0, 2)
    low_x = jnp.concatenate([none_x, sum_x + flux_x]).reshape(pb_size, pa_size, y_span).transpose(1, 0, 2)
    reply = jnp.stack([jnp.concatenate([low_y, low_x], axis=2), jnp.concatenate([high_y, high_x], axis=2)])
    reply = reply.reshape(2, group_count, width)
    home = lax.all_to_all(reply, ("pa", "pb"), split_axis=1, concat_axis=1, tiled=True)
    sums = home[:, ::repeats].reshape(2 * NZ, width)
    pressure_modes = second_solve(
        spectrum, sums, local["y"], local["yr"], local["x"], local["xt"], local["edge_y"], local["edge_x"],
        local["eigen"], local["levels"], kinds
    )
    return tuple(
        finish(pressure_modes, star, sums, jnp.asarray(tables["cosine_t"]), jnp.asarray(tables["cosine8t"]), inverse,
               kinds, slots)
    )


def make_tables(pa_size, pb_size):
    y_span, x_span = NY // pa_size, NX // pb_size
    cosine, levels = cosine_basis()
    cosine8 = np.einsum("kz,ab->kabz", cosine, np.eye(8)).reshape(8 * NZ, 8 * NZ)
    tables = {
        "cosine": single(cosine),
        "levels": single(levels),
        "cosine_t": single(cosine.T),
        "cosine8": left_table(cosine8),
        "cosine8t": left_table(cosine8.T),
    }
    values = {}
    for name, length in (("y", y_span), ("x", x_span)):
        bases = tile_bases(length)
        if name == "x":
            tables["exact_x"] = single(np.stack([b for b, _ in bases]))
            tables["x"] = np.stack([right_table(b) for b, _ in bases])
            tables["xt"] = np.stack([right_table(b.T) for b, _ in bases])
        else:
            tables["exact_yt"] = single(np.stack([b.T for b, _ in bases]))
            tables["y"] = np.stack([left_table(b) for b, _ in bases])
            tables["yr"] = np.stack([right_table(b) for b, _ in bases])
            tables["yt"] = np.stack([left_table(b.T) for b, _ in bases])
            tables["ytr"] = np.stack([right_table(b.T) for b, _ in bases])
        edges = np.stack([np.repeat(b[[0, -1]], 8, axis=0) for b, _ in bases])
        tables["edge_" + name] = single(edges)
        few = np.zeros((3, 16, length), ml_dtypes.bfloat16)
        for i, (b, _) in enumerate(bases):
            few[i, 0:2], few[i, 8:10] = parts_of(b[[0, -1]])
        tables["few_" + name] = few
        values[name] = [v for _, v in bases]
    tables["eigen"] = single(
        np.stack([ey[:, None] + ex[None, :] for ey in values["y"] for ex in values["x"]])
    )
    basis_x, eig_x = sine_basis(NX, 1.0, 1.0)
    basis_y, eig_y = sine_basis(NY, 1.0, 1.0)
    half = NX // 2
    order = np.concatenate([np.arange(0, NX, 2), np.arange(1, NX, 2)])
    tables["fold_x"] = np.stack([split(basis_x[:half, parity::2]) for parity in range(2)])
    tables["line_y"] = split(basis_y)
    tables["eig_x"] = single(np.repeat(eig_x[order][:, None], LANES, axis=1))
    tables["eig_y"] = single(np.repeat(eig_y[None, :], 8, axis=0))
    for name, basis, tile in (("x", basis_x[:, order], x_span), ("y", basis_y, y_span)):
        above, below = basis[tile::tile], basis[tile - 1 : -1 : tile]
        count, length = above.shape
        picks = np.zeros((2, padded_rows(count), length))
        picks[0, : 2 * count] = np.concatenate([above + below, above])
        picks[1, :count] = above + below
        tables["picks_" + name] = single(picks)
    return tables


def solution(mesh):
    tables = make_tables(mesh.shape["pa"], mesh.shape["pb"])
    return jax.shard_map(
        functools.partial(shards, tables),
        mesh=mesh,
        in_specs=(P(None, ("pa", "pb"), None, None), P(("pa", "pb"), None, None), P(("pa", "pb"))),
        out_specs=(P(None, ("pa", "pb"), None, None), P(("pa", "pb"), None, None)),
        check_vma=False,
    )
```

```python
import functools

import jax
import jax.numpy as jnp
import ml_dtypes
import numpy as np
from jax import lax
from jax.experimental import pallas as pl
from jax.experimental.pallas import tpu as pltpu
from jax.sharding import PartitionSpec as P

NX = 2048
NY = 1024
NZ = 32
B = 32
LANES = 128
highest = lax.Precision.HIGHEST
f32 = jnp.float32
VMEM_LIMIT = 56 * 1024 * 1024


def cosine_basis():
    k = np.arange(NZ)[:, None]
    z = np.arange(NZ)[None, :]
    table = np.cos(np.pi * k * (z + 0.5) / NZ)
    table /= np.sqrt((table**2).sum(axis=1, keepdims=True))
    return table, 2.0 - 2.0 * np.cos(np.pi * np.arange(NZ) / NZ)


def sine_basis(length, lower_gap, upper_gap):
    span = length - 1 + lower_gap + upper_gap
    i = np.arange(length)[:, None]
    k = np.arange(1, length + 1)[None, :]
    table = np.sin(np.pi * k * (i + lower_gap) / span)
    table /= np.sqrt((table**2).sum(axis=0, keepdims=True))
    return table, 4.0 * np.sin(np.pi * np.arange(1, length + 1) / (2 * span)) ** 2


def tile_bases(length):
    return [sine_basis(length, *gaps) for gaps in ((1.0, 0.5), (0.5, 0.5), (0.5, 1.0))]


def parts_of(table):
    table = np.asarray(table, np.float64)
    high = table.astype(np.float32).astype(ml_dtypes.bfloat16)
    low = (table - high.astype(np.float64)).astype(np.float32).astype(ml_dtypes.bfloat16)
    return high, low


def split(table):
    return np.stack(parts_of(table), axis=-3)


def left_table(table):
    high, low = parts_of(table)
    return np.concatenate([high, high, low], axis=-1)


def right_table(table):
    high, low = parts_of(table)
    return np.concatenate([high, low, high], axis=-2)


def single(table):
    return np.asarray(table, np.float32)


def pieces(values):
    high = values.astype(jnp.bfloat16)
    return high, (values - high.astype(f32)).astype(jnp.bfloat16)


def mm(left, right):
    return jnp.dot(left, right, preferred_element_type=f32)


def table_times(table_ref, values):
    high, low = pieces(values)
    return mm(table_ref[...], jnp.concatenate([high, low, high], axis=0))


def times_table(values, table_ref):
    high, low = pieces(values)
    return mm(jnp.concatenate([high, high, low], axis=1), table_ref[...])


def mm_transposed(left, right):
    return lax.dot_general(left, right, (((1,), (1,)), ((), ())), preferred_element_type=f32)


def few_rows_times(values, high, low, product=mm):
    rows = values.shape[0]
    both = jnp.concatenate(pieces(values), axis=0)
    first = product(both, high)
    return first[:rows] + (first[rows:] + product(both[:rows], low))


def inverse_of(values):
    found = pl.reciprocal(values, approx=True)
    found = found * (2.0 - values * found)
    return found * (2.0 - values * found)


def dot_full(left, right, dims):
    return lax.dot_general(left, right, (dims, ((), ())), precision=highest, preferred_element_type=f32)


def lane_ids(rows=NZ):
    return lax.broadcasted_iota(jnp.int32, (rows, LANES), 1)


def swap_groups(four, lanes):
    odd = (lanes & 32) != 0
    high = lanes >= 64
    pairs = [jnp.where(odd, four[(d + 1) % 4], four[d]) for d in range(4)]
    picked = [jnp.where(high, pairs[(d + 2) % 4], pairs[d]) for d in range(4)]
    moved = [picked[0]] + [pltpu.roll(picked[d], 32 * d, 1) for d in range(1, 4)]
    pairs = [jnp.where(odd, moved[(1 - t) % 4], moved[-t % 4]) for t in range(4)]
    return [jnp.where(high, pairs[(t - 2) % 4], pairs[t]) for t in range(4)]


def spread(part):
    high, low = pieces(part)
    return jnp.concatenate([high, high, low], axis=0)


def spread_other(part):
    high, low = pieces(part)
    return jnp.concatenate([high, low, high], axis=0)


def params():
    return pltpu.CompilerParams(vmem_limit_bytes=VMEM_LIMIT)


def gather_tile(velocity, fluid, inverse, rows_n, cols_n):
    y_span, x_span = rows_n * B, cols_n * B
    quads = cols_n // 4

    def kernel(inverse_ref, *refs):
        flow_refs = refs[:cols_n]
        fraction_refs = refs[cols_n : 2 * cols_n]
        out_ref, low_ref, high_ref = refs[2 * cols_n :]
        step = pl.program_id(0)
        lanes = lane_ids()
        place = step % 2
        chunk = pl.ds(pl.multiple_of(step // 2 * LANES, LANES), LANES)
        high_mine = ((lanes & 31) // 16) == place
        low_mine = (((lanes + 1) & 31) // 16) == place
        for channel in range(4):
            low_edge = jnp.zeros((NZ, LANES), f32)
            high_edge = jnp.zeros((NZ, LANES), f32)
            for jq in range(8):
                for quad in range(quads):
                    four = []
                    for g in range(4):
                        at = quad * 4 + g
                        part = slice(jq * LANES, (jq + 1) * LANES)
                        if channel < 3:
                            four.append(flow_refs[at][channel, 0, :, part])
                        else:
                            four.append(fraction_refs[at][0, :, part])
                    rows = swap_groups(four, lanes)
                    for t in range(4):
                        out_ref[channel, jq * 4 + t, :, quad * LANES : (quad + 1) * LANES] = rows[t]
                    if channel < 3 and quad == 0:
                        here = ((lanes + 1) & 31) == 2 * jq
                        low_edge = jnp.where(here, pltpu.roll(four[0], (2 * jq + 127) % LANES, 1), low_edge)
                    if channel < 3 and quad == quads - 1:
                        here = (lanes & 31) == 2 * jq
                        high_edge = jnp.where(here, pltpu.roll(four[3], 97 + 2 * jq, 1), high_edge)
            if channel < 3:
                shift = place * 16
                low_ref[channel, :, chunk] = jnp.where(low_mine, pltpu.roll(low_edge, shift, 1), low_ref[channel, :, chunk])
                high_ref[channel, :, chunk] = jnp.where(
                    high_mine, pltpu.roll(high_edge, shift, 1), high_ref[channel, :, chunk])

    def flow_spec(col):
        return pl.BlockSpec((3, 1, NZ, B * B), lambda s, inv: (0, inv[s * cols_n + col], 0, 0))

    def fraction_spec(col):
        return pl.BlockSpec((1, NZ, B * B), lambda s, inv: (inv[s * cols_n + col], 0, 0))

    edge = pl.BlockSpec((3, NZ, 2 * y_span), lambda s, inv: (0, 0, 0))
    return pl.pallas_call(
        kernel,
        grid_spec=pltpu.PrefetchScalarGridSpec(
            num_scalar_prefetch=1,
            grid=(rows_n,),
            in_specs=[flow_spec(c) for c in range(cols_n)] + [fraction_spec(c) for c in range(cols_n)],
            out_specs=[pl.BlockSpec((4, B, NZ, x_span), lambda s, inv: (0, s, 0, 0)), edge, edge],
        ),
        out_shape=[
            jax.ShapeDtypeStruct((4, y_span, NZ, x_span), f32),
            jax.ShapeDtypeStruct((3, NZ, 2 * y_span), f32),
            jax.ShapeDtypeStruct((3, NZ, 2 * y_span), f32),
        ],
        compiler_params=params(),
    )(inverse, *([velocity] * cols_n), *([fluid] * cols_n))


def advance(tile, x_below, x_above, y_below, y_above, cosine, sine_x, kinds):
    _, y_span, _, x_span = tile.shape
    steps = y_span // B
    chunks = x_span // LANES

    def kernel(kinds_ref, main_ref, prev_ref, next_ref, xb_ref, xa_ref, yb_ref, ya_ref, cosine_ref, sine_ref,
               star_ref, modes_ref, gx_ref, gy_ref, mean_ref, rows_ref, source_ref, carry_ref):
        step = pl.program_id(0)
        lanes = lane_ids()
        layers = lax.broadcasted_iota(jnp.int32, (NZ, LANES), 0)
        first_layer, last_layer = layers == 0, layers == NZ - 1
        first_lane, last_lane = lanes == 0, lanes == LANES - 1

        @pl.when(step == 0)
        def _():
            rows_ref[:, 0] = yb_ref[...]
            carry_ref[...] = jnp.zeros_like(carry_ref)

        @pl.when(step > 0)
        def _():
            rows_ref[:, 0] = prev_ref[:3, 0]

        @pl.when(step == steps - 1)
        def _():
            rows_ref[:, 1] = ya_ref[...]

        @pl.when(step < steps - 1)
        def _():
            rows_ref[:, 1] = next_ref[:3, 0]

        y_chunk = pl.ds(pl.multiple_of(step // 4 * LANES, LANES), LANES)
        halo_chunk = pl.ds(pl.multiple_of(step // 2 * LANES, LANES), LANES)
        even_lane = (lanes & 1) == 0

        def neighbour_row(group, r, c, part):
            if 0 <= r < 8:
                return main_ref[c, group * 8 + r, :, part]
            if r < 0:
                inside = main_ref[c, jnp.maximum(group * 8 - 1, 0), :, part]
                return jnp.where(group == 0, rows_ref[c, 0, :, part], inside)
            inside = main_ref[c, jnp.minimum(group * 8 + 8, B - 1), :, part]
            return jnp.where(group == B // 8 - 1, rows_ref[c, 1, :, part], inside)

        def row(group, r):
            j = group * 8 + r
            held = r % 4 * 32 + (step % 2) * 16 + 2 * (group * 2 + r // 4)
            at = (step % 4) * B + j
            star = {}
            flow = {}
            for h in range(chunks):
                for c in range(3):
                    flow[c, h] = main_ref[c, j, :, h * LANES : (h + 1) * LANES]
            edge, to_right, to_left = {}, {}, {}
            for c in range(3):
                both = jnp.where(even_lane, xb_ref[c, :, halo_chunk], xa_ref[c, :, halo_chunk])
                edge[c] = pltpu.roll(both, (LANES - held) % LANES, 1)
                for h in range(chunks):
                    to_right[c, h] = pltpu.roll(flow[c, h], 1, 1)
                    to_left[c, h] = pltpu.roll(flow[c, h], LANES - 1, 1)
            for h in range(chunks):
                part = slice(h * LANES, (h + 1) * LANES)
                take_up, take_down = [], []
                for e in range(3):
                    scaled = 0.125 * flow[e, h]
                    take_up.append(0.025 - scaled)
                    take_down.append(0.025 + scaled)
                fraction = main_ref[3, j, :, part]
                for c in range(3):
                    center = flow[c, h]
                    before = edge[c] if h == 0 else to_right[c, h - 1]
                    after = edge[c] if h == chunks - 1 else to_left[c, h + 1]
                    x_low = jnp.where(first_lane, before, to_right[c, h])
                    x_up = jnp.where(last_lane, after, to_left[c, h])
                    y_low = neighbour_row(group, r - 1, c, part)
                    y_up = neighbour_row(group, r + 1, c, part)
                    z_low = jnp.where(first_layer, 0.0, pltpu.roll(center, 1, 0))
                    z_up = jnp.where(last_layer, 0.0, pltpu.roll(center, NZ - 1, 0))
                    total = (
                        0.85 * center
                        + (take_up[0] * x_up + take_down[0] * x_low)
                        + (take_up[1] * y_up + take_down[1] * y_low)
                        + (take_up[2] * z_up + take_down[2] * z_low)
                    )
                    value = fraction * total
                    if c == 2:
                        value = jnp.where(last_layer, 0.0, value)
                    star[c, h] = value
                    star_ref[c, j, :, part] = value
            before = 0.0
            for h in range(chunks):
                part = slice(h * LANES, (h + 1) * LANES)
                moved = pltpu.roll(star[0, h], 1, 1)
                x_low = jnp.where(first_lane, before, moved)
                before = moved
                z_low = jnp.where(first_layer, 0.0, pltpu.roll(star[2, h], 1, 0))
                y_low = carry_ref[:, part]
                source_ref[j, :, part] = (x_low - star[0, h]) + (y_low - star[1, h]) + (z_low - star[2, h])
                carry_ref[:, part] = star[1, h]
            edge = pltpu.roll(star[0, chunks - 1], (at + 1) % LANES, 1)
            gx_ref[:, y_chunk] = jnp.where(lanes == at, edge, gx_ref[:, y_chunk])

        def transform(group):
            rows = pl.ds(pl.multiple_of(group * 8, 8), 8)
            part = source_ref[rows]
            mean_ref[rows, :] = jnp.sum(part, axis=1) * NZ**-0.5
            part = part.reshape(8 * NZ, x_span)
            modes = times_table(table_times(cosine_ref, part), sine_ref)
            modes_ref[:, rows, :] = modes.reshape(NZ, 8, x_span)

        for r in range(8):
            row(0, r)

        def group_of_rows(group, _):
            transform(group - 1)
            for r in range(8):
                row(group, r)
            return _

        lax.fori_loop(1, B // 8, group_of_rows, 0)
        transform(B // 8 - 1)
        gy_ref[...] = carry_ref[...]

    full3 = pl.BlockSpec((3, NZ, 2 * y_span), lambda s, kinds: (0, 0, 0))
    return pl.pallas_call(
        kernel,
        grid_spec=pltpu.PrefetchScalarGridSpec(
            num_scalar_prefetch=1,
            grid=(steps,),
            in_specs=[
                pl.BlockSpec((4, B, NZ, x_span), lambda s, kinds: (0, s, 0, 0)),
                pl.BlockSpec((4, 1, NZ, x_span), lambda s, kinds: (0, jnp.maximum(s * B - 1, 0), 0, 0)),
                pl.BlockSpec((4, 1, NZ, x_span), lambda s, kinds: (0, jnp.minimum(s * B + B, y_span - 1), 0, 0)),
                full3,
                full3,
                pl.BlockSpec((3, NZ, x_span), lambda s, kinds: (0, 0, 0)),
                pl.BlockSpec((3, NZ, x_span), lambda s, kinds: (0, 0, 0)),
                pl.BlockSpec((8 * NZ, 24 * NZ), lambda s, kinds: (0, 0)),
                pl.BlockSpec((None, 3 * x_span, x_span), lambda s, kinds: (kinds[1], 0, 0)),
            ],
            out_specs=[
                pl.BlockSpec((3, B, NZ, x_span), lambda s, kinds: (0, s, 0, 0)),
                pl.BlockSpec((NZ, B, x_span), lambda s, kinds: (0, s, 0)),
                pl.BlockSpec((NZ, y_span), lambda s, kinds: (0, 0)),
                pl.BlockSpec((NZ, x_span), lambda s, kinds: (0, 0)),
                pl.BlockSpec((B, x_span), lambda s, kinds: (s, 0)),
            ],
            scratch_shapes=[
                pltpu.VMEM((3, 2, NZ, x_span), f32),
                pltpu.VMEM((B, NZ, x_span), f32),
                pltpu.VMEM((NZ, x_span), f32),
            ],
        ),
        out_shape=[
            jax.ShapeDtypeStruct((3, y_span, NZ, x_span), f32),
            jax.ShapeDtypeStruct((NZ, y_span, x_span), f32),
            jax.ShapeDtypeStruct((NZ, y_span), f32),
            jax.ShapeDtypeStruct((NZ, x_span), f32),
            jax.ShapeDtypeStruct((y_span, x_span), f32),
        ],
        compiler_params=params(),
    )(kinds, tile, tile, tile, x_below, x_above, y_below, y_above, cosine, sine_x)


def first_solve(modes, sine_yt, sine_ytr, sine_xt, edge_y, edge_x, eigen, levels, flux_x, flux_y, cosine, mean, exact_yt, exact_x, kinds):
    layers, y_span, x_span = modes.shape
    batch = 4
    steps = layers // batch
    sides = 2 * layers

    def kernel(kinds_ref, modes_ref, yt_ref, ytr_ref, xt_ref, edge_y_ref, edge_x_ref, eigen_ref, levels_ref,
               flux_x_ref, flux_y_ref, cosine_ref, mean_ref, exact_yt_ref, exact_x_ref, spectrum_ref, bundle_ref, rows_ref, columns_ref, exact_ref):
        step = pl.program_id(0)
        @pl.when(step == 0)
        def _():
            along_x = dot_full(mean_ref[...], exact_x_ref[...], ((1,), (0,)))
            exact_ref[...] = dot_full(exact_yt_ref[...], along_x, ((1,), (0,)))

        for i in range(batch):
            k = step * batch + i
            spectrum = table_times(yt_ref, modes_ref[i])
            if i == 0:
                spectrum = jnp.where(step == 0, exact_ref[...], spectrum)
            spectrum_ref[i] = spectrum
            high, low = pieces(spectrum * inverse_of(eigen_ref[...] + levels_ref[k]))
            found = mm(edge_y_ref[...], high) + mm(edge_y_ref[...], low)
            found = found[:8] + found[8:]
            rows_ref[pl.ds(k, 1)] = found[0:1]
            rows_ref[pl.ds(layers + k, 1)] = found[1:2]
            found = mm_transposed(edge_x_ref[...], high) + mm_transposed(edge_x_ref[...], low)
            found = found[:8] + found[8:]
            columns_ref[pl.ds(k, 1)] = found[0:1]
            columns_ref[pl.ds(layers + k, 1)] = found[1:2]

        @pl.when(step == steps - 1)
        def _():
            along_x = times_table(rows_ref[...], xt_ref)
            along_y = times_table(columns_ref[...], ytr_ref)
            cosine_table = cosine_ref[...]
            for line, values, flux_ref in ((0, along_x, flux_y_ref), (x_span, along_y, flux_x_ref)):
                part = slice(line, line + values.shape[1])
                bundle_ref[0, :, part] = values[:layers]
                bundle_ref[1, :, part] = values[layers:]
                bundle_ref[2, :, part] = dot_full(cosine_table, flux_ref[...], ((1,), (0,)))

    return pl.pallas_call(
        kernel,
        grid_spec=pltpu.PrefetchScalarGridSpec(
            num_scalar_prefetch=1,
            grid=(steps,),
            in_specs=[
                pl.BlockSpec((batch, y_span, x_span), lambda k, kinds: (k, 0, 0)),
                pl.BlockSpec((None, y_span, 3 * y_span), lambda k, kinds: (kinds[0], 0, 0)),
                pl.BlockSpec((None, 3 * y_span, y_span), lambda k, kinds: (kinds[0], 0, 0)),
                pl.BlockSpec((None, 3 * x_span, x_span), lambda k, kinds: (kinds[1], 0, 0)),
                pl.BlockSpec((None, 16, y_span), lambda k, kinds: (kinds[0], 0, 0)),
                pl.BlockSpec((None, 16, x_span), lambda k, kinds: (kinds[1], 0, 0)),
                pl.BlockSpec((None, y_span, x_span), lambda k, kinds: (kinds[0] * 3 + kinds[1], 0, 0)),
                pl.BlockSpec(memory_space=pltpu.SMEM),
                pl.BlockSpec((layers, y_span), lambda k, kinds: (0, 0)),
                pl.BlockSpec((layers, x_span), lambda k, kinds: (0, 0)),
                pl.BlockSpec((layers, layers), lambda k, kinds: (0, 0)),
                pl.BlockSpec((y_span, x_span), lambda k, kinds: (0, 0)),
                pl.BlockSpec((None, y_span, y_span), lambda k, kinds: (kinds[0], 0, 0)),
                pl.BlockSpec((None, x_span, x_span), lambda k, kinds: (kinds[1], 0, 0)),
            ],
            out_specs=[
                pl.BlockSpec((batch, y_span, x_span), lambda k, kinds: (k, 0, 0)),
                pl.BlockSpec((3, layers, x_span + y_span), lambda k, kinds: (0, 0, 0)),
            ],
            scratch_shapes=[pltpu.VMEM((sides, x_span), f32), pltpu.VMEM((sides, y_span), f32), pltpu.VMEM((y_span, x_span), f32)],
        ),
        out_shape=[
            jax.ShapeDtypeStruct((layers, y_span, x_span), f32),
            jax.ShapeDtypeStruct((3, layers, x_span + y_span), f32),
        ],
        compiler_params=params(),
    )(kinds, modes, sine_yt, sine_ytr, sine_xt, edge_y, edge_x, eigen, levels, flux_x, flux_y, cosine, mean, exact_yt, exact_x)


def second_solve(spectrum, sums, sine_y, sine_yr, sine_x, sine_xt, edge_y, edge_x, eigen, levels, kinds):
    layers, y_span, x_span = spectrum.shape
    batch = 8
    sides = 2 * layers

    def kernel(kinds_ref, spectrum_ref, sums_ref, y_ref, yr_ref, x_ref, xt_ref, edge_y_ref, edge_x_ref,
               eigen_ref, levels_ref, out_ref, along_x_ref, along_y_ref):
        step = pl.program_id(0)

        @pl.when(step == 0)
        def _():
            along_x_ref[...] = times_table(sums_ref[:, :x_span], x_ref)
            along_y_ref[...] = times_table(sums_ref[:, x_span:], yr_ref)

        low_side = pl.ds(pl.multiple_of(step * batch, batch), batch)
        high_side = pl.ds(pl.multiple_of(layers + step * batch, batch), batch)
        left = jnp.concatenate([along_y_ref[low_side], along_y_ref[high_side], edge_y_ref[...]], axis=0)
        right = jnp.concatenate([edge_x_ref[...], along_x_ref[low_side], along_x_ref[high_side]], axis=0)
        left_high = left.astype(jnp.bfloat16).astype(f32)
        blank = jnp.zeros((LANES - 12 * batch, y_span), f32)
        left = jnp.concatenate([left_high, left_high, left - left_high, blank], axis=0).T.astype(jnp.bfloat16)
        blank = jnp.zeros((LANES - 12 * batch, x_span), jnp.bfloat16)
        row_ids = lax.broadcasted_iota(jnp.int32, (4 * batch, x_span), 0) & (batch - 1)
        for start in range(0, batch, 4):
            along_y = []
            for i in range(start, start + 4):
                high, low = pieces(jnp.where(row_ids == i, right, 0.0))
                added = mm(left, jnp.concatenate([high, low, high, blank], axis=0))
                solved = (spectrum_ref[i] + added) * inverse_of(eigen_ref[...] + levels_ref[step * batch + i])
                along_y.append(table_times(y_ref, solved))
            found = times_table(jnp.concatenate(along_y, axis=0), xt_ref)
            out_ref[start : start + 4] = found.reshape(4, y_span, x_span)

    return pl.pallas_call(
        kernel,
        grid_spec=pltpu.PrefetchScalarGridSpec(
            num_scalar_prefetch=1,
            grid=(layers // batch,),
            in_specs=[
                pl.BlockSpec((batch, y_span, x_span), lambda k, kinds: (k, 0, 0)),
                pl.BlockSpec((sides, x_span + y_span), lambda k, kinds: (0, 0)),
                pl.BlockSpec((None, y_span, 3 * y_span), lambda k, kinds: (kinds[0], 0, 0)),
                pl.BlockSpec((None, 3 * y_span, y_span), lambda k, kinds: (kinds[0], 0, 0)),
                pl.BlockSpec((None, 3 * x_span, x_span), lambda k, kinds: (kinds[1], 0, 0)),
                pl.BlockSpec((None, 3 * x_span, x_span), lambda k, kinds: (kinds[1], 0, 0)),
                pl.BlockSpec((None, 2 * batch, y_span), lambda k, kinds: (kinds[0], 0, 0)),
                pl.BlockSpec((None, 2 * batch, x_span), lambda k, kinds: (kinds[1], 0, 0)),
                pl.BlockSpec((None, y_span, x_span), lambda k, kinds: (kinds[0] * 3 + kinds[1], 0, 0)),
                pl.BlockSpec(memory_space=pltpu.SMEM),
            ],
            out_specs=pl.BlockSpec((batch, y_span, x_span), lambda k, kinds: (k, 0, 0)),
            scratch_shapes=[
                pltpu.VMEM((sides, x_span), f32),
                pltpu.VMEM((sides, y_span), f32),
            ],
        ),
        out_shape=jax.ShapeDtypeStruct((layers, y_span, x_span), f32),
        compiler_params=params(),
    )(kinds, spectrum, sums, sine_y, sine_yr, sine_x, sine_xt, edge_y, edge_x, eigen, levels)


def finish(modes, star, sums, cosine_inverse, cosine_t, inverse, kinds, slots):
    layers, y_span, x_span = modes.shape
    rows_n, cols_n = y_span // B, x_span // B
    chunks = x_span // LANES

    def kernel(inverse_ref, kinds_ref, modes_ref, after_ref, star_ref, sums_ref, inverse_cosine_ref, cosine_ref,
               flow_out, pressure_out, rows_ref, blocks_ref, beyond_ref, flow_sem, pressure_sem):
        step = pl.program_id(0)
        half = step % 2

        def copies(at_step, at_half):
            found = []
            for col in range(cols_n):
                slot = inverse_ref[at_step * cols_n + col]
                found.append(pltpu.make_async_copy(
                    blocks_ref.at[at_half, col, pl.ds(0, 3)], flow_out.at[:, slot], flow_sem.at[at_half, col]))
                found.append(pltpu.make_async_copy(
                    blocks_ref.at[at_half, col, 3], pressure_out.at[slot], pressure_sem.at[at_half, col]))
            return found

        @pl.when(step >= 2)
        def _():
            for copy in copies(step - 2, half):
                copy.wait()

        @pl.when(step == 0)
        def _():
            beyond_ref[...] = dot_full(inverse_cosine_ref[...], sums_ref[layers:], ((1,), (0,)))

        lanes = lane_ids()
        layers_at = lax.broadcasted_iota(jnp.int32, (NZ, LANES), 0)
        last_layer = layers_at == NZ - 1
        last_lane = lanes == LANES - 1
        def layers_of(part):
            return table_times(cosine_ref, part.reshape(8 * NZ, x_span)).reshape(8, NZ, x_span)

        @pl.when(step == 0)
        def _():
            rows_ref[:8] = layers_of(modes_ref[:, :8, :])

        @pl.when(step > 0)
        def _():
            rows_ref[:8] = rows_ref[B:]

        def four_rows(jq):
            y = step * B + jq * 4
            y_chunk = pl.ds(pl.multiple_of(x_span + step * B // LANES * LANES, LANES), LANES)
            block = slice(jq * LANES, (jq + 1) * LANES)
            to_left = [
                [pltpu.roll(rows_ref[jq * 4 + t, :, h * LANES : (h + 1) * LANES], LANES - 1, 1) for t in range(4)]
                for h in range(chunks)
            ]
            for h in range(chunks):
                part = slice(h * LANES, (h + 1) * LANES)
                found = [[], [], [], []]
                for t in range(4):
                    j = jq * 4 + t
                    here = rows_ref[j, :, part]
                    if h == chunks - 1:
                        after = pltpu.roll(beyond_ref[:, y_chunk], LANES - 1 - (y + t) % LANES, 1)
                        after = jnp.where(kinds_ref[1] == 2, 0.0, after - here)
                    else:
                        after = to_left[h + 1][t]
                    x_up = jnp.where(last_lane, after, to_left[h][t])
                    y_up = rows_ref[j + 1, :, part]
                    z_up = jnp.where(last_layer, here, pltpu.roll(here, NZ - 1, 0))
                    found[0].append(star_ref[0, j, :, part] - (x_up - here))
                    found[1].append(star_ref[1, j, :, part] - (y_up - here))
                    found[2].append(star_ref[2, j, :, part] - (z_up - here))
                    found[3].append(here)
                for channel in range(4):
                    swapped = swap_groups(found[channel], lanes)
                    for g in range(4):
                        blocks_ref[half, 4 * h + g, channel, :, block] = swapped[g]

        groups = B // 8
        rows_ref[8:16] = layers_of(modes_ref[:, 8:16, :])
        for group in range(groups):
            ahead = group + 2
            if ahead < groups:
                rows_ref[8 * ahead : 8 * ahead + 8] = layers_of(modes_ref[:, 8 * ahead : 8 * ahead + 8, :])
            elif ahead == groups:
                beyond = jnp.where(kinds_ref[0] == 2, 0.0, beyond_ref[:, :x_span] - rows_ref[B - 1])
                found = layers_of(after_ref[...])
                rows_ref[B] = jnp.where(step == rows_n - 1, beyond, found[0])
                rows_ref[B + 1 :] = found[1:]
            four_rows(2 * group)
            four_rows(2 * group + 1)

        for copy in copies(step, half):
            copy.start()

        @pl.when(step == rows_n - 1)
        def _():
            for copy in copies(step - 1, 1 - half) + copies(step, half):
                copy.wait()

    return pl.pallas_call(
        kernel,
        grid_spec=pltpu.PrefetchScalarGridSpec(
            num_scalar_prefetch=2,
            grid=(rows_n,),
            in_specs=[
                pl.BlockSpec((layers, B, x_span), lambda s, inv, kinds: (0, s, 0)),
                pl.BlockSpec((layers, 8, x_span), lambda s, inv, kinds: (0, jnp.minimum((s + 1) * (B // 8), y_span // 8 - 1), 0)),
                pl.BlockSpec((3, B, NZ, x_span), lambda s, inv, kinds: (0, s, 0, 0)),
                pl.BlockSpec((2 * layers, x_span + y_span), lambda s, inv, kinds: (0, 0)),
                pl.BlockSpec((layers, layers), lambda s, inv, kinds: (0, 0)),
                pl.BlockSpec((8 * NZ, 24 * NZ), lambda s, inv, kinds: (0, 0)),
            ],
            out_specs=[pl.BlockSpec(memory_space=pl.ANY), pl.BlockSpec(memory_space=pl.ANY)],
            scratch_shapes=[
                pltpu.VMEM((B + 8, NZ, x_span), f32),
                pltpu.VMEM((2, cols_n, 4, NZ, B * B), f32),
                pltpu.VMEM((NZ, x_span + y_span), f32),
                pltpu.SemaphoreType.DMA((2, cols_n)),
                pltpu.SemaphoreType.DMA((2, cols_n)),
            ],
        ),
        out_shape=[
            jax.ShapeDtypeStruct((3, slots, NZ, B * B), f32),
            jax.ShapeDtypeStruct((slots, NZ, B * B), f32),
        ],
        compiler_params=params(),
    )(inverse, kinds, modes, modes, star, sums, cosine_inverse, cosine_t)


def solve_interfaces(lines_x, lines_y, picks_x, picks_y, table_x, table_y, eig_x, eig_y, levels, kinds):
    rows_x, rows_y = lines_x.shape[0], lines_y.shape[1]
    half_x = lines_y.shape[2]
    width = min(256, half_x)

    def kernel(kinds_ref, lines_x_ref, lines_y_ref, picks_x_ref, picks_y_ref, table_x_ref, table_y_ref, eig_x_ref,
               eig_y_ref, levels_ref, sum_x_ref, fold_ref, hat_ref, out_hat_ref):
        level = levels_ref[kinds_ref[2]]
        hat_x = few_rows_times(lines_x_ref[...], table_y_ref[0], table_y_ref[1])
        for parity in range(2):
            hat_ref[:, parity * half_x : (parity + 1) * half_x] = few_rows_times(
                lines_y_ref[parity], table_x_ref[parity, 0], table_x_ref[parity, 1])
        right = spread(jnp.concatenate([hat_x, picks_y_ref[0]], axis=0))
        along = jnp.zeros((rows_x, NY), f32)
        for start in range(0, 2 * half_x, width):
            part = slice(start, start + width)
            left = spread_other(jnp.concatenate([picks_x_ref[0, :, part], hat_ref[:, part]], axis=0))
            field = lax.dot_general(left, right, (((0,), (0,)), ((), ())), preferred_element_type=f32)
            field = field * inverse_of(eig_x_ref[part, :1] + eig_y_ref[:1] + level)
            high, low = pieces(field)
            along += few_rows_times(picks_x_ref[1, :, part], high, low)
            out_hat_ref[:, part] = hat_ref[:, part] + few_rows_times(picks_y_ref[1], high, low, mm_transposed)
        sum_x_ref[...] = few_rows_times(hat_x + along, table_y_ref[0], table_y_ref[1])
        for parity in range(2):
            fold_ref[parity] = few_rows_times(
                out_hat_ref[:, parity * half_x : (parity + 1) * half_x],
                table_x_ref[parity, 0], table_x_ref[parity, 1], mm_transposed)

    vmem = pl.BlockSpec(memory_space=pltpu.VMEM)
    return pl.pallas_call(
        kernel,
        grid_spec=pltpu.PrefetchScalarGridSpec(
            num_scalar_prefetch=1,
            grid=(),
            in_specs=[vmem] * 8 + [pl.BlockSpec(memory_space=pltpu.SMEM)],
            out_specs=[vmem, vmem],
            scratch_shapes=[pltpu.VMEM((rows_y, NX), f32), pltpu.VMEM((rows_y, NX), f32)],
        ),
        out_shape=[
            jax.ShapeDtypeStruct((rows_x, NY), f32),
            jax.ShapeDtypeStruct((2, rows_y, half_x), f32),
        ],
        compiler_params=params(),
    )(kinds, lines_x, lines_y, picks_x, picks_y, table_x, table_y, eig_x, eig_y, levels)


def padded_rows(count):
    return -(-2 * count // 16) * 16


def shards(tables, velocity, fluid, block_place):
    pa_size = lax.axis_size("pa")
    pb_size = lax.axis_size("pb")
    group_count = pa_size * pb_size
    y_span, x_span = NY // pa_size, NX // pb_size
    rows_n, cols_n = y_span // B, x_span // B
    slots = block_place.shape[0]
    pa, pb = lax.axis_index("pa"), lax.axis_index("pb")

    def kind(index, size):
        return jnp.where(index == 0, 0, jnp.where(index == size - 1, 2, 1)).astype(jnp.int32)

    repeats = group_count // NZ
    kinds = jnp.stack([kind(pa, pa_size), kind(pb, pb_size), (pa * pb_size + pb) // repeats])
    slot_ids = jnp.arange(slots, dtype=jnp.int32)
    matches = block_place[None, :] == slot_ids[:, None]
    inverse = jnp.sum(jnp.where(matches, slot_ids[None, :], 0), axis=1).astype(jnp.int32)

    tile, low_edge, high_edge = gather_tile(velocity, fluid, inverse, rows_n, cols_n)

    def up(values, axis, size):
        return lax.ppermute(values, axis, [(i, i + 1) for i in range(size - 1)])

    def down(values, axis, size):
        return lax.ppermute(values, axis, [(i + 1, i) for i in range(size - 1)])

    x_below, x_above = up(high_edge, "pb", pb_size), down(low_edge, "pb", pb_size)
    y_below, y_above = up(tile[:3, -1], "pa", pa_size), down(tile[:3, 0], "pa", pa_size)

    cosine = jnp.asarray(tables["cosine"])
    local = {name: jnp.asarray(tables[name]) for name in (
        "y", "yr", "yt", "ytr", "x", "xt", "edge_y", "edge_x", "few_y", "few_x", "exact_yt", "exact_x", "eigen", "levels", "picks_x", "picks_y", "fold_x", "line_y",
        "eig_x", "eig_y")}
    star, modes, flux_x, flux_y, mean = advance(
        tile, x_below, x_above, y_below, y_above, jnp.asarray(tables["cosine8"]), local["x"], kinds
    )
    spectrum, bundle = first_solve(
        modes, local["yt"], local["ytr"], local["xt"], local["few_y"], local["few_x"], local["eigen"],
        local["levels"], flux_x, flux_y, cosine, mean, local["exact_yt"], local["exact_x"], kinds
    )
    width = x_span + y_span
    bundle = jnp.repeat(bundle, repeats, axis=1) if repeats > 1 else bundle
    arrived = lax.all_to_all(bundle, ("pa", "pb"), split_axis=1, concat_axis=1, tiled=True)
    arrived = arrived.reshape(3, pa_size, pb_size, width)
    on_y, on_x = arrived[..., :x_span], arrived[..., x_span:]
    count_y, count_x = pa_size - 1, pb_size - 1
    rows_y, rows_x = padded_rows(count_y), padded_rows(count_x)
    sums_y = on_y[1, :-1] + on_y[0, 1:]
    lines_y = jnp.concatenate([sums_y, on_y[2, :-1]]).reshape(2 * count_y, NX)
    lines_y = jnp.pad(lines_y, ((0, rows_y - 2 * count_y), (0, 0)))
    sums_x = on_x[1, :, :-1] + on_x[0, :, 1:]
    lines_x = jnp.stack([sums_x, on_x[2, :, :-1]]).transpose(0, 2, 1, 3).reshape(2 * count_x, NY)
    lines_x = jnp.pad(lines_x, ((0, rows_x - 2 * count_x), (0, 0)))
    lower, upper = lines_y[:, : NX // 2], lines_y[:, NX // 2 :][:, ::-1]
    sum_x, folded = solve_interfaces(
        lines_x, jnp.stack([lower + upper, lower - upper]), local["picks_x"], local["picks_y"], local["fold_x"],
        local["line_y"], local["eig_x"], local["eig_y"], local["levels"], kinds
    )
    sum_x = sum_x[:count_x]
    even, odd = folded[0, :count_y], folded[1, :count_y]
    sum_y = jnp.concatenate([even + odd, (even - odd)[:, ::-1]], axis=1)
    flux_y, flux_x = lines_y[count_y : 2 * count_y], lines_x[count_x : 2 * count_x]
    none_y, none_x = jnp.zeros((1, NX), f32), jnp.zeros((1, NY), f32)
    high_y = jnp.concatenate([sum_y, none_y]).reshape(pa_size, pb_size, x_span)
    low_y = jnp.concatenate([none_y, sum_y + flux_y]).reshape(pa_size, pb_size, x_span)
    high_x = jnp.concatenate([sum_x, none_x]).reshape(pb_size, pa_size, y_span).transpose(1, 0, 2)
    low_x = jnp.concatenate([none_x, sum_x + flux_x]).reshape(pb_size, pa_size, y_span).transpose(1, 0, 2)
    reply = jnp.stack([jnp.concatenate([low_y, low_x], axis=2), jnp.concatenate([high_y, high_x], axis=2)])
    reply = reply.reshape(2, group_count, width)
    home = lax.all_to_all(reply, ("pa", "pb"), split_axis=1, concat_axis=1, tiled=True)
    sums = home[:, ::repeats].reshape(2 * NZ, width)
    pressure_modes = second_solve(
        spectrum, sums, local["y"], local["yr"], local["x"], local["xt"], local["edge_y"], local["edge_x"],
        local["eigen"], local["levels"], kinds
    )
    return tuple(
        finish(pressure_modes, star, sums, jnp.asarray(tables["cosine_t"]), jnp.asarray(tables["cosine8t"]), inverse,
               kinds, slots)
    )


def make_tables(pa_size, pb_size):
    y_span, x_span = NY // pa_size, NX // pb_size
    cosine, levels = cosine_basis()
    cosine8 = np.einsum("kz,ab->kabz", cosine, np.eye(8)).reshape(8 * NZ, 8 * NZ)
    tables = {
        "cosine": single(cosine),
        "levels": single(levels),
        "cosine_t": single(cosine.T),
        "cosine8": left_table(cosine8),
        "cosine8t": left_table(cosine8.T),
    }
    values = {}
    for name, length in (("y", y_span), ("x", x_span)):
        bases = tile_bases(length)
        if name == "x":
            tables["exact_x"] = single(np.stack([b for b, _ in bases]))
            tables["x"] = np.stack([right_table(b) for b, _ in bases])
            tables["xt"] = np.stack([right_table(b.T) for b, _ in bases])
        else:
            tables["exact_yt"] = single(np.stack([b.T for b, _ in bases]))
            tables["y"] = np.stack([left_table(b) for b, _ in bases])
            tables["yr"] = np.stack([right_table(b) for b, _ in bases])
            tables["yt"] = np.stack([left_table(b.T) for b, _ in bases])
            tables["ytr"] = np.stack([right_table(b.T) for b, _ in bases])
        edges = np.stack([np.repeat(b[[0, -1]], 8, axis=0) for b, _ in bases])
        tables["edge_" + name] = single(edges)
        few = np.zeros((3, 16, length), ml_dtypes.bfloat16)
        for i, (b, _) in enumerate(bases):
            few[i, 0:2], few[i, 8:10] = parts_of(b[[0, -1]])
        tables["few_" + name] = few
        values[name] = [v for _, v in bases]
    tables["eigen"] = single(
        np.stack([ey[:, None] + ex[None, :] for ey in values["y"] for ex in values["x"]])
    )
    basis_x, eig_x = sine_basis(NX, 1.0, 1.0)
    basis_y, eig_y = sine_basis(NY, 1.0, 1.0)
    half = NX // 2
    order = np.concatenate([np.arange(0, NX, 2), np.arange(1, NX, 2)])
    tables["fold_x"] = np.stack([split(basis_x[:half, parity::2]) for parity in range(2)])
    tables["line_y"] = split(basis_y)
    tables["eig_x"] = single(np.repeat(eig_x[order][:, None], LANES, axis=1))
    tables["eig_y"] = single(np.repeat(eig_y[None, :], 8, axis=0))
    for name, basis, tile in (("x", basis_x[:, order], x_span), ("y", basis_y, y_span)):
        above, below = basis[tile::tile], basis[tile - 1 : -1 : tile]
        count, length = above.shape
        picks = np.zeros((2, padded_rows(count), length))
        picks[0, : 2 * count] = np.concatenate([above + below, above])
        picks[1, :count] = above + below
        tables["picks_" + name] = single(picks)
    return tables


def solution(mesh):
    tables = make_tables(mesh.shape["pa"], mesh.shape["pb"])
    return jax.shard_map(
        functools.partial(shards, tables),
        mesh=mesh,
        in_specs=(P(None, ("pa", "pb"), None, None), P(("pa", "pb"), None, None), P(("pa", "pb"))),
        out_specs=(P(None, ("pa", "pb"), None, None), P(("pa", "pb"), None, None)),
        check_vma=False,
    )
```

```python
import functools

import jax
import jax.numpy as jnp
import ml_dtypes
import numpy as np
from jax import lax
from jax.experimental import pallas as pl
from jax.experimental.pallas import tpu as pltpu
from jax.sharding import PartitionSpec as P

NX = 2048
NY = 1024
NZ = 32
B = 32
LANES = 128
highest = lax.Precision.HIGHEST
f32 = jnp.float32
VMEM_LIMIT = 34 * 1024 * 1024


def cosine_basis():
    k = np.arange(NZ)[:, None]
    z = np.arange(NZ)[None, :]
    table = np.cos(np.pi * k * (z + 0.5) / NZ)
    table /= np.sqrt((table**2).sum(axis=1, keepdims=True))
    return table, 2.0 - 2.0 * np.cos(np.pi * np.arange(NZ) / NZ)


def sine_basis(length, lower_gap, upper_gap):
    span = length - 1 + lower_gap + upper_gap
    i = np.arange(length)[:, None]
    k = np.arange(1, length + 1)[None, :]
    table = np.sin(np.pi * k * (i + lower_gap) / span)
    table /= np.sqrt((table**2).sum(axis=0, keepdims=True))
    return table, 4.0 * np.sin(np.pi * np.arange(1, length + 1) / (2 * span)) ** 2


def tile_bases(length):
    return [sine_basis(length, *gaps) for gaps in ((1.0, 0.5), (0.5, 0.5), (0.5, 1.0))]


def parts_of(table):
    table = np.asarray(table, np.float64)
    high = table.astype(np.float32).astype(ml_dtypes.bfloat16)
    low = (table - high.astype(np.float64)).astype(np.float32).astype(ml_dtypes.bfloat16)
    return high, low


def split(table):
    return np.stack(parts_of(table), axis=-3)


def left_table(table):
    high, low = parts_of(table)
    return np.concatenate([high, high, low], axis=-1)


def right_table(table):
    high, low = parts_of(table)
    return np.concatenate([high, low, high], axis=-2)


def single(table):
    return np.asarray(table, np.float32)


def pieces(values):
    high = values.astype(jnp.bfloat16)
    return high, (values - high.astype(f32)).astype(jnp.bfloat16)


def mm(left, right):
    return jnp.dot(left, right, preferred_element_type=f32)


def table_times(table_ref, values):
    high, low = pieces(values)
    return mm(table_ref[...], jnp.concatenate([high, low, high], axis=0))


def times_table(values, table_ref):
    high, low = pieces(values)
    return mm(jnp.concatenate([high, high, low], axis=1), table_ref[...])


def mm_transposed(left, right):
    return lax.dot_general(left, right, (((1,), (1,)), ((), ())), preferred_element_type=f32)


def few_rows_times(values, high, low, product=mm):
    rows = values.shape[0]
    both = jnp.concatenate(pieces(values), axis=0)
    first = product(both, high)
    return first[:rows] + (first[rows:] + product(both[:rows], low))


def inverse_of(values):
    found = pl.reciprocal(values, approx=True)
    found = found * (2.0 - values * found)
    return found * (2.0 - values * found)


def dot_full(left, right, dims):
    return lax.dot_general(left, right, (dims, ((), ())), precision=highest, preferred_element_type=f32)


def lane_ids(rows=NZ):
    return lax.broadcasted_iota(jnp.int32, (rows, LANES), 1)


def swap_groups(four, lanes):
    odd = (lanes & 32) != 0
    high = lanes >= 64
    pairs = [jnp.where(odd, four[(d + 1) % 4], four[d]) for d in range(4)]
    picked = [jnp.where(high, pairs[(d + 2) % 4], pairs[d]) for d in range(4)]
    moved = [picked[0]] + [pltpu.roll(picked[d], 32 * d, 1) for d in range(1, 4)]
    pairs = [jnp.where(odd, moved[(1 - t) % 4], moved[-t % 4]) for t in range(4)]
    return [jnp.where(high, pairs[(t - 2) % 4], pairs[t]) for t in range(4)]


def spread(part):
    high, low = pieces(part)
    return jnp.concatenate([high, high, low], axis=0)


def spread_other(part):
    high, low = pieces(part)
    return jnp.concatenate([high, low, high], axis=0)


def params():
    return pltpu.CompilerParams(vmem_limit_bytes=VMEM_LIMIT)


def gather_tile(velocity, fluid, inverse, rows_n, cols_n):
    y_span, x_span = rows_n * B, cols_n * B
    quads = cols_n // 4

    def kernel(inverse_ref, *refs):
        flow_refs = refs[:cols_n]
        fraction_refs = refs[cols_n : 2 * cols_n]
        out_ref, low_ref, high_ref = refs[2 * cols_n :]
        step = pl.program_id(0)
        lanes = lane_ids()
        place = step % 2
        chunk = pl.ds(pl.multiple_of(step // 2 * LANES, LANES), LANES)
        high_mine = ((lanes & 31) // 16) == place
        low_mine = (((lanes + 1) & 31) // 16) == place
        for channel in range(4):
            low_edge = jnp.zeros((NZ, LANES), f32)
            high_edge = jnp.zeros((NZ, LANES), f32)
            for jq in range(8):
                for quad in range(quads):
                    four = []
                    for g in range(4):
                        at = quad * 4 + g
                        part = slice(jq * LANES, (jq + 1) * LANES)
                        if channel < 3:
                            four.append(flow_refs[at][channel, 0, :, part])
                        else:
                            four.append(fraction_refs[at][0, :, part])
                    rows = swap_groups(four, lanes)
                    for t in range(4):
                        out_ref[channel, jq * 4 + t, :, quad * LANES : (quad + 1) * LANES] = rows[t]
                    if channel < 3 and quad == 0:
                        here = ((lanes + 1) & 31) == 2 * jq
                        low_edge = jnp.where(here, pltpu.roll(four[0], (2 * jq + 127) % LANES, 1), low_edge)
                    if channel < 3 and quad == quads - 1:
                        here = (lanes & 31) == 2 * jq
                        high_edge = jnp.where(here, pltpu.roll(four[3], 97 + 2 * jq, 1), high_edge)
            if channel < 3:
                shift = place * 16
                low_ref[channel, :, chunk] = jnp.where(low_mine, pltpu.roll(low_edge, shift, 1), low_ref[channel, :, chunk])
                high_ref[channel, :, chunk] = jnp.where(
                    high_mine, pltpu.roll(high_edge, shift, 1), high_ref[channel, :, chunk])

    def flow_spec(col):
        return pl.BlockSpec((3, 1, NZ, B * B), lambda s, inv: (0, inv[s * cols_n + col], 0, 0))

    def fraction_spec(col):
        return pl.BlockSpec((1, NZ, B * B), lambda s, inv: (inv[s * cols_n + col], 0, 0))

    edge = pl.BlockSpec((3, NZ, 2 * y_span), lambda s, inv: (0, 0, 0))
    return pl.pallas_call(
        kernel,
        grid_spec=pltpu.PrefetchScalarGridSpec(
            num_scalar_prefetch=1,
            grid=(rows_n,),
            in_specs=[flow_spec(c) for c in range(cols_n)] + [fraction_spec(c) for c in range(cols_n)],
            out_specs=[pl.BlockSpec((4, B, NZ, x_span), lambda s, inv: (0, s, 0, 0)), edge, edge],
        ),
        out_shape=[
            jax.ShapeDtypeStruct((4, y_span, NZ, x_span), f32),
            jax.ShapeDtypeStruct((3, NZ, 2 * y_span), f32),
            jax.ShapeDtypeStruct((3, NZ, 2 * y_span), f32),
        ],
        compiler_params=params(),
    )(inverse, *([velocity] * cols_n), *([fluid] * cols_n))


def advance(tile, x_below, x_above, y_below, y_above, cosine, sine_x, kinds):
    _, y_span, _, x_span = tile.shape
    steps = y_span // B
    chunks = x_span // LANES

    def kernel(kinds_ref, main_ref, prev_ref, next_ref, xb_ref, xa_ref, yb_ref, ya_ref, cosine_ref, sine_ref,
               star_ref, modes_ref, gx_ref, gy_ref, mean_ref, rows_ref, source_ref, carry_ref):
        step = pl.program_id(0)
        lanes = lane_ids()
        layers = lax.broadcasted_iota(jnp.int32, (NZ, LANES), 0)
        first_layer, last_layer = layers == 0, layers == NZ - 1
        first_lane, last_lane = lanes == 0, lanes == LANES - 1

        @pl.when(step == 0)
        def _():
            rows_ref[:, 0] = yb_ref[...]
            carry_ref[...] = jnp.zeros_like(carry_ref)

        @pl.when(step > 0)
        def _():
            rows_ref[:, 0] = prev_ref[:3, 0]

        @pl.when(step == steps - 1)
        def _():
            rows_ref[:, 1] = ya_ref[...]

        @pl.when(step < steps - 1)
        def _():
            rows_ref[:, 1] = next_ref[:3, 0]

        y_chunk = pl.ds(pl.multiple_of(step // 4 * LANES, LANES), LANES)
        halo_chunk = pl.ds(pl.multiple_of(step // 2 * LANES, LANES), LANES)
        even_lane = (lanes & 1) == 0

        def neighbour_row(group, r, c, part):
            if 0 <= r < 8:
                return main_ref[c, group * 8 + r, :, part]
            if r < 0:
                inside = main_ref[c, jnp.maximum(group * 8 - 1, 0), :, part]
                return jnp.where(group == 0, rows_ref[c, 0, :, part], inside)
            inside = main_ref[c, jnp.minimum(group * 8 + 8, B - 1), :, part]
            return jnp.where(group == B // 8 - 1, rows_ref[c, 1, :, part], inside)

        def row(group, r):
            j = group * 8 + r
            held = r % 4 * 32 + (step % 2) * 16 + 2 * (group * 2 + r // 4)
            at = (step % 4) * B + j
            star = {}
            flow = {}
            for h in range(chunks):
                for c in range(3):
                    flow[c, h] = main_ref[c, j, :, h * LANES : (h + 1) * LANES]
            edge, to_right, to_left = {}, {}, {}
            for c in range(3):
                both = jnp.where(even_lane, xb_ref[c, :, halo_chunk], xa_ref[c, :, halo_chunk])
                edge[c] = pltpu.roll(both, (LANES - held) % LANES, 1)
                for h in range(chunks):
                    to_right[c, h] = pltpu.roll(flow[c, h], 1, 1)
                    to_left[c, h] = pltpu.roll(flow[c, h], LANES - 1, 1)
            for h in range(chunks):
                part = slice(h * LANES, (h + 1) * LANES)
                take_up, take_down = [], []
                for e in range(3):
                    scaled = 0.125 * flow[e, h]
                    take_up.append(0.025 - scaled)
                    take_down.append(0.025 + scaled)
                fraction = main_ref[3, j, :, part]
                for c in range(3):
                    center = flow[c, h]
                    before = edge[c] if h == 0 else to_right[c, h - 1]
                    after = edge[c] if h == chunks - 1 else to_left[c, h + 1]
                    x_low = jnp.where(first_lane, before, to_right[c, h])
                    x_up = jnp.where(last_lane, after, to_left[c, h])
                    y_low = neighbour_row(group, r - 1, c, part)
                    y_up = neighbour_row(group, r + 1, c, part)
                    z_low = jnp.where(first_layer, 0.0, pltpu.roll(center, 1, 0))
                    z_up = jnp.where(last_layer, 0.0, pltpu.roll(center, NZ - 1, 0))
                    total = (
                        0.85 * center
                        + (take_up[0] * x_up + take_down[0] * x_low)
                        + (take_up[1] * y_up + take_down[1] * y_low)
                        + (take_up[2] * z_up + take_down[2] * z_low)
                    )
                    value = fraction * total
                    if c == 2:
                        value = jnp.where(last_layer, 0.0, value)
                    star[c, h] = value
                    star_ref[c, j, :, part] = value
            before = 0.0
            for h in range(chunks):
                part = slice(h * LANES, (h + 1) * LANES)
                moved = pltpu.roll(star[0, h], 1, 1)
                x_low = jnp.where(first_lane, before, moved)
                before = moved
                z_low = jnp.where(first_layer, 0.0, pltpu.roll(star[2, h], 1, 0))
                y_low = carry_ref[:, part]
                source_ref[j, :, part] = (x_low - star[0, h]) + (y_low - star[1, h]) + (z_low - star[2, h])
                carry_ref[:, part] = star[1, h]
            edge = pltpu.roll(star[0, chunks - 1], (at + 1) % LANES, 1)
            gx_ref[:, y_chunk] = jnp.where(lanes == at, edge, gx_ref[:, y_chunk])

        def transform(group):
            rows = pl.ds(pl.multiple_of(group * 8, 8), 8)
            part = source_ref[rows]
            mean_ref[rows, :] = jnp.sum(part, axis=1) * NZ**-0.5
            part = part.reshape(8 * NZ, x_span)
            modes = times_table(table_times(cosine_ref, part), sine_ref)
            modes_ref[:, rows, :] = modes.reshape(NZ, 8, x_span)

        for r in range(8):
            row(0, r)

        def group_of_rows(group, _):
            transform(group - 1)
            for r in range(8):
                row(group, r)
            return _

        lax.fori_loop(1, B // 8, group_of_rows, 0)
        transform(B // 8 - 1)
        gy_ref[...] = carry_ref[...]

    full3 = pl.BlockSpec((3, NZ, 2 * y_span), lambda s, kinds: (0, 0, 0))
    return pl.pallas_call(
        kernel,
        grid_spec=pltpu.PrefetchScalarGridSpec(
            num_scalar_prefetch=1,
            grid=(steps,),
            in_specs=[
                pl.BlockSpec((4, B, NZ, x_span), lambda s, kinds: (0, s, 0, 0)),
                pl.BlockSpec((4, 1, NZ, x_span), lambda s, kinds: (0, jnp.maximum(s * B - 1, 0), 0, 0)),
                pl.BlockSpec((4, 1, NZ, x_span), lambda s, kinds: (0, jnp.minimum(s * B + B, y_span - 1), 0, 0)),
                full3,
                full3,
                pl.BlockSpec((3, NZ, x_span), lambda s, kinds: (0, 0, 0)),
                pl.BlockSpec((3, NZ, x_span), lambda s, kinds: (0, 0, 0)),
                pl.BlockSpec((8 * NZ, 24 * NZ), lambda s, kinds: (0, 0)),
                pl.BlockSpec((None, 3 * x_span, x_span), lambda s, kinds: (kinds[1], 0, 0)),
            ],
            out_specs=[
                pl.BlockSpec((3, B, NZ, x_span), lambda s, kinds: (0, s, 0, 0)),
                pl.BlockSpec((NZ, B, x_span), lambda s, kinds: (0, s, 0)),
                pl.BlockSpec((NZ, y_span), lambda s, kinds: (0, 0)),
                pl.BlockSpec((NZ, x_span), lambda s, kinds: (0, 0)),
                pl.BlockSpec((B, x_span), lambda s, kinds: (s, 0)),
            ],
            scratch_shapes=[
                pltpu.VMEM((3, 2, NZ, x_span), f32),
                pltpu.VMEM((B, NZ, x_span), f32),
                pltpu.VMEM((NZ, x_span), f32),
            ],
        ),
        out_shape=[
            jax.ShapeDtypeStruct((3, y_span, NZ, x_span), f32),
            jax.ShapeDtypeStruct((NZ, y_span, x_span), f32),
            jax.ShapeDtypeStruct((NZ, y_span), f32),
            jax.ShapeDtypeStruct((NZ, x_span), f32),
            jax.ShapeDtypeStruct((y_span, x_span), f32),
        ],
        compiler_params=params(),
    )(kinds, tile, tile, tile, x_below, x_above, y_below, y_above, cosine, sine_x)


def first_solve(modes, sine_yt, sine_ytr, sine_xt, edge_y, edge_x, eigen, levels, flux_x, flux_y, cosine, mean, exact_yt, exact_x, kinds):
    layers, y_span, x_span = modes.shape
    batch = 4
    steps = layers // batch
    sides = 2 * layers

    def kernel(kinds_ref, modes_ref, yt_ref, ytr_ref, xt_ref, edge_y_ref, edge_x_ref, eigen_ref, levels_ref,
               flux_x_ref, flux_y_ref, cosine_ref, mean_ref, exact_yt_ref, exact_x_ref, spectrum_ref, bundle_ref, rows_ref, columns_ref, exact_ref):
        step = pl.program_id(0)
        @pl.when(step == 0)
        def _():
            along_x = dot_full(mean_ref[...], exact_x_ref[...], ((1,), (0,)))
            exact_ref[...] = dot_full(exact_yt_ref[...], along_x, ((1,), (0,)))

        for i in range(batch):
            k = step * batch + i
            spectrum = table_times(yt_ref, modes_ref[i])
            if i == 0:
                spectrum = jnp.where(step == 0, exact_ref[...], spectrum)
            spectrum_ref[i] = spectrum
            high, low = pieces(spectrum * inverse_of(eigen_ref[...] + levels_ref[k]))
            found = mm(edge_y_ref[...], high) + mm(edge_y_ref[...], low)
            found = found[:8] + found[8:]
            rows_ref[pl.ds(k, 1)] = found[0:1]
            rows_ref[pl.ds(layers + k, 1)] = found[1:2]
            found = mm_transposed(edge_x_ref[...], high) + mm_transposed(edge_x_ref[...], low)
            found = found[:8] + found[8:]
            columns_ref[pl.ds(k, 1)] = found[0:1]
            columns_ref[pl.ds(layers + k, 1)] = found[1:2]

        @pl.when(step == steps - 1)
        def _():
            along_x = times_table(rows_ref[...], xt_ref)
            along_y = times_table(columns_ref[...], ytr_ref)
            cosine_table = cosine_ref[...]
            for line, values, flux_ref in ((0, along_x, flux_y_ref), (x_span, along_y, flux_x_ref)):
                part = slice(line, line + values.shape[1])
                bundle_ref[0, :, part] = values[:layers]
                bundle_ref[1, :, part] = values[layers:]
                bundle_ref[2, :, part] = dot_full(cosine_table, flux_ref[...], ((1,), (0,)))

    return pl.pallas_call(
        kernel,
        grid_spec=pltpu.PrefetchScalarGridSpec(
            num_scalar_prefetch=1,
            grid=(steps,),
            in_specs=[
                pl.BlockSpec((batch, y_span, x_span), lambda k, kinds: (k, 0, 0)),
                pl.BlockSpec((None, y_span, 3 * y_span), lambda k, kinds: (kinds[0], 0, 0)),
                pl.BlockSpec((None, 3 * y_span, y_span), lambda k, kinds: (kinds[0], 0, 0)),
                pl.BlockSpec((None, 3 * x_span, x_span), lambda k, kinds: (kinds[1], 0, 0)),
                pl.BlockSpec((None, 16, y_span), lambda k, kinds: (kinds[0], 0, 0)),
                pl.BlockSpec((None, 16, x_span), lambda k, kinds: (kinds[1], 0, 0)),
                pl.BlockSpec((None, y_span, x_span), lambda k, kinds: (kinds[0] * 3 + kinds[1], 0, 0)),
                pl.BlockSpec(memory_space=pltpu.SMEM),
                pl.BlockSpec((layers, y_span), lambda k, kinds: (0, 0)),
                pl.BlockSpec((layers, x_span), lambda k, kinds: (0, 0)),
                pl.BlockSpec((layers, layers), lambda k, kinds: (0, 0)),
                pl.BlockSpec((y_span, x_span), lambda k, kinds: (0, 0)),
                pl.BlockSpec((None, y_span, y_span), lambda k, kinds: (kinds[0], 0, 0)),
                pl.BlockSpec((None, x_span, x_span), lambda k, kinds: (kinds[1], 0, 0)),
            ],
            out_specs=[
                pl.BlockSpec((batch, y_span, x_span), lambda k, kinds: (k, 0, 0)),
                pl.BlockSpec((3, layers, x_span + y_span), lambda k, kinds: (0, 0, 0)),
            ],
            scratch_shapes=[pltpu.VMEM((sides, x_span), f32), pltpu.VMEM((sides, y_span), f32), pltpu.VMEM((y_span, x_span), f32)],
        ),
        out_shape=[
            jax.ShapeDtypeStruct((layers, y_span, x_span), f32),
            jax.ShapeDtypeStruct((3, layers, x_span + y_span), f32),
        ],
        compiler_params=params(),
    )(kinds, modes, sine_yt, sine_ytr, sine_xt, edge_y, edge_x, eigen, levels, flux_x, flux_y, cosine, mean, exact_yt, exact_x)


def second_solve(spectrum, sums, sine_y, sine_yr, sine_x, sine_xt, edge_y, edge_x, eigen, levels, kinds):
    layers, y_span, x_span = spectrum.shape
    batch = 8
    sides = 2 * layers

    def kernel(kinds_ref, spectrum_ref, sums_ref, y_ref, yr_ref, x_ref, xt_ref, edge_y_ref, edge_x_ref,
               eigen_ref, levels_ref, out_ref, along_x_ref, along_y_ref):
        step = pl.program_id(0)

        @pl.when(step == 0)
        def _():
            along_x_ref[...] = times_table(sums_ref[:, :x_span], x_ref)
            along_y_ref[...] = times_table(sums_ref[:, x_span:], yr_ref)

        low_side = pl.ds(pl.multiple_of(step * batch, batch), batch)
        high_side = pl.ds(pl.multiple_of(layers + step * batch, batch), batch)
        left = jnp.concatenate([along_y_ref[low_side], along_y_ref[high_side], edge_y_ref[...]], axis=0)
        right = jnp.concatenate([edge_x_ref[...], along_x_ref[low_side], along_x_ref[high_side]], axis=0)
        left_high = left.astype(jnp.bfloat16).astype(f32)
        blank = jnp.zeros((LANES - 12 * batch, y_span), f32)
        left = jnp.concatenate([left_high, left_high, left - left_high, blank], axis=0).T.astype(jnp.bfloat16)
        blank = jnp.zeros((LANES - 12 * batch, x_span), jnp.bfloat16)
        row_ids = lax.broadcasted_iota(jnp.int32, (4 * batch, x_span), 0) & (batch - 1)
        for start in range(0, batch, 4):
            along_y = []
            for i in range(start, start + 4):
                high, low = pieces(jnp.where(row_ids == i, right, 0.0))
                added = mm(left, jnp.concatenate([high, low, high, blank], axis=0))
                solved = (spectrum_ref[i] + added) * inverse_of(eigen_ref[...] + levels_ref[step * batch + i])
                along_y.append(table_times(y_ref, solved))
            found = times_table(jnp.concatenate(along_y, axis=0), xt_ref)
            out_ref[start : start + 4] = found.reshape(4, y_span, x_span)

    return pl.pallas_call(
        kernel,
        grid_spec=pltpu.PrefetchScalarGridSpec(
            num_scalar_prefetch=1,
            grid=(layers // batch,),
            in_specs=[
                pl.BlockSpec((batch, y_span, x_span), lambda k, kinds: (k, 0, 0)),
                pl.BlockSpec((sides, x_span + y_span), lambda k, kinds: (0, 0)),
                pl.BlockSpec((None, y_span, 3 * y_span), lambda k, kinds: (kinds[0], 0, 0)),
                pl.BlockSpec((None, 3 * y_span, y_span), lambda k, kinds: (kinds[0], 0, 0)),
                pl.BlockSpec((None, 3 * x_span, x_span), lambda k, kinds: (kinds[1], 0, 0)),
                pl.BlockSpec((None, 3 * x_span, x_span), lambda k, kinds: (kinds[1], 0, 0)),
                pl.BlockSpec((None, 2 * batch, y_span), lambda k, kinds: (kinds[0], 0, 0)),
                pl.BlockSpec((None, 2 * batch, x_span), lambda k, kinds: (kinds[1], 0, 0)),
                pl.BlockSpec((None, y_span, x_span), lambda k, kinds: (kinds[0] * 3 + kinds[1], 0, 0)),
                pl.BlockSpec(memory_space=pltpu.SMEM),
            ],
            out_specs=pl.BlockSpec((batch, y_span, x_span), lambda k, kinds: (k, 0, 0)),
            scratch_shapes=[
                pltpu.VMEM((sides, x_span), f32),
                pltpu.VMEM((sides, y_span), f32),
            ],
        ),
        out_shape=jax.ShapeDtypeStruct((layers, y_span, x_span), f32),
        compiler_params=params(),
    )(kinds, spectrum, sums, sine_y, sine_yr, sine_x, sine_xt, edge_y, edge_x, eigen, levels)


def finish(modes, star, sums, cosine_inverse, cosine_t, inverse, kinds, slots):
    layers, y_span, x_span = modes.shape
    rows_n, cols_n = y_span // B, x_span // B
    chunks = x_span // LANES

    def kernel(inverse_ref, kinds_ref, modes_ref, after_ref, star_ref, sums_ref, inverse_cosine_ref, cosine_ref,
               flow_out, pressure_out, rows_ref, blocks_ref, beyond_ref, flow_sem, pressure_sem):
        step = pl.program_id(0)
        half = step % 2

        def copies(at_step, at_half):
            found = []
            for col in range(cols_n):
                slot = inverse_ref[at_step * cols_n + col]
                found.append(pltpu.make_async_copy(
                    blocks_ref.at[at_half, col, pl.ds(0, 3)], flow_out.at[:, slot], flow_sem.at[at_half, col]))
                found.append(pltpu.make_async_copy(
                    blocks_ref.at[at_half, col, 3], pressure_out.at[slot], pressure_sem.at[at_half, col]))
            return found

        @pl.when(step >= 2)
        def _():
            for copy in copies(step - 2, half):
                copy.wait()

        @pl.when(step == 0)
        def _():
            beyond_ref[...] = dot_full(inverse_cosine_ref[...], sums_ref[layers:], ((1,), (0,)))

        lanes = lane_ids()
        layers_at = lax.broadcasted_iota(jnp.int32, (NZ, LANES), 0)
        last_layer = layers_at == NZ - 1
        last_lane = lanes == LANES - 1
        def layers_of(part):
            return table_times(cosine_ref, part.reshape(8 * NZ, x_span)).reshape(8, NZ, x_span)

        @pl.when(step == 0)
        def _():
            rows_ref[:8] = layers_of(modes_ref[:, :8, :])

        @pl.when(step > 0)
        def _():
            rows_ref[:8] = rows_ref[B:]

        def four_rows(jq):
            y = step * B + jq * 4
            y_chunk = pl.ds(pl.multiple_of(x_span + step * B // LANES * LANES, LANES), LANES)
            block = slice(jq * LANES, (jq + 1) * LANES)
            to_left = [
                [pltpu.roll(rows_ref[jq * 4 + t, :, h * LANES : (h + 1) * LANES], LANES - 1, 1) for t in range(4)]
                for h in range(chunks)
            ]
            for h in range(chunks):
                part = slice(h * LANES, (h + 1) * LANES)
                found = [[], [], [], []]
                for t in range(4):
                    j = jq * 4 + t
                    here = rows_ref[j, :, part]
                    if h == chunks - 1:
                        after = pltpu.roll(beyond_ref[:, y_chunk], LANES - 1 - (y + t) % LANES, 1)
                        after = jnp.where(kinds_ref[1] == 2, 0.0, after - here)
                    else:
                        after = to_left[h + 1][t]
                    x_up = jnp.where(last_lane, after, to_left[h][t])
                    y_up = rows_ref[j + 1, :, part]
                    z_up = jnp.where(last_layer, here, pltpu.roll(here, NZ - 1, 0))
                    found[0].append(star_ref[0, j, :, part] - (x_up - here))
                    found[1].append(star_ref[1, j, :, part] - (y_up - here))
                    found[2].append(star_ref[2, j, :, part] - (z_up - here))
                    found[3].append(here)
                for channel in range(4):
                    swapped = swap_groups(found[channel], lanes)
                    for g in range(4):
                        blocks_ref[half, 4 * h + g, channel, :, block] = swapped[g]

        groups = B // 8
        rows_ref[8:16] = layers_of(modes_ref[:, 8:16, :])
        for group in range(groups):
            ahead = group + 2
            if ahead < groups:
                rows_ref[8 * ahead : 8 * ahead + 8] = layers_of(modes_ref[:, 8 * ahead : 8 * ahead + 8, :])
            elif ahead == groups:
                beyond = jnp.where(kinds_ref[0] == 2, 0.0, beyond_ref[:, :x_span] - rows_ref[B - 1])
                found = layers_of(after_ref[...])
                rows_ref[B] = jnp.where(step == rows_n - 1, beyond, found[0])
                rows_ref[B + 1 :] = found[1:]
            four_rows(2 * group)
            four_rows(2 * group + 1)

        for copy in copies(step, half):
            copy.start()

        @pl.when(step == rows_n - 1)
        def _():
            for copy in copies(step - 1, 1 - half) + copies(step, half):
                copy.wait()

    return pl.pallas_call(
        kernel,
        grid_spec=pltpu.PrefetchScalarGridSpec(
            num_scalar_prefetch=2,
            grid=(rows_n,),
            in_specs=[
                pl.BlockSpec((layers, B, x_span), lambda s, inv, kinds: (0, s, 0)),
                pl.BlockSpec((layers, 8, x_span), lambda s, inv, kinds: (0, jnp.minimum((s + 1) * (B // 8), y_span // 8 - 1), 0)),
                pl.BlockSpec((3, B, NZ, x_span), lambda s, inv, kinds: (0, s, 0, 0)),
                pl.BlockSpec((2 * layers, x_span + y_span), lambda s, inv, kinds: (0, 0)),
                pl.BlockSpec((layers, layers), lambda s, inv, kinds: (0, 0)),
                pl.BlockSpec((8 * NZ, 24 * NZ), lambda s, inv, kinds: (0, 0)),
            ],
            out_specs=[pl.BlockSpec(memory_space=pl.ANY), pl.BlockSpec(memory_space=pl.ANY)],
            scratch_shapes=[
                pltpu.VMEM((B + 8, NZ, x_span), f32),
                pltpu.VMEM((2, cols_n, 4, NZ, B * B), f32),
                pltpu.VMEM((NZ, x_span + y_span), f32),
                pltpu.SemaphoreType.DMA((2, cols_n)),
                pltpu.SemaphoreType.DMA((2, cols_n)),
            ],
        ),
        out_shape=[
            jax.ShapeDtypeStruct((3, slots, NZ, B * B), f32),
            jax.ShapeDtypeStruct((slots, NZ, B * B), f32),
        ],
        compiler_params=params(),
    )(inverse, kinds, modes, modes, star, sums, cosine_inverse, cosine_t)


def solve_interfaces(lines_x, lines_y, picks_x, picks_y, table_x, table_y, eig_x, eig_y, levels, kinds):
    rows_x, rows_y = lines_x.shape[0], lines_y.shape[1]
    half_x = lines_y.shape[2]
    width = min(256, half_x)

    def kernel(kinds_ref, lines_x_ref, lines_y_ref, picks_x_ref, picks_y_ref, table_x_ref, table_y_ref, eig_x_ref,
               eig_y_ref, levels_ref, sum_x_ref, fold_ref, hat_ref, out_hat_ref):
        level = levels_ref[kinds_ref[2]]
        hat_x = few_rows_times(lines_x_ref[...], table_y_ref[0], table_y_ref[1])
        for parity in range(2):
            hat_ref[:, parity * half_x : (parity + 1) * half_x] = few_rows_times(
                lines_y_ref[parity], table_x_ref[parity, 0], table_x_ref[parity, 1])
        right = spread(jnp.concatenate([hat_x, picks_y_ref[0]], axis=0))
        along = jnp.zeros((rows_x, NY), f32)
        for start in range(0, 2 * half_x, width):
            part = slice(start, start + width)
            left = spread_other(jnp.concatenate([picks_x_ref[0, :, part], hat_ref[:, part]], axis=0))
            field = lax.dot_general(left, right, (((0,), (0,)), ((), ())), preferred_element_type=f32)
            field = field * inverse_of(eig_x_ref[part, :1] + eig_y_ref[:1] + level)
            high, low = pieces(field)
            along += few_rows_times(picks_x_ref[1, :, part], high, low)
            out_hat_ref[:, part] = hat_ref[:, part] + few_rows_times(picks_y_ref[1], high, low, mm_transposed)
        sum_x_ref[...] = few_rows_times(hat_x + along, table_y_ref[0], table_y_ref[1])
        for parity in range(2):
            fold_ref[parity] = few_rows_times(
                out_hat_ref[:, parity * half_x : (parity + 1) * half_x],
                table_x_ref[parity, 0], table_x_ref[parity, 1], mm_transposed)

    vmem = pl.BlockSpec(memory_space=pltpu.VMEM)
    return pl.pallas_call(
        kernel,
        grid_spec=pltpu.PrefetchScalarGridSpec(
            num_scalar_prefetch=1,
            grid=(),
            in_specs=[vmem] * 8 + [pl.BlockSpec(memory_space=pltpu.SMEM)],
            out_specs=[vmem, vmem],
            scratch_shapes=[pltpu.VMEM((rows_y, NX), f32), pltpu.VMEM((rows_y, NX), f32)],
        ),
        out_shape=[
            jax.ShapeDtypeStruct((rows_x, NY), f32),
            jax.ShapeDtypeStruct((2, rows_y, half_x), f32),
        ],
        compiler_params=params(),
    )(kinds, lines_x, lines_y, picks_x, picks_y, table_x, table_y, eig_x, eig_y, levels)


def padded_rows(count):
    return -(-2 * count // 16) * 16


def shards(tables, velocity, fluid, block_place):
    pa_size = lax.axis_size("pa")
    pb_size = lax.axis_size("pb")
    group_count = pa_size * pb_size
    y_span, x_span = NY // pa_size, NX // pb_size
    rows_n, cols_n = y_span // B, x_span // B
    slots = block_place.shape[0]
    pa, pb = lax.axis_index("pa"), lax.axis_index("pb")

    def kind(index, size):
        return jnp.where(index == 0, 0, jnp.where(index == size - 1, 2, 1)).astype(jnp.int32)

    repeats = group_count // NZ
    kinds = jnp.stack([kind(pa, pa_size), kind(pb, pb_size), (pa * pb_size + pb) // repeats])
    slot_ids = jnp.arange(slots, dtype=jnp.int32)
    matches = block_place[None, :] == slot_ids[:, None]
    inverse = jnp.sum(jnp.where(matches, slot_ids[None, :], 0), axis=1).astype(jnp.int32)

    tile, low_edge, high_edge = gather_tile(velocity, fluid, inverse, rows_n, cols_n)

    def up(values, axis, size):
        return lax.ppermute(values, axis, [(i, i + 1) for i in range(size - 1)])

    def down(values, axis, size):
        return lax.ppermute(values, axis, [(i + 1, i) for i in range(size - 1)])

    x_below, x_above = up(high_edge, "pb", pb_size), down(low_edge, "pb", pb_size)
    y_below, y_above = up(tile[:3, -1], "pa", pa_size), down(tile[:3, 0], "pa", pa_size)

    cosine = jnp.asarray(tables["cosine"])
    local = {name: jnp.asarray(tables[name]) for name in (
        "y", "yr", "yt", "ytr", "x", "xt", "edge_y", "edge_x", "few_y", "few_x", "exact_yt", "exact_x", "eigen", "levels", "picks_x", "picks_y", "fold_x", "line_y",
        "eig_x", "eig_y")}
    star, modes, flux_x, flux_y, mean = advance(
        tile, x_below, x_above, y_below, y_above, jnp.asarray(tables["cosine8"]), local["x"], kinds
    )
    spectrum, bundle = first_solve(
        modes, local["yt"], local["ytr"], local["xt"], local["few_y"], local["few_x"], local["eigen"],
        local["levels"], flux_x, flux_y, cosine, mean, local["exact_yt"], local["exact_x"], kinds
    )
    width = x_span + y_span
    bundle = jnp.repeat(bundle, repeats, axis=1) if repeats > 1 else bundle
    arrived = lax.all_to_all(bundle, ("pa", "pb"), split_axis=1, concat_axis=1, tiled=True)
    arrived = arrived.reshape(3, pa_size, pb_size, width)
    on_y, on_x = arrived[..., :x_span], arrived[..., x_span:]
    count_y, count_x = pa_size - 1, pb_size - 1
    rows_y, rows_x = padded_rows(count_y), padded_rows(count_x)
    sums_y = on_y[1, :-1] + on_y[0, 1:]
    lines_y = jnp.concatenate([sums_y, on_y[2, :-1]]).reshape(2 * count_y, NX)
    lines_y = jnp.pad(lines_y, ((0, rows_y - 2 * count_y), (0, 0)))
    sums_x = on_x[1, :, :-1] + on_x[0, :, 1:]
    lines_x = jnp.stack([sums_x, on_x[2, :, :-1]]).transpose(0, 2, 1, 3).reshape(2 * count_x, NY)
    lines_x = jnp.pad(lines_x, ((0, rows_x - 2 * count_x), (0, 0)))
    lower, upper = lines_y[:, : NX // 2], lines_y[:, NX // 2 :][:, ::-1]
    sum_x, folded = solve_interfaces(
        lines_x, jnp.stack([lower + upper, lower - upper]), local["picks_x"], local["picks_y"], local["fold_x"],
        local["line_y"], local["eig_x"], local["eig_y"], local["levels"], kinds
    )
    sum_x = sum_x[:count_x]
    even, odd = folded[0, :count_y], folded[1, :count_y]
    sum_y = jnp.concatenate([even + odd, (even - odd)[:, ::-1]], axis=1)
    flux_y, flux_x = lines_y[count_y : 2 * count_y], lines_x[count_x : 2 * count_x]
    none_y, none_x = jnp.zeros((1, NX), f32), jnp.zeros((1, NY), f32)
    high_y = jnp.concatenate([sum_y, none_y]).reshape(pa_size, pb_size, x_span)
    low_y = jnp.concatenate([none_y, sum_y + flux_y]).reshape(pa_size, pb_size, x_span)
    high_x = jnp.concatenate([sum_x, none_x]).reshape(pb_size, pa_size, y_span).transpose(1, 0, 2)
    low_x = jnp.concatenate([none_x, sum_x + flux_x]).reshape(pb_size, pa_size, y_span).transpose(1, 0, 2)
    reply = jnp.stack([jnp.concatenate([low_y, low_x], axis=2), jnp.concatenate([high_y, high_x], axis=2)])
    reply = reply.reshape(2, group_count, width)
    home = lax.all_to_all(reply, ("pa", "pb"), split_axis=1, concat_axis=1, tiled=True)
    sums = home[:, ::repeats].reshape(2 * NZ, width)
    pressure_modes = second_solve(
        spectrum, sums, local["y"], local["yr"], local["x"], local["xt"], local["edge_y"], local["edge_x"],
        local["eigen"], local["levels"], kinds
    )
    return tuple(
        finish(pressure_modes, star, sums, jnp.asarray(tables["cosine_t"]), jnp.asarray(tables["cosine8t"]), inverse,
               kinds, slots)
    )


def make_tables(pa_size, pb_size):
    y_span, x_span = NY // pa_size, NX // pb_size
    cosine, levels = cosine_basis()
    cosine8 = np.einsum("kz,ab->kabz", cosine, np.eye(8)).reshape(8 * NZ, 8 * NZ)
    tables = {
        "cosine": single(cosine),
        "levels": single(levels),
        "cosine_t": single(cosine.T),
        "cosine8": left_table(cosine8),
        "cosine8t": left_table(cosine8.T),
    }
    values = {}
    for name, length in (("y", y_span), ("x", x_span)):
        bases = tile_bases(length)
        if name == "x":
            tables["exact_x"] = single(np.stack([b for b, _ in bases]))
            tables["x"] = np.stack([right_table(b) for b, _ in bases])
            tables["xt"] = np.stack([right_table(b.T) for b, _ in bases])
        else:
            tables["exact_yt"] = single(np.stack([b.T for b, _ in bases]))
            tables["y"] = np.stack([left_table(b) for b, _ in bases])
            tables["yr"] = np.stack([right_table(b) for b, _ in bases])
            tables["yt"] = np.stack([left_table(b.T) for b, _ in bases])
            tables["ytr"] = np.stack([right_table(b.T) for b, _ in bases])
        edges = np.stack([np.repeat(b[[0, -1]], 8, axis=0) for b, _ in bases])
        tables["edge_" + name] = single(edges)
        few = np.zeros((3, 16, length), ml_dtypes.bfloat16)
        for i, (b, _) in enumerate(bases):
            few[i, 0:2], few[i, 8:10] = parts_of(b[[0, -1]])
        tables["few_" + name] = few
        values[name] = [v for _, v in bases]
    tables["eigen"] = single(
        np.stack([ey[:, None] + ex[None, :] for ey in values["y"] for ex in values["x"]])
    )
    basis_x, eig_x = sine_basis(NX, 1.0, 1.0)
    basis_y, eig_y = sine_basis(NY, 1.0, 1.0)
    half = NX // 2
    order = np.concatenate([np.arange(0, NX, 2), np.arange(1, NX, 2)])
    tables["fold_x"] = np.stack([split(basis_x[:half, parity::2]) for parity in range(2)])
    tables["line_y"] = split(basis_y)
    tables["eig_x"] = single(np.repeat(eig_x[order][:, None], LANES, axis=1))
    tables["eig_y"] = single(np.repeat(eig_y[None, :], 8, axis=0))
    for name, basis, tile in (("x", basis_x[:, order], x_span), ("y", basis_y, y_span)):
        above, below = basis[tile::tile], basis[tile - 1 : -1 : tile]
        count, length = above.shape
        picks = np.zeros((2, padded_rows(count), length))
        picks[0, : 2 * count] = np.concatenate([above + below, above])
        picks[1, :count] = above + below
        tables["picks_" + name] = single(picks)
    return tables


def solution(mesh):
    tables = make_tables(mesh.shape["pa"], mesh.shape["pb"])
    return jax.shard_map(
        functools.partial(shards, tables),
        mesh=mesh,
        in_specs=(P(None, ("pa", "pb"), None, None), P(("pa", "pb"), None, None), P(("pa", "pb"))),
        out_specs=(P(None, ("pa", "pb"), None, None), P(("pa", "pb"), None, None)),
        check_vma=False,
    )
```
